128 devices in a mesh: dp: 2 (over y_hi), heads: 32 (over x, z, y_lo), tensor: 2 (over core).
Axes of the slice: x: 4, y: 4 (y_hi: 2, y_lo: 2; y = y_hi * 2 + y_lo), z: 4, core: 2. Of those that a mesh axis runs over, the one named last changes fastest.
Arguments:
- tokens: bfloat16 [2, 4096, 2048], P('dp', 'heads'), may hold values from -6 to 6
- segments: int32 [2, 4096], P('dp', 'heads'), may hold values from 0 to 9, never falling along the last dimension, each value on 1 to 2048 neighbouring positions
- cotangent: bfloat16 [2, 4096, 2048], P('dp', 'heads'), may hold values from -6 to 6
- query_weight: float32 [2048, 2048], P(('dp', 'heads'), 'tensor'), may hold values from -0.125 to 0.125
- key_weight: float32 [2048, 512], P(('dp', 'heads'), 'tensor'), may hold values from -0.125 to 0.125
- value_weight: float32 [2048, 512], P(('dp', 'heads'), 'tensor'), may hold values from -0.125 to 0.125
- output_weight: float32 [2048, 2048], P('tensor', ('dp', 'heads')), may hold values from -0.375 to 0.375
- gate_weight: float32 [2048, 8192], P(('dp', 'heads'), 'tensor'), may hold values from -0.125 to 0.125
- up_weight: float32 [2048, 8192], P(('dp', 'heads'), 'tensor'), may hold values from -0.125 to 0.125
- down_weight: float32 [8192, 2048], P('tensor', ('dp', 'heads')), may hold values from -0.0625 to 0.0625
- norm_gain_pair: float32 [2, 2048], P(None, ('dp', 'heads')), may hold values from 0.5 to 1.5
- query_first: float32 [2048, 2048], P(('dp', 'heads'), 'tensor'), may hold values from -64 to 64
- key_first: float32 [2048, 512], P(('dp', 'heads'), 'tensor'), may hold values from -64 to 64
- value_first: float32 [2048, 512], P(('dp', 'heads'), 'tensor'), may hold values from -64 to 64
- output_first: float32 [2048, 2048], P('tensor', ('dp', 'heads')), may hold values from -16 to 16
- gate_first: float32 [2048, 8192], P(('dp', 'heads'), 'tensor'), may hold values from -16 to 16
- up_first: float32 [2048, 8192], P(('dp', 'heads'), 'tensor'), may hold values from -16 to 16
- down_first: float32 [8192, 2048], P('tensor', ('dp', 'heads')), may hold values from -32 to 32
- gains_first: float32 [2, 2048], P(None, ('dp', 'heads')), may hold values from -48 to 48
- query_second: float32 [2048, 2048], P(('dp', 'heads'), 'tensor'), may hold values from 212.992 to 3440.64
- key_second: float32 [2048, 512], P(('dp', 'heads'), 'tensor'), may hold values from 212.992 to 3440.64
- value_second: float32 [2048, 512], P(('dp', 'heads'), 'tensor'), may hold values from 212.992 to 3440.64
- output_second: float32 [2048, 2048], P('tensor', ('dp', 'heads')), may hold values from 18.8416 to 311.296
- gate_second: float32 [2048, 8192], P(('dp', 'heads'), 'tensor'), may hold values from 18.8416 to 311.296
- up_second: float32 [2048, 8192], P(('dp', 'heads'), 'tensor'), may hold values from 18.8416 to 311.296
- down_second: float32 [8192, 2048], P('tensor', ('dp', 'heads')), may hold values from 77.0048 to 1236.992
- gains_second: float32 [2, 2048], P(None, ('dp', 'heads')), may hold values from 135.9872 to 2203.648
Outputs:
- block_out: bfloat16 [2, 4096, 2048], P('dp', 'heads')
- input_grad: float32 [2, 4096, 2048], P('dp', 'heads')
- query_grad: float32 [2048, 2048], P(('dp', 'heads'), 'tensor')
- query_first_new: float32 [2048, 2048], P(('dp', 'heads'), 'tensor')
- query_second_new: float32 [2048, 2048], P(('dp', 'heads'), 'tensor')
- query_new: float32 [2048, 2048], P(('dp', 'heads'), 'tensor')
- key_grad: float32 [2048, 512], P(('dp', 'heads'), 'tensor')
- key_first_new: float32 [2048, 512], P(('dp', 'heads'), 'tensor')
- key_second_new: float32 [2048, 512], P(('dp', 'heads'), 'tensor')
- key_new: float32 [2048, 512], P(('dp', 'heads'), 'tensor')
- value_grad: float32 [2048, 512], P(('dp', 'heads'), 'tensor')
- value_first_new: float32 [2048, 512], P(('dp', 'heads'), 'tensor')
- value_second_new: float32 [2048, 512], P(('dp', 'heads'), 'tensor')
- value_new: float32 [2048, 512], P(('dp', 'heads'), 'tensor')
- output_grad: float32 [2048, 2048], P('tensor', ('dp', 'heads'))
- output_first_new: float32 [2048, 2048], P('tensor', ('dp', 'heads'))
- output_second_new: float32 [2048, 2048], P('tensor', ('dp', 'heads'))
- output_new: float32 [2048, 2048], P('tensor', ('dp', 'heads'))
- gate_grad: float32 [2048, 8192], P(('dp', 'heads'), 'tensor')
- gate_first_new: float32 [2048, 8192], P(('dp', 'heads'), 'tensor')
- gate_second_new: float32 [2048, 8192], P(('dp', 'heads'), 'tensor')
- gate_new: float32 [2048, 8192], P(('dp', 'heads'), 'tensor')
- up_grad: float32 [2048, 8192], P(('dp', 'heads'), 'tensor')
- up_first_new: float32 [2048, 8192], P(('dp', 'heads'), 'tensor')
- up_second_new: float32 [2048, 8192], P(('dp', 'heads'), 'tensor')
- up_new: float32 [2048, 8192], P(('dp', 'heads'), 'tensor')
- down_grad: float32 [8192, 2048], P('tensor', ('dp', 'heads'))
- down_first_new: float32 [8192, 2048], P('tensor', ('dp', 'heads'))
- down_second_new: float32 [8192, 2048], P('tensor', ('dp', 'heads'))
- down_new: float32 [8192, 2048], P('tensor', ('dp', 'heads'))
- gains_grad: float32 [2, 2048], P(None, ('dp', 'heads'))
- gains_first_new: float32 [2, 2048], P(None, ('dp', 'heads'))
- gains_second_new: float32 [2, 2048], P(None, ('dp', 'heads'))
- gains_new: float32 [2, 2048], P(None, ('dp', 'heads'))
The draws below stay inside these ranges and needn't reach their ends.
Inputs may be any that keep to these rules, and one draw needn't show every extreme that they name: `segments`: along each sequence the numbers never fall; each document holds 1 to 2048 tokens and one holds exactly 2048.
All inputs are finite; a program needn't handle non-finite values.
Results may differ from the reference program's by a relative error of at most 0.015.
Values may be sent and summed in bfloat16 or wider, within the bound.
A program may use at most 320 MiB of HBM per device.

```python
import math
import jax
import jax.numpy as jnp
import numpy as np
from jax import lax

D = 2048
FF = 8192
HEADS = 32
KV_HEADS = 8
HEAD_DIM = 64
STEP = 10
SEQS = 2
LENGTH = 4096
TOKENS = 8192
QD = 2048
KVD = 512
DOCS = 10
DOC_MOST = 2048


def steps_of(rng, dims, split, low, largest):
    factor_of, own = 1.0, jax.random.fold_in(rng, 6)
    for position, parts in split:
        draws = jnp.exp(jax.random.uniform(jax.random.fold_in(own, position), (parts,), jnp.float32, low / len(split), largest / len(split)))
        factor_of = factor_of * jnp.repeat(draws, dims[position] // parts).reshape([-1 if axis == position else 1 for axis in range(len(dims))])
    return factor_of


def split_up(amount, total, bound, skew):
    loads = [(1 << 20) // math.isqrt(grade ** skew) + 1 for grade in range(2, amount + 1)]
    rest, given = total - bound - (amount - 1), [1] * (amount - 1)
    while rest > 0:
        free = [i for i in range(amount - 1) if given[i] < bound]
        whole, budget = sum([loads[i] for i in free]), rest
        for i in free:
            addition = min(bound - given[i], max(1, budget * loads[i] // whole), rest)
            given[i] = given[i] + addition
            rest = rest - addition
    return np.array([bound] + given)


def uneven(own_key, count, total, limit, slope):
    if count == 2:
        one = jax.random.randint(own_key, (), max(1, total - limit), min(limit, total - 1) + 1)
        return jnp.stack([one, total - one])
    tallies = jnp.asarray(split_up(count, total, limit, slope), jnp.int32)
    twos = (count - 1) // 2
    donor, receiver = tallies[1:1 + 2 * twos:2], tallies[2:2 + 2 * twos:2]
    slack = jnp.minimum(donor - 1, limit - receiver)
    moved = jax.random.randint(jax.random.fold_in(own_key, 1), (twos,), 0, 1 << 20) % (slack + 1)
    tallies = tallies.at[1:1 + 2 * twos:2].set(donor - moved).at[2:2 + 2 * twos:2].set(receiver + moved)
    return tallies[jax.random.permutation(jax.random.fold_in(own_key, 2), count)]


def centred(rng, extent, scale, most, shards=(), held_as=jnp.bfloat16):
    gain = steps_of(rng, extent, shards, -0.22, 0.18) if shards else 1.0
    values = jax.random.normal(rng, extent, jnp.float32) * scale * gain
    return jnp.minimum(jnp.maximum(values, -most), most).astype(held_as)


def setup_inputs(seed: int = 0) -> dict:
    keys = jax.random.split(jax.random.key(seed), 28)
    tokens = centred(keys[0], (SEQS, LENGTH, D), 1.0, 6.0, ((0, 2), (1, 32)))
    segments = jax.vmap(lambda own: jnp.searchsorted(jnp.cumsum(uneven(own, DOCS, LENGTH, DOC_MOST, 2)), jnp.arange(LENGTH), side="right"))(jax.random.split(keys[1], SEQS)).reshape((SEQS, LENGTH)).astype(jnp.int32)
    cotangent = centred(keys[2], (SEQS, LENGTH, D), 1.0, 6.0, ((0, 2), (1, 32)))
    query_weight = centred(keys[3], (D, QD), D ** -0.5, 0.125, ((0, 64), (1, 2)), jnp.float32)
    key_weight = centred(keys[4], (D, KVD), D ** -0.5, 0.125, ((0, 64), (1, 2)), jnp.float32)
    value_weight = centred(keys[5], (D, KVD), D ** -0.5, 0.125, ((0, 64), (1, 2)), jnp.float32)
    output_weight = centred(keys[6], (QD, D), (4 * HEAD_DIM) ** -0.5, 0.375, ((0, 2), (1, 64)), jnp.float32)
    gate_weight = centred(keys[7], (D, FF), D ** -0.5, 0.125, ((0, 64), (1, 2)), jnp.float32)
    up_weight = centred(keys[8], (D, FF), D ** -0.5, 0.125, ((0, 64), (1, 2)), jnp.float32)
    down_weight = centred(keys[9], (FF, D), FF ** -0.5, 0.0625, ((0, 2), (1, 64)), jnp.float32)
    norm_gain_pair = jnp.clip(1.0 + 0.1 * jax.random.normal(keys[10], (2, D), jnp.float32), 0.5, 1.5)
    query_first = centred(keys[11], (D, QD), (0.11 * TOKENS ** 0.5), 64.0, ((0, 64), (1, 2)), jnp.float32)
    key_first = centred(keys[12], (D, KVD), (0.11 * TOKENS ** 0.5), 64.0, ((0, 64), (1, 2)), jnp.float32)
    value_first = centred(keys[13], (D, KVD), (0.11 * TOKENS ** 0.5), 64.0, ((0, 64), (1, 2)), jnp.float32)
    output_first = centred(keys[14], (QD, D), (0.033 * TOKENS ** 0.5), 16.0, ((0, 2), (1, 64)), jnp.float32)
    gate_first = centred(keys[15], (D, FF), (0.033 * TOKENS ** 0.5), 16.0, ((0, 64), (1, 2)), jnp.float32)
    up_first = centred(keys[16], (D, FF), (0.033 * TOKENS ** 0.5), 16.0, ((0, 64), (1, 2)), jnp.float32)
    down_first = centred(keys[17], (FF, D), (0.066 * TOKENS ** 0.5), 32.0, ((0, 2), (1, 64)), jnp.float32)
    gains_first = centred(keys[18], (2, D), (0.088 * TOKENS ** 0.5), 48.0, ((1, 64),), jnp.float32)
    query_second = jnp.clip(jnp.exp(math.log(3440.64) - 2.7821581 * jax.random.uniform(keys[19], (D, QD), jnp.float32) ** steps_of(keys[19], (D, QD), ((0, 64), (1, 2)), -0.2, 0.2)), 212.992, 3440.64)
    key_second = jnp.clip(jnp.exp(math.log(3440.64) - 2.7821581 * jax.random.uniform(keys[20], (D, KVD), jnp.float32) ** steps_of(keys[20], (D, KVD), ((0, 64), (1, 2)), -0.2, 0.2)), 212.992, 3440.64)
    value_second = jnp.clip(jnp.exp(math.log(3440.64) - 2.7821581 * jax.random.uniform(keys[21], (D, KVD), jnp.float32) ** steps_of(keys[21], (D, KVD), ((0, 64), (1, 2)), -0.2, 0.2)), 212.992, 3440.64)
    output_second = jnp.clip(jnp.exp(math.log(311.296) - 2.804677 * jax.random.uniform(keys[22], (QD, D), jnp.float32) ** steps_of(keys[22], (QD, D), ((0, 2), (1, 64)), -0.2, 0.2)), 18.8416, 311.296)
    gate_second = jnp.clip(jnp.exp(math.log(311.296) - 2.804677 * jax.random.uniform(keys[23], (D, FF), jnp.float32) ** steps_of(keys[23], (D, FF), ((0, 64), (1, 2)), -0.2, 0.2)), 18.8416, 311.296)
    up_second = jnp.clip(jnp.exp(math.log(311.296) - 2.804677 * jax.random.uniform(keys[24], (D, FF), jnp.float32) ** steps_of(keys[24], (D, FF), ((0, 64), (1, 2)), -0.2, 0.2)), 18.8416, 311.296)
    down_second = jnp.clip(jnp.exp(math.log(1236.992) - 2.77657 * jax.random.uniform(keys[25], (FF, D), jnp.float32) ** steps_of(keys[25], (FF, D), ((0, 2), (1, 64)), -0.2, 0.2)), 77.0048, 1236.992)
    gains_second = jnp.clip(jnp.exp(math.log(2203.648) - 2.7853087 * jax.random.uniform(keys[26], (2, D), jnp.float32) ** steps_of(keys[26], (2, D), ((1, 64),), -0.2, 0.2)), 135.9872, 2203.648)
    return {"tokens": tokens, "segments": segments, "cotangent": cotangent, "query_weight": query_weight, "key_weight": key_weight, "value_weight": value_weight, "output_weight": output_weight, "gate_weight": gate_weight, "up_weight": up_weight, "down_weight": down_weight, "norm_gain_pair": norm_gain_pair, "query_first": query_first, "key_first": key_first, "value_first": value_first, "output_first": output_first, "gate_first": gate_first, "up_first": up_first, "down_first": down_first, "gains_first": gains_first, "query_second": query_second, "key_second": key_second, "value_second": value_second, "output_second": output_second, "gate_second": gate_second, "up_second": up_second, "down_second": down_second, "gains_second": gains_second}


@jax.custom_vjp
def low(v):
    return lax.optimization_barrier(v.astype(jnp.bfloat16)).astype(jnp.float32)

@jax.custom_vjp
def low_back(v):
    return v

def low_keep(v):
    return (low(v), None)

def low_pass(kept, grad):
    return (grad,)

def back_keep(v):
    return (v, None)

def back_low(kept, grad):
    return (low(grad),)
low.defvjp(low_keep, low_pass)
low_back.defvjp(back_keep, back_low)
EPS = 1e-05

def hdot(left, right):
    return jnp.dot(left, right, precision=lax.Precision.HIGHEST, preferred_element_type=jnp.float32)

def rms_unit(values):
    return values * lax.rsqrt(lax.optimization_barrier(jnp.mean(values * values, axis=-1, keepdims=True)) + EPS)

def doc_positions(segment_row):
    token_index = jnp.arange(segment_row.shape[0], dtype=jnp.int32)
    previous = jnp.concatenate([jnp.full((1,), -1, jnp.int32), segment_row[:-1]])
    starts = lax.cummax(jnp.where(segment_row != previous, token_index, jnp.zeros_like(token_index)), axis=0)
    return token_index - starts

def rope_frequency():
    half_size = HEAD_DIM // 2
    base_freq = 500000.0 ** (-(jnp.arange(half_size, dtype=jnp.float32) * 2.0 / HEAD_DIM))
    wavelength = 2.0 * math.pi / base_freq
    smooth = (8192.0 / wavelength - 1.0) / 3.0
    blended = (1.0 - smooth) * base_freq / 32.0 + smooth * base_freq
    return jnp.where(wavelength < 2048.0, base_freq, jnp.where(wavelength > 8192.0, base_freq / 32.0, blended))

def rotary_tables(positions):
    frequency = rope_frequency()
    angles = positions.astype(jnp.float32)[:, None] * frequency[None, :]
    return (jnp.cos(angles), jnp.sin(angles))

def rotate(values, cos_tab, sin_tab):
    half_size = values.shape[-1] // 2
    front_part = values[..., :half_size]
    back_part = values[..., half_size:]
    cos_wide = cos_tab[:, None, :]
    sin_wide = sin_tab[:, None, :]
    return jnp.concatenate([front_part * cos_wide - back_part * sin_wide, back_part * cos_wide + front_part * sin_wide], axis=-1)

def head_attention(query_head, key_head, value_head, allowed):
    scores = low_back(hdot(query_head, key_head.T) * HEAD_DIM ** (-0.5))
    scores = jnp.where(allowed, scores, -1e+30)
    shifted = scores - lax.optimization_barrier(jnp.max(scores, axis=-1, keepdims=True))
    exponent = jnp.exp(shifted)
    probability = exponent / lax.optimization_barrier(jnp.sum(exponent, axis=-1, keepdims=True))
    return hdot(low(probability), value_head)

def block(params, input_rows, allowed, cos_tab, sin_tab):
    query_weight, key_weight, value_weight, output_weight, gate_weight, up_weight, down_weight, norm_gain_pair = params
    length = input_rows.shape[0]
    gains_low = low(norm_gain_pair)
    attention_normalized = low(rms_unit(input_rows) * gains_low[0])
    query_heads = low_back(hdot(attention_normalized, low(query_weight))).reshape(length, HEADS, HEAD_DIM)
    key_heads = low_back(hdot(attention_normalized, low(key_weight))).reshape(length, KV_HEADS, HEAD_DIM)
    value_heads = low(low_back(hdot(attention_normalized, low(value_weight)))).reshape(length, KV_HEADS, HEAD_DIM)
    query_heads = low(rotate(query_heads, cos_tab, sin_tab))
    key_heads = low(rotate(key_heads, cos_tab, sin_tab))
    key_all = jnp.repeat(key_heads, HEADS // KV_HEADS, axis=1)
    value_all = jnp.repeat(value_heads, HEADS // KV_HEADS, axis=1)

    def one_head(pieces):
        return head_attention(pieces[0], pieces[1], pieces[2], allowed)
    attended = lax.map(jax.checkpoint(one_head), (query_heads.transpose(1, 0, 2), key_all.transpose(1, 0, 2), value_all.transpose(1, 0, 2)))
    attended = low(low_back(attended.transpose(1, 0, 2).reshape(length, HEADS * HEAD_DIM)))
    residual_stream = input_rows + low_back(hdot(attended, low(output_weight)))
    feedforward_normalized = low(rms_unit(residual_stream) * gains_low[1])
    gate_proj = low_back(hdot(feedforward_normalized, low(gate_weight)))
    up_proj = low_back(hdot(feedforward_normalized, low(up_weight)))
    active = low(gate_proj * jax.nn.sigmoid(gate_proj) * up_proj)
    return residual_stream + low_back(hdot(active, low(down_weight)))

def adamw(weight, first_moment, second_moment, gradient, step_rate):
    first_new = 0.9 * first_moment + 0.1 * gradient
    second_new = 0.95 * second_moment + 0.05 * gradient * gradient
    corrected = first_new / (1.0 - 0.9 ** STEP) / (jnp.sqrt(second_new / (1.0 - 0.95 ** STEP)) + 1e-08)
    return (first_new, second_new, weight - step_rate * (corrected + 0.1 * weight))

def reference(tokens, segments, cotangent, query_weight, key_weight, value_weight, output_weight, gate_weight, up_weight, down_weight, norm_gain_pair, query_first, key_first, value_first, output_first, gate_first, up_first, down_first, gains_first, query_second, key_second, value_second, output_second, gate_second, up_second, down_second, gains_second):
    params = (query_weight, key_weight, value_weight, output_weight, gate_weight, up_weight, down_weight, norm_gain_pair)

    def per_sequence(running, pieces):
        seq_tokens, seq_segments, seq_cotangent = pieces
        cos_tab, sin_tab = rotary_tables(doc_positions(seq_segments))
        token_index = jnp.arange(seq_segments.shape[0], dtype=jnp.int32)
        allowed = (seq_segments[:, None] == seq_segments[None, :]) & (token_index[None, :] <= token_index[:, None])

        def forward(weights, input_rows):
            return block(weights, input_rows, allowed, cos_tab, sin_tab)
        result, pullback = jax.vjp(forward, params, seq_tokens.astype(jnp.float32))
        weight_grads, token_grad = pullback(seq_cotangent.astype(jnp.float32))
        running = jax.tree.map(jnp.add, running, weight_grads)
        return (running, (result.astype(jnp.bfloat16), token_grad))
    zeros_tree = jax.tree.map(jnp.zeros_like, params)
    totals, outputs = lax.scan(per_sequence, zeros_tree, (tokens, segments, cotangent))
    block_out, input_grad = outputs
    query_grad, key_grad, value_grad, output_grad, gate_grad, up_grad, down_grad, gains_grad = totals
    wide_rate = 2.0 * D ** (-0.5)
    query_first_new, query_second_new, query_new = adamw(query_weight, query_first, query_second, query_grad, wide_rate)
    key_first_new, key_second_new, key_new = adamw(key_weight, key_first, key_second, key_grad, wide_rate)
    value_first_new, value_second_new, value_new = adamw(value_weight, value_first, value_second, value_grad, wide_rate)
    output_first_new, output_second_new, output_new = adamw(output_weight, output_first, output_second, output_grad, 2.0 * (4 * HEAD_DIM) ** (-0.5))
    gate_first_new, gate_second_new, gate_new = adamw(gate_weight, gate_first, gate_second, gate_grad, wide_rate)
    up_first_new, up_second_new, up_new = adamw(up_weight, up_first, up_second, up_grad, wide_rate)
    down_first_new, down_second_new, down_new = adamw(down_weight, down_first, down_second, down_grad, 2.0 * FF ** (-0.5))
    gains_first_new, gains_second_new, gains_new = adamw(norm_gain_pair, gains_first, gains_second, gains_grad, 1.5)
    return (block_out, input_grad, query_grad, query_first_new, query_second_new, query_new, key_grad, key_first_new, key_second_new, key_new, value_grad, value_first_new, value_second_new, value_new, output_grad, output_first_new, output_second_new, output_new, gate_grad, gate_first_new, gate_second_new, gate_new, up_grad, up_first_new, up_second_new, up_new, down_grad, down_first_new, down_second_new, down_new, gains_grad, gains_first_new, gains_second_new, gains_new)
```

```python
import functools
import itertools
import math

import jax
import jax.numpy as jnp
from jax import lax
from jax.experimental import pallas as pl
from jax.experimental.pallas import tpu as pltpu
from jax.sharding import Mesh
from jax.sharding import PartitionSpec as P

D = 2048
FF = 8192
HEADS = 32
KV_HEADS = 8
HEAD_DIM = 64
STEP = 10
EPS = 1e-05

SIZES = {"dp": 2, "x": 4, "z": 4, "yl": 2, "t": 2}
GROUP = ("z", "yl")
CROSS = ("dp", "x")
MEMBERS = 8
HALF = 64
ROWS = 1024
LENGTH = 4096
QB = 256
KB = 512
BF = jnp.bfloat16
F32 = jnp.float32


def shifts(axes):
    return list(itertools.product(*[range(SIZES[a]) for a in axes]))


def place(axes, shift, sign=1):
    index = 0
    for a, s in zip(axes, shift):
        index = index * SIZES[a] + lax.rem(
            lax.axis_index(a) + (s if sign > 0 else SIZES[a] - s), SIZES[a]
        )
    return index


def peer(axes, shift):
    return {
        a: lax.rem(lax.axis_index(a) + s, SIZES[a]) for a, s in zip(axes, shift) if s
    }


def other_core():
    return {"t": 1 - lax.axis_index("t")}


def greet(devices):
    sem = pltpu.get_barrier_semaphore()
    for device in devices:
        pl.semaphore_signal(
            sem, inc=1, device_id=device, device_id_type=pl.DeviceIdType.MESH
        )
    pl.semaphore_wait(sem, len(devices))


def remote(src, dst, send, recv, device):
    return pltpu.make_async_remote_copy(
        src_ref=src,
        dst_ref=dst,
        send_sem=send,
        recv_sem=recv,
        device_id=device,
        device_id_type=pl.DeviceIdType.MESH,
    )


def gather_kernel(with_segments, *refs):
    if with_segments:
        x_ref, seg_ref, out_ref, seg_out, send, recv, tsend, trecv, local, ssend, srecv, xsend, xrecv, slocal = refs
    else:
        x_ref, out_ref, send, recv, tsend, trecv, local = refs
    t = lax.axis_index("t")
    moves = shifts(GROUP)[1:]
    crossings = [(s,) for s in (1, 2, 3)]
    devices = [other_core()] + [peer(GROUP, s) for s in moves]
    if with_segments:
        devices = devices + [peer(("x",), s) for s in crossings]
    greet(devices)
    me = place(GROUP, (0, 0))
    copies = []
    own = pltpu.make_async_copy(x_ref, out_ref.at[me, t], local)
    own.start()
    if with_segments:
        x = lax.axis_index("x")
        seg_own = pltpu.make_async_copy(seg_ref, seg_out.at[x, me], slocal)
        seg_own.start()
        seg_copies = []
        for i, s in enumerate(moves):
            c = remote(seg_ref, seg_out.at[x, me], ssend.at[i], srecv.at[i], peer(GROUP, s))
            c.start()
            seg_copies.append(c)
    for i, s in enumerate(moves):
        c = remote(x_ref, out_ref.at[me, t], send.at[i], recv.at[i], peer(GROUP, s))
        c.start()
        copies.append(c)
    c = remote(x_ref, out_ref.at[me, t], tsend.at[7], trecv.at[7], other_core())
    c.start()
    passed = [c]
    if with_segments:
        seg_own.wait()
        for c in seg_copies:
            c.wait()
        crossed = []
        for i, s in enumerate(crossings):
            c = remote(seg_out.at[x], seg_out.at[x], xsend.at[i], xrecv.at[i], peer(("x",), s))
            c.start()
            crossed.append(c)
    for i, s in enumerate(moves):
        copies[i].wait_recv()
        source = place(GROUP, s, -1)
        c = remote(
            out_ref.at[source, t], out_ref.at[source, t], tsend.at[i], trecv.at[i], other_core()
        )
        c.start()
        passed.append(c)
    own.wait()
    for c in copies:
        c.wait_send()
    for c in passed:
        c.wait()
    if with_segments:
        for c in crossed:
            c.wait()


def gather_tokens(x, segments=None):
    with_segments = segments is not None
    wide = x.shape[1]
    dma = pltpu.SemaphoreType.DMA
    out_shape = [jax.ShapeDtypeStruct((MEMBERS, 2, HALF, wide), x.dtype)]
    scratch = [dma((7,)), dma((7,)), dma((8,)), dma((8,)), dma]
    args = [x]
    if with_segments:
        out_shape.append(jax.ShapeDtypeStruct((4, MEMBERS, 8, 128), jnp.int32))
        scratch = scratch + [dma((7,)), dma((7,)), dma((3,)), dma((3,)), dma]
        args.append(segments)
    hbm = pl.BlockSpec(memory_space=pl.ANY)
    out = pl.pallas_call(
        functools.partial(gather_kernel, with_segments),
        out_shape=out_shape,
        in_specs=[hbm] * len(args),
        out_specs=[hbm] * len(out_shape),
        scratch_shapes=scratch,
        compiler_params=pltpu.CompilerParams(
            collective_id=1 if with_segments else 2, has_side_effects=True
        ),
        cost_estimate=pl.CostEstimate(flops=0, bytes_accessed=60_000_000, transcendentals=0),
        name="gather_tokens_first" if with_segments else "gather_tokens",
    )(*args)
    gathered = out[0].reshape(ROWS, wide)
    return (gathered, out[1]) if with_segments else gathered


def scatter_kernel(p_ref, out_ref, mine, theirs, sums, land, lsem, tsend, trecv, send, recv):
    t = lax.axis_index("t")
    moves = shifts(GROUP)
    order = moves[1:] + moves[:1]
    greet([other_core()] + [peer(GROUP, s) for s in moves[1:]])
    loads, swaps = [], []
    for i, s in enumerate(order):
        chunk = place(GROUP, s)
        c = remote(p_ref.at[chunk, 1 - t], theirs.at[i], tsend.at[i], trecv.at[i], other_core())
        c.start()
        swaps.append(c)
        c = pltpu.make_async_copy(p_ref.at[chunk, t], mine.at[i], lsem.at[i])
        c.start()
        loads.append(c)
    copies = []
    for i, s in enumerate(order[:7]):
        loads[i].wait()
        swaps[i].wait_recv()
        sums[i] = (mine[i].astype(F32) + theirs[i].astype(F32)).astype(BF)
        c = remote(sums.at[i], land.at[i], send.at[i], recv.at[i], peer(GROUP, s))
        c.start()
        copies.append(c)
    loads[7].wait()
    swaps[7].wait_recv()
    out_ref[...] = mine[7].astype(F32) + theirs[7].astype(F32)
    for i in range(7):
        copies[i].wait_recv()
        out_ref[...] += land[i].astype(F32)
    for c in copies:
        c.wait_send()
    for c in swaps:
        c.wait_send()


def scatter_sum(partial_sum):
    wide = partial_sum.shape[1]
    dma = pltpu.SemaphoreType.DMA
    slots = (MEMBERS, HALF, wide)
    return pl.pallas_call(
        scatter_kernel,
        out_shape=jax.ShapeDtypeStruct((HALF, wide), F32),
        in_specs=[pl.BlockSpec(memory_space=pl.ANY)],
        out_specs=pl.BlockSpec(memory_space=pltpu.VMEM),
        scratch_shapes=[
            pltpu.VMEM(slots, BF),
            pltpu.VMEM(slots, BF),
            pltpu.VMEM((7, HALF, wide), BF),
            pltpu.VMEM((7, HALF, wide), BF),
            dma((8,)),
            dma((8,)),
            dma((8,)),
            dma((7,)),
            dma((7,)),
        ],
        compiler_params=pltpu.CompilerParams(
            collective_id=3, has_side_effects=True, vmem_limit_bytes=32 * 2**20
        ),
        cost_estimate=pl.CostEstimate(flops=0, bytes_accessed=60_000_000, transcendentals=0),
        name="scatter_sum",
    )(partial_sum.reshape(MEMBERS, 2, HALF, wide))


def gather_x_kernel(x_ref, out_ref, send, recv, local):
    moves = [(s,) for s in (1, 2, 3)]
    greet([peer(("x",), s) for s in moves])
    me = lax.axis_index("x")
    own = pltpu.make_async_copy(x_ref, out_ref.at[me], local)
    own.start()
    copies = []
    for i, s in enumerate(moves):
        c = remote(x_ref, out_ref.at[me], send.at[i], recv.at[i], peer(("x",), s))
        c.start()
        copies.append(c)
    own.wait()
    for c in copies:
        c.wait()


def gather_x(x):
    dma = pltpu.SemaphoreType.DMA
    hbm = pl.BlockSpec(memory_space=pl.ANY)
    out = pl.pallas_call(
        gather_x_kernel,
        out_shape=jax.ShapeDtypeStruct((4,) + x.shape, x.dtype),
        in_specs=[hbm],
        out_specs=hbm,
        scratch_shapes=[dma((3,)), dma((3,)), dma],
        compiler_params=pltpu.CompilerParams(collective_id=4, has_side_effects=True),
        cost_estimate=pl.CostEstimate(flops=0, bytes_accessed=30_000_000, transcendentals=0),
        name="gather_keys",
    )(x)
    return out.reshape(4 * x.shape[0], x.shape[1])


def scatter_x_kernel(p_ref, out_ref, mine, land, lsem, send, recv):
    moves = [(s,) for s in (1, 2, 3)]
    greet([peer(("x",), s) for s in moves])
    me = lax.axis_index("x")
    own = pltpu.make_async_copy(p_ref.at[me], mine, lsem)
    own.start()
    copies = []
    for i, s in enumerate(moves):
        c = remote(p_ref.at[place(("x",), s)], land.at[i], send.at[i], recv.at[i], peer(("x",), s))
        c.start()
        copies.append(c)
    own.wait()
    out_ref[...] = mine[...].astype(F32)
    for i in range(3):
        copies[i].wait()
        out_ref[...] += land[i].astype(F32)


def scatter_x(p):
    dma = pltpu.SemaphoreType.DMA
    wide = p.shape[1]
    return pl.pallas_call(
        scatter_x_kernel,
        out_shape=jax.ShapeDtypeStruct((ROWS, wide), F32),
        in_specs=[pl.BlockSpec(memory_space=pl.ANY)],
        out_specs=pl.BlockSpec(memory_space=pltpu.VMEM),
        scratch_shapes=[
            pltpu.VMEM((ROWS, wide), BF),
            pltpu.VMEM((3, ROWS, wide), BF),
            dma,
            dma((3,)),
            dma((3,)),
        ],
        compiler_params=pltpu.CompilerParams(collective_id=5, has_side_effects=True),
        cost_estimate=pl.CostEstimate(flops=0, bytes_accessed=30_000_000, transcendentals=0),
        name="scatter_key_grads",
    )(p.reshape(4, ROWS, wide))


def abt(left, right):
    return lax.dot_general(left, right, (((1,), (1,)), ((), ())), preferred_element_type=F32)


def atb(left, right):
    return lax.dot_general(left, right, (((0,), (0,)), ((), ())), preferred_element_type=F32)


def attend_kernel(lo_ref, hi_ref, q_ref, kv_ref, kvt_ref, qi_ref, st_ref, o_ref, lse_ref):
    i = pl.program_id(0)
    q = q_ref[...]
    row, start = qi_ref[...], st_ref[...]
    wide = q.shape[0]

    def step(j, carry):
        top, total, acc = carry
        base = pl.multiple_of(j * KB, KB)
        s = abt(kv_ref[pl.ds(base, KB), :], q)
        key = base + lax.broadcasted_iota(jnp.int32, (KB, wide), 0)
        s = jnp.where((key <= row) & (key >= start), s, -1e30)
        new_top = jnp.maximum(top, jnp.max(s, axis=0, keepdims=True))
        p = jnp.exp(s - new_top)
        fade = jnp.exp(top - new_top)
        total = total * fade + jnp.sum(p, axis=0, keepdims=True)
        acc = acc * fade + jnp.dot(
            kvt_ref[:, pl.ds(base, KB)], p.astype(BF), preferred_element_type=F32
        )
        return (new_top, total, acc)

    init = (
        jnp.full((1, wide), -1e30, F32),
        jnp.zeros((1, wide), F32),
        jnp.zeros((2 * HEAD_DIM, wide), F32),
    )
    top, total, acc = lax.fori_loop(lo_ref[i], hi_ref[i], step, init)
    o_ref[...] = acc / total
    lse_ref[...] = top + jnp.log(total)


def attend_back_kernel(
    lo_ref, hi_ref, q_ref, g_ref, kv_ref, kvt_ref, qi_ref, st_ref, lse_ref, dot_ref, dq_ref, dkv_ref, acc_ref
):
    i = pl.program_id(0)
    q, g = q_ref[...], g_ref[...]
    row, start, lse, row_dot = qi_ref[...], st_ref[...], lse_ref[...], dot_ref[...]
    wide = q.shape[0]

    @pl.when(i == 0)
    def _():
        acc_ref[...] = jnp.zeros_like(acc_ref)

    def step(j, dq):
        base = pl.multiple_of(j * KB, KB)
        kv = kv_ref[pl.ds(base, KB), :]
        s = abt(kv, q)
        key = base + lax.broadcasted_iota(jnp.int32, (KB, wide), 0)
        s = jnp.where((key <= row) & (key >= start), s, -1e30)
        p = jnp.exp(s - lse)
        ds = (p * (abt(kv, g) - row_dot)).astype(BF)
        acc_ref[pl.ds(base, KB), :] += jnp.dot(ds, q, preferred_element_type=F32) + jnp.dot(
            p.astype(BF), g, preferred_element_type=F32
        )
        return dq + jnp.dot(kvt_ref[:, pl.ds(base, KB)], ds, preferred_element_type=F32)

    dq_ref[...] = lax.fori_loop(
        lo_ref[i], hi_ref[i], step, jnp.zeros((2 * HEAD_DIM, wide), F32)
    )

    @pl.when(i == pl.num_programs(0) - 1)
    def _():
        dkv_ref[...] = acc_ref[...].astype(BF)


def whole(shape):
    return pl.BlockSpec(shape, lambda i: (0,) * len(shape))


def block(rows, columns):
    return pl.BlockSpec((None, rows, columns), lambda i: (i, 0, 0))


BLOCKS = ROWS // QB
WIDE = 2 * QB
SCALARS = pl.BlockSpec(memory_space=pltpu.SMEM)


def attend(lo, hi, q, kv, kvt, row, start):
    return pl.pallas_call(
        attend_kernel,
        grid=(BLOCKS,),
        out_shape=[
            jax.ShapeDtypeStruct((BLOCKS, 128, WIDE), F32),
            jax.ShapeDtypeStruct((BLOCKS, 1, WIDE), F32),
        ],
        in_specs=[
            SCALARS,
            SCALARS,
            block(WIDE, 128),
            whole((LENGTH, 128)),
            whole((128, LENGTH)),
            block(1, WIDE),
            block(1, WIDE),
        ],
        out_specs=[block(128, WIDE), block(1, WIDE)],
        compiler_params=pltpu.CompilerParams(vmem_limit_bytes=48 * 2**20),
        cost_estimate=pl.CostEstimate(
            flops=2_000_000_000, bytes_accessed=60_000_000, transcendentals=4_000_000
        ),
        name="attend",
    )(lo, hi, q, kv, kvt, row, start)


def attend_back(lo, hi, q, g, kv, kvt, row, start, lse, row_dot):
    return pl.pallas_call(
        attend_back_kernel,
        grid=(BLOCKS,),
        out_shape=[
            jax.ShapeDtypeStruct((BLOCKS, 128, WIDE), F32),
            jax.ShapeDtypeStruct((LENGTH, 128), BF),
        ],
        in_specs=[
            SCALARS,
            SCALARS,
            block(WIDE, 128),
            block(WIDE, 128),
            whole((LENGTH, 128)),
            whole((128, LENGTH)),
            block(1, WIDE),
            block(1, WIDE),
            block(1, WIDE),
            block(1, WIDE),
        ],
        out_specs=[block(128, WIDE), whole((LENGTH, 128))],
        scratch_shapes=[pltpu.VMEM((LENGTH, 128), F32)],
        compiler_params=pltpu.CompilerParams(vmem_limit_bytes=48 * 2**20),
        cost_estimate=pl.CostEstimate(
            flops=5_000_000_000, bytes_accessed=120_000_000, transcendentals=4_000_000
        ),
        name="attend_back",
    )(lo, hi, q, g, kv, kvt, row, start, lse, row_dot)


def permute(x, axes, shift):
    count = math.prod(SIZES[a] for a in axes)
    pairs = []
    for source, at in enumerate(shifts(axes)):
        target = 0
        for a, c, s in zip(axes, at, shift):
            target = target * SIZES[a] + (c + s) % SIZES[a]
        pairs.append((source, target))
    assert len(pairs) == count
    return lax.ppermute(x, axes, pairs)


def swap_cores(x):
    return lax.ppermute(x, "t", [(0, 1), (1, 0)])


def gather_over(x, axes):
    moves = shifts(axes)
    out = jnp.zeros((len(moves),) + x.shape, x.dtype)
    out = lax.dynamic_update_index_in_dim(out, x, place(axes, moves[0]), 0)
    for s in moves[1:]:
        out = lax.dynamic_update_index_in_dim(out, permute(x, axes, s), place(axes, s, -1), 0)
    return out


def sum_over(x, axes):
    moves = shifts(axes)
    total = lax.dynamic_index_in_dim(x, place(axes, moves[0]), 0, keepdims=False).astype(F32)
    for s in moves[1:]:
        chunk = lax.dynamic_index_in_dim(x, place(axes, s), 0, keepdims=False)
        total = total + permute(chunk, axes, s).astype(F32)
    return total


def deal(x):
    return lax.all_to_all(x, GROUP, split_axis=0, concat_axis=0, tiled=True)


def spread(weight_slots):
    dealt = deal(weight_slots)
    wide = weight_slots.shape[2]
    return gather_over(dealt.reshape(MEMBERS * 32, wide), CROSS).reshape(D, wide)


def collect(gradient):
    wide = gradient.shape[1]
    own = sum_over(gradient.reshape(8, 256, wide), CROSS)
    return deal(own.astype(BF).reshape(MEMBERS, 32, wide)).astype(F32)


def rope_frequency():
    half_size = HEAD_DIM // 2
    base_freq = 500000.0 ** (-(jnp.arange(half_size, dtype=F32) * 2.0 / HEAD_DIM))
    wavelength = 2.0 * math.pi / base_freq
    smooth = (8192.0 / wavelength - 1.0) / 3.0
    blended = (1.0 - smooth) * base_freq / 32.0 + smooth * base_freq
    return jnp.where(
        wavelength < 2048.0, base_freq, jnp.where(wavelength > 8192.0, base_freq / 32.0, blended)
    )


def rotate(values, cos_tab, sin_tab):
    rows = values.shape[0]
    v = values.reshape(rows, -1, 2, HEAD_DIM // 2)
    a, b = v[:, :, 0], v[:, :, 1]
    c, s = cos_tab[:, None, :], sin_tab[:, None, :]
    return jnp.stack([a * c - b * s, b * c + a * s], axis=2).reshape(rows, -1)


def adamw(weight, first_moment, second_moment, gradient, step_rate):
    first_new = 0.9 * first_moment + 0.1 * gradient
    second_new = 0.95 * second_moment + 0.05 * gradient * gradient
    corrected = first_new / (1.0 - 0.9**STEP) / (jnp.sqrt(second_new / (1.0 - 0.95**STEP)) + 1e-08)
    return (first_new, second_new, weight - step_rate * (corrected + 0.1 * weight))


def slots(w, columns):
    return w.reshape(w.shape[0], -1, columns).transpose(1, 0, 2)


def unslots(g):
    return g.transpose(1, 0, 2).reshape(g.shape[1], -1)


def heads_apart(x):
    return x.reshape(BLOCKS, QB, 2, HEAD_DIM).transpose(0, 2, 1, 3).reshape(BLOCKS, WIDE, HEAD_DIM)


def heads_beside(x):
    return x.reshape(BLOCKS, HEAD_DIM, 2, QB).transpose(0, 3, 2, 1).reshape(ROWS, 2 * HEAD_DIM)


def body(
    tokens,
    segments,
    cotangent,
    query_weight,
    key_weight,
    value_weight,
    output_weight,
    gate_weight,
    up_weight,
    down_weight,
    norm_gain_pair,
    query_first,
    key_first,
    value_first,
    output_first,
    gate_first,
    up_first,
    down_first,
    gains_first,
    query_second,
    key_second,
    value_second,
    output_second,
    gate_second,
    up_second,
    down_second,
    gains_second,
):
    t = lax.axis_index("t")
    x_place = lax.axis_index("x")

    gains = norm_gain_pair.astype(BF).astype(F32)
    gain_a, gain_m = gains[0][:, None], gains[1][:, None]
    low = lambda w: w.astype(BF).astype(F32)
    fold = lambda g, w: (g * low(w)).astype(BF)
    twice = lambda w: jnp.repeat(slots(w, HEAD_DIM), 2, axis=0)
    attn_slots = jnp.concatenate(
        [
            slots(fold(gain_a, query_weight), 128),
            twice(fold(gain_a, key_weight)),
            twice(fold(gain_a, value_weight)),
            slots(output_weight.astype(BF).T, 128),
        ],
        axis=2,
    )
    mlp_slots = jnp.concatenate(
        [
            slots(fold(gain_m, gate_weight), 512),
            slots(fold(gain_m, up_weight), 512),
            slots(down_weight.astype(BF).T, 512),
        ],
        axis=2,
    )
    attn_w = spread(attn_slots)
    mlp_w = spread(mlp_slots)
    w_qkv, w_out = attn_w[:, :256], attn_w[:, 256:]
    w_gate_up, w_down = mlp_w[:, :1024], mlp_w[:, 1024:]

    rows = lax.dynamic_slice_in_dim(tokens[0], t * HALF, HALF, 0).astype(F32)
    inv_a = lax.rsqrt(jnp.mean(rows * rows, axis=1, keepdims=True) + EPS)
    unit_a = rows * inv_a
    all_a, seg = gather_tokens(unit_a.astype(BF), jnp.broadcast_to(segments, (8, 128)))
    segment = seg[:, :, 0, :].reshape(LENGTH)
    index = jnp.arange(LENGTH, dtype=jnp.int32)
    previous = jnp.concatenate([jnp.full((1,), -1, jnp.int32), segment[:-1]])
    starts = lax.cummax(jnp.where(segment != previous, index, 0), axis=0)
    first_row = x_place * ROWS
    own_start = lax.dynamic_slice_in_dim(starts, first_row, ROWS, 0)
    own_index = first_row + jnp.arange(ROWS, dtype=jnp.int32)
    angles = (own_index - own_start).astype(F32)[:, None] * rope_frequency()[None, :]
    cos_tab, sin_tab = jnp.cos(angles), jnp.sin(angles)
    lo = own_start.reshape(BLOCKS, QB)[:, 0] // KB
    hi = (first_row + (jnp.arange(BLOCKS, dtype=jnp.int32) + 1) * QB + KB - 1) // KB
    by_block = lambda v: jnp.concatenate([v.reshape(BLOCKS, 1, QB)] * 2, axis=2)
    row_ids, row_starts = by_block(own_index), by_block(own_start)

    qkv = jnp.dot(all_a, w_qkv, preferred_element_type=F32)
    rotated = rotate(qkv[:, :192], cos_tab, sin_tab).astype(BF)
    kv_own = jnp.concatenate([rotated[:, 128:], qkv[:, 192:].astype(BF)], axis=1)
    kv = gather_x(kv_own)
    kvt = kv.T
    scale = HEAD_DIM ** (-0.5)
    q_low = heads_apart(rotated[:, :128])
    nothing = jnp.zeros_like(q_low)
    q_wide = jnp.concatenate([q_low * jnp.asarray(scale, BF), nothing], axis=2)
    o_cols, lse = attend(lo, hi, q_wide, kv, kvt, row_ids, row_starts)
    o_full = heads_beside(o_cols[:, HEAD_DIM:])
    o_low = o_full.astype(BF)

    resid = rows + scatter_sum(abt(o_low, w_out).astype(BF))
    inv_m = lax.rsqrt(jnp.mean(resid * resid, axis=1, keepdims=True) + EPS)
    unit_m = resid * inv_m
    all_m = gather_tokens(unit_m.astype(BF))
    gate_up = jnp.dot(all_m, w_gate_up, preferred_element_type=F32)
    gate, up = gate_up[:, :512], gate_up[:, 512:]
    sig = jax.nn.sigmoid(gate)
    silu = gate * sig
    act = (silu * up).astype(BF)

    cot_half = lax.dynamic_slice_in_dim(cotangent[0], t * HALF, HALF, 0)
    cot_own = gather_over(cot_half, GROUP)
    cot_other = swap_cores(cot_own)
    all_g = jnp.where(
        t == 0, jnp.stack([cot_own, cot_other], axis=1), jnp.stack([cot_other, cot_own], axis=1)
    ).reshape(ROWS, D)

    g_act = jnp.dot(all_g, w_down, preferred_element_type=F32)
    g_gate = g_act * up * sig * (1.0 + gate * (1.0 - sig))
    g_up = g_act * silu
    g_gate_up = jnp.concatenate([g_gate, g_up], axis=1).astype(BF)
    g_unit_m = scatter_sum(abt(g_gate_up, w_gate_up).astype(BF))
    grad_out = cot_half.astype(F32)
    g_resid = grad_out + inv_m * (
        g_unit_m - unit_m * jnp.mean(g_unit_m * unit_m, axis=1, keepdims=True)
    )
    all_r = gather_tokens(g_resid.astype(BF))

    mlp_grad = jnp.concatenate([atb(all_m, g_gate_up), atb(all_g, act)], axis=1).astype(BF)
    mlp_sum = collect(mlp_grad)

    down = abt(act, w_down).astype(BF).reshape(MEMBERS, 2, HALF, D)
    pick = lambda v, i: lax.dynamic_index_in_dim(v, i, 1, keepdims=False)
    down_pair = pick(down, t).astype(F32) + swap_cores(pick(down, 1 - t)).astype(F32)
    out_half = (resid + sum_over(down_pair.astype(BF), GROUP)).astype(BF)
    halves = lambda own: jnp.where(
        t == 0,
        jnp.concatenate([own, swap_cores(own)], axis=0),
        jnp.concatenate([swap_cores(own), own], axis=0),
    )
    block_out = halves(out_half)

    g_o = jnp.dot(all_r, w_out, preferred_element_type=F32).astype(BF)
    row_dot = (
        (o_full * g_o.astype(F32))
        .reshape(BLOCKS, QB, 2, HEAD_DIM)
        .sum(axis=3)
        .transpose(0, 2, 1)
        .reshape(BLOCKS, 1, WIDE)
    )
    g_wide = jnp.concatenate([nothing, heads_apart(g_o)], axis=2)
    dq_cols, dkv = attend_back(
        lo, hi, q_wide, g_wide, kv, kvt, row_ids, row_starts, lse, row_dot
    )
    g_kv = scatter_x(dkv)
    g_q = heads_beside(dq_cols[:, :HEAD_DIM]) * scale
    g_turned = rotate(jnp.concatenate([g_q, g_kv[:, :HEAD_DIM]], axis=1), cos_tab, -sin_tab)
    g_qkv = jnp.concatenate([g_turned, g_kv[:, HEAD_DIM:]], axis=1).astype(BF)
    attn_grad = jnp.concatenate([atb(all_a, g_qkv), atb(all_r, o_low)], axis=1).astype(BF)
    attn_sum = collect(attn_grad)
    g_unit_a = scatter_sum(abt(g_qkv, w_qkv).astype(BF))
    input_half = g_resid + inv_a * (
        g_unit_a - unit_a * jnp.mean(g_unit_a * unit_a, axis=1, keepdims=True)
    )
    input_grad = halves(input_half)

    pairs = lambda g: unslots(g.reshape(4, 2, 32, HEAD_DIM).sum(axis=1))
    q_sum = unslots(attn_sum[:, :, :128])
    k_sum = pairs(attn_sum[:, :, 128:192])
    v_sum = pairs(attn_sum[:, :, 192:256])
    gate_sum = unslots(mlp_sum[:, :, :512])
    up_sum = unslots(mlp_sum[:, :, 512:1024])
    dots = lambda g, w: jnp.sum(g * low(w), axis=1)
    gains_half = jnp.stack(
        [
            dots(q_sum, query_weight) + dots(k_sum, key_weight) + dots(v_sum, value_weight),
            dots(gate_sum, gate_weight) + dots(up_sum, up_weight),
        ],
        axis=0,
    )
    gains_grad = gains_half + swap_cores(gains_half)
    query_grad, key_grad, value_grad = gain_a * q_sum, gain_a * k_sum, gain_a * v_sum
    gate_grad, up_grad = gain_m * gate_sum, gain_m * up_sum
    output_grad = unslots(attn_sum[:, :, 256:]).T
    down_grad = unslots(mlp_sum[:, :, 1024:]).T
    wide_rate = 2.0 * D ** (-0.5)
    outs = [block_out[None], input_grad[None]]
    for weight, first, second, grad, rate in (
        (query_weight, query_first, query_second, query_grad, wide_rate),
        (key_weight, key_first, key_second, key_grad, wide_rate),
        (value_weight, value_first, value_second, value_grad, wide_rate),
        (output_weight, output_first, output_second, output_grad, 2.0 * (4 * HEAD_DIM) ** (-0.5)),
        (gate_weight, gate_first, gate_second, gate_grad, wide_rate),
        (up_weight, up_first, up_second, up_grad, wide_rate),
        (down_weight, down_first, down_second, down_grad, 2.0 * FF ** (-0.5)),
        (norm_gain_pair, gains_first, gains_second, gains_grad, 1.5),
    ):
        outs.append(grad)
        outs.extend(adamw(weight, first, second, grad, rate))
    return tuple(outs)


def solution(mesh):
    split = Mesh(
        mesh.devices.reshape(tuple(SIZES.values())), tuple(SIZES)
    )
    heads = ("x", "z", "yl")
    every = ("dp", "x", "z", "yl")
    acts = P("dp", heads, None)
    rows_cut = P(every, "t")
    columns_cut = P("t", every)
    gains = P(None, every)
    weights = (rows_cut,) * 3 + (columns_cut,) + (rows_cut,) * 2 + (columns_cut, gains)
    in_specs = (acts, P("dp", heads), acts) + weights * 3
    out_specs = (acts, acts) + tuple(spec for spec in weights for _ in range(4))
    return jax.shard_map(
        body, mesh=split, in_specs=in_specs, out_specs=out_specs, check_vma=False
    )
```

```python
import functools
import itertools
import math

import jax
import jax.numpy as jnp
from jax import lax
from jax.experimental import pallas as pl
from jax.experimental.pallas import tpu as pltpu
from jax.sharding import Mesh
from jax.sharding import PartitionSpec as P

D = 2048
FF = 8192
HEADS = 32
KV_HEADS = 8
HEAD_DIM = 64
STEP = 10
EPS = 1e-05

SIZES = {"dp": 2, "x": 4, "z": 4, "yl": 2, "t": 2}
GROUP = ("z", "yl")
CROSS = ("dp", "x")
MEMBERS = 8
HALF = 64
ROWS = 1024
LENGTH = 4096
QB = 256
KB = 512
BF = jnp.bfloat16
F32 = jnp.float32


def shifts(axes):
    return list(itertools.product(*[range(SIZES[a]) for a in axes]))


def place(axes, shift, sign=1):
    index = 0
    for a, s in zip(axes, shift):
        index = index * SIZES[a] + lax.rem(
            lax.axis_index(a) + (s if sign > 0 else SIZES[a] - s), SIZES[a]
        )
    return index


def peer(axes, shift):
    return {
        a: lax.rem(lax.axis_index(a) + s, SIZES[a]) for a, s in zip(axes, shift) if s
    }


def other_core():
    return {"t": 1 - lax.axis_index("t")}


def greet(devices):
    sem = pltpu.get_barrier_semaphore()
    for device in devices:
        pl.semaphore_signal(
            sem, inc=1, device_id=device, device_id_type=pl.DeviceIdType.MESH
        )
    pl.semaphore_wait(sem, len(devices))


def remote(src, dst, send, recv, device):
    return pltpu.make_async_remote_copy(
        src_ref=src,
        dst_ref=dst,
        send_sem=send,
        recv_sem=recv,
        device_id=device,
        device_id_type=pl.DeviceIdType.MESH,
    )


DMA = pltpu.SemaphoreType.DMA
HBM = pl.BlockSpec(memory_space=pl.ANY)
VMEM = pl.BlockSpec(memory_space=pltpu.VMEM)
MOVES = shifts(GROUP)[1:]
TURNS = (1, 3, 2)


def members():
    return [other_core()] + [peer(GROUP, s) for s in MOVES]


def across():
    return [peer(("dp",), (1,))] + [peer(("x",), (s,)) for s in TURNS]


def finish(copies):
    for c in copies:
        c.wait()


GATHER_SEMS = [DMA((7,)), DMA((7,)), DMA((8,)), DMA((8,)), DMA]


def gather_start(x_ref, out_ref, sems):
    send, recv, tsend, trecv, local = sems
    t, me = lax.axis_index("t"), place(GROUP, (0, 0))
    own = pltpu.make_async_copy(x_ref, out_ref.at[me, t], local)
    own.start()
    copies = []
    for i, s in enumerate(MOVES):
        c = remote(x_ref, out_ref.at[me, t], send.at[i], recv.at[i], peer(GROUP, s))
        c.start()
        copies.append(c)
    c = remote(x_ref, out_ref.at[me, t], tsend.at[7], trecv.at[7], other_core())
    c.start()
    return own, copies, [c]


def gather_finish(state, out_ref, sems):
    own, copies, passed = state
    _, _, tsend, trecv, _ = sems
    t = lax.axis_index("t")
    for i, s in enumerate(MOVES):
        copies[i].wait_recv()
        part = out_ref.at[place(GROUP, s, -1), t]
        c = remote(part, part, tsend.at[i], trecv.at[i], other_core())
        c.start()
        passed.append(c)
    own.wait()
    for c in copies:
        c.wait_send()
    finish(passed)


SCATTER_SEMS = [DMA((8,)), DMA((8,)), DMA((8,)), DMA((7,)), DMA((7,))]


def scatter_slots(wide):
    return [
        pltpu.VMEM((MEMBERS, HALF, wide), BF),
        pltpu.VMEM((MEMBERS, HALF, wide), BF),
        pltpu.VMEM((7, HALF, wide), BF),
        pltpu.VMEM((7, HALF, wide), BF),
    ]


def scatter_start(p_ref, slots, sems):
    mine, theirs, _, _ = slots
    lsem, tsend, trecv, _, _ = sems
    t = lax.axis_index("t")
    loads, swaps = [], []
    for i, s in enumerate(MOVES + [(0, 0)]):
        chunk = place(GROUP, s)
        c = remote(p_ref.at[chunk, 1 - t], theirs.at[i], tsend.at[i], trecv.at[i], other_core())
        c.start()
        swaps.append(c)
        c = pltpu.make_async_copy(p_ref.at[chunk, t], mine.at[i], lsem.at[i])
        c.start()
        loads.append(c)
    return loads, swaps


def scatter_send(state, slots, sems):
    loads, swaps = state
    mine, theirs, sums, land = slots
    _, _, _, send, recv = sems
    copies = []
    for i, s in enumerate(MOVES):
        loads[i].wait()
        swaps[i].wait_recv()
        sums[i] = (mine[i].astype(F32) + theirs[i].astype(F32)).astype(BF)
        c = remote(sums.at[i], land.at[i], send.at[i], recv.at[i], peer(GROUP, s))
        c.start()
        copies.append(c)
    loads[7].wait()
    swaps[7].wait_recv()
    return copies


def scatter_total(state, copies, slots, total):
    _, swaps = state
    mine, theirs, _, land = slots
    total[...] = mine[7].astype(F32) + theirs[7].astype(F32)
    for i in range(7):
        copies[i].wait_recv()
        total[...] += land[i].astype(F32)
    for c in copies + swaps:
        c.wait_send()


SPREAD_SEMS = [DMA((7,)), DMA((7,)), DMA]


def spread_start(x_ref, out_ref, sems):
    send, recv, local = sems
    dp, x = lax.axis_index("dp"), lax.axis_index("x")
    own = pltpu.make_async_copy(x_ref, out_ref.at[dp, x], local)
    own.start()
    copies = []
    for i, to in enumerate(across()):
        c = remote(x_ref, out_ref.at[dp, x], send.at[i], recv.at[i], to)
        c.start()
        copies.append(c)
    return own, copies


def spread_pass(state, out_ref, sems):
    _, copies = state
    send, recv, _ = sems
    part = out_ref.at[1 - lax.axis_index("dp"), lax.axis_index("x")]
    copies[0].wait_recv()
    for i, to in enumerate(across()[1:]):
        c = remote(part, part, send.at[4 + i], recv.at[4 + i], to)
        c.start()
        copies.append(c)


def spread_finish(state):
    own, copies = state
    own.wait()
    copies[0].wait_send()
    finish(copies[1:])


REDUCE_SEMS = [DMA((2,)), DMA((7,)), DMA((7,))]


def reduce_slots(wide):
    return [
        pltpu.VMEM((2, 256, wide), BF),
        pltpu.VMEM((6, 256, wide), BF),
        pltpu.VMEM((256, wide), BF),
        pltpu.VMEM((256, wide), BF),
    ]


def reduce_start(p_ref, slots, sems):
    mine, land, _, _ = slots
    lsem, send, recv = sems
    dp, x = lax.axis_index("dp"), lax.axis_index("x")
    loads, copies = [], []
    for j, row in enumerate((1 - dp, dp)):
        c = pltpu.make_async_copy(p_ref.at[row, x], mine.at[j], lsem.at[j])
        c.start()
        loads.append(c)
        for i, s in enumerate(TURNS):
            k = 3 * j + i
            c = remote(
                p_ref.at[row, place(("x",), (s,))],
                land.at[k],
                send.at[k],
                recv.at[k],
                peer(("x",), (s,)),
            )
            c.start()
            copies.append(c)
    return loads, copies


def add_rows(out_ref, terms):
    rows = 32

    def step(r, carry):
        at = pl.ds(pl.multiple_of(r * rows, rows), rows)
        total = terms[0][at, :].astype(F32)
        for term in terms[1:]:
            total = total + term[at, :].astype(F32)
        out_ref[at, :] = total.astype(out_ref.dtype)
        return carry

    lax.fori_loop(0, 256 // rows, step, 0)


def reduce_pass(state, slots, sems):
    loads, copies = state
    mine, land, fold, back = slots
    _, send, recv = sems
    loads[0].wait()
    for c in copies[:3]:
        c.wait_recv()
    add_rows(fold, [mine.at[0]] + [land.at[i] for i in range(3)])
    c = remote(fold, back, send.at[6], recv.at[6], peer(("dp",), (1,)))
    c.start()
    copies.append(c)


def reduce_total(state, slots, out_ref):
    loads, copies = state
    mine, land, _, back = slots
    loads[1].wait()
    for c in copies[3:]:
        c.wait_recv()
    add_rows(out_ref, [mine.at[1], back] + [land.at[3 + i] for i in range(3)])
    for c in copies:
        c.wait_send()


DEAL_SEMS = [DMA((7,)), DMA((7,)), DMA]


def deal_start(x_ref, out_ref, sems):
    send, recv, local = sems
    me = place(GROUP, (0, 0))
    own = pltpu.make_async_copy(x_ref.at[me], out_ref.at[me], local)
    own.start()
    copies = []
    for i, s in enumerate(MOVES):
        c = remote(
            x_ref.at[place(GROUP, s)], out_ref.at[me], send.at[i], recv.at[i], peer(GROUP, s)
        )
        c.start()
        copies.append(c)
    return [own] + copies


def split(refs, *counts):
    parts, at = [], 0
    for count in counts:
        parts.append(refs[at : at + count])
        at += count
    assert at == len(refs)
    return parts


def scale_rows(x):
    return lax.rsqrt(jnp.mean(x * x, axis=1, keepdims=True) + EPS)


def norm_back(unit, inverse, grad):
    return inverse * (grad - unit * jnp.mean(grad * unit, axis=1, keepdims=True))


def call(kernel, collective_id, name, args, in_specs, outs, out_specs, scratch):
    sent = 60_000_000
    return pl.pallas_call(
        kernel,
        out_shape=[jax.ShapeDtypeStruct(s, d) for s, d in outs],
        in_specs=in_specs,
        out_specs=out_specs,
        scratch_shapes=scratch,
        compiler_params=pltpu.CompilerParams(
            collective_id=collective_id, has_side_effects=True, vmem_limit_bytes=56 * 2**20
        ),
        cost_estimate=pl.CostEstimate(flops=0, bytes_accessed=sent, transcendentals=0),
        name=name,
    )(*args)


def first_kernel(*refs):
    ins, outs, dealt, gather, deal_a, deal_b, spread_a, spread_b, seg_sems = split(
        refs, 4, 4, 2, 5, 3, 3, 3, 3, 5
    )
    x_ref, seg_ref, qkv_ref, wo_ref = ins
    all_ref, seg_out, w_qkv, w_out = outs
    part_a, part_b = dealt
    ssend, srecv, xsend, xrecv, slocal = seg_sems
    greet(members() + across())
    deals = deal_start(qkv_ref, part_a, deal_a) + deal_start(wo_ref, part_b, deal_b)
    me, x = place(GROUP, (0, 0)), lax.axis_index("x")
    seg_own = pltpu.make_async_copy(seg_ref, seg_out.at[x, me], slocal)
    seg_own.start()
    seg_copies = [seg_own]
    for i, s in enumerate(MOVES):
        c = remote(seg_ref, seg_out.at[x, me], ssend.at[i], srecv.at[i], peer(GROUP, s))
        c.start()
        seg_copies.append(c)
    tokens = gather_start(x_ref, all_ref, gather)
    finish(deals)
    spreads = [spread_start(part_a, w_qkv, spread_a), spread_start(part_b, w_out, spread_b)]
    finish(seg_copies)
    crossed = []
    for i, to in enumerate(across()[1:]):
        c = remote(seg_out.at[x], seg_out.at[x], xsend.at[i], xrecv.at[i], to)
        c.start()
        crossed.append(c)
    spread_pass(spreads[0], w_qkv, spread_a)
    spread_pass(spreads[1], w_out, spread_b)
    gather_finish(tokens, all_ref, gather)
    for s in spreads:
        spread_finish(s)
    finish(crossed)


def first_exchange(unit, segments, qkv_slots, out_slots):
    outs = [
        ((MEMBERS, 2, HALF, D), BF),
        ((4, MEMBERS, 8, 128), jnp.int32),
        ((2, 4, MEMBERS, 32, 256), BF),
        ((2, 4, MEMBERS, 32, 128), BF),
    ]
    scratch = [pltpu.VMEM((MEMBERS, 32, 256), BF), pltpu.VMEM((MEMBERS, 32, 128), BF)]
    scratch += GATHER_SEMS + DEAL_SEMS * 2 + SPREAD_SEMS * 2
    scratch += [DMA((7,)), DMA((7,)), DMA((3,)), DMA((3,)), DMA]
    args = (unit, segments, qkv_slots, out_slots)
    tokens, seg, w_qkv, w_out = call(
        first_kernel, 1, "first_exchange", args, [HBM] * 4, outs, [HBM] * 4, scratch
    )
    return tokens.reshape(ROWS, D), seg, w_qkv.reshape(D, 256), w_out.reshape(D, 128)


def keys_kernel(*refs):
    ins, outs, sems, deal_a, deal_b = split(refs, 3, 3, 3, 3, 3)
    kv_ref, gu_ref, down_ref = ins
    out_ref, gu_part, down_part = outs
    send, recv, local = sems
    greet(members()[1:] + across()[1:])
    x = lax.axis_index("x")
    copies = [pltpu.make_async_copy(kv_ref, out_ref.at[x], local)]
    copies[0].start()
    for i, to in enumerate(across()[1:]):
        c = remote(kv_ref, out_ref.at[x], send.at[i], recv.at[i], to)
        c.start()
        copies.append(c)
    copies = copies + deal_start(gu_ref, gu_part, deal_a) + deal_start(down_ref, down_part, deal_b)
    finish(copies)


def exchange_keys(kv, gate_up_slots, down_slots):
    outs = [
        ((4, ROWS, 128), BF),
        ((MEMBERS, 32, 1024), BF),
        ((MEMBERS, 32, 512), BF),
    ]
    scratch = [DMA((3,)), DMA((3,)), DMA] + DEAL_SEMS * 2
    args = (kv, gate_up_slots, down_slots)
    kv, gate_up, down = call(
        keys_kernel, 2, "exchange_keys", args, [HBM] * 3, outs, [HBM] * 3, scratch
    )
    return kv.reshape(LENGTH, 128), gate_up, down


def forward_kernel(*refs):
    ins, outs, buffers, scatter_sems, gather, gather_b, spread_a, spread_b = split(
        refs, 5, 5, 6, 5, 5, 5, 3, 3
    )
    p_ref, rows_ref, cot_ref, gu_ref, down_ref = ins
    resid_ref, all_m, all_g, w_gu, w_down = outs
    *scatter, total, unit = buffers
    greet(members() + across())
    partial_sums = scatter_start(p_ref, scatter, scatter_sems)
    spreads = [spread_start(gu_ref, w_gu, spread_a), spread_start(down_ref, w_down, spread_b)]
    sent = scatter_send(partial_sums, scatter, scatter_sems)
    spread_pass(spreads[0], w_gu, spread_a)
    scatter_total(partial_sums, sent, scatter, total)
    resid = rows_ref[...] + total[...]
    resid_ref[...] = resid
    unit[...] = (resid * scale_rows(resid)).astype(BF)
    tokens = gather_start(unit, all_m, gather)
    cots = gather_start(cot_ref, all_g, gather_b)
    spread_pass(spreads[1], w_down, spread_b)
    gather_finish(tokens, all_m, gather)
    gather_finish(cots, all_g, gather_b)
    for s in spreads:
        spread_finish(s)


def forward_exchange(p, rows, cot, gate_up_part, down_part):
    slots = (MEMBERS, 2, HALF, D)
    outs = [
        ((HALF, D), F32),
        (slots, BF),
        (slots, BF),
        ((2, 4, MEMBERS, 32, 1024), BF),
        ((2, 4, MEMBERS, 32, 512), BF),
    ]
    scratch = scatter_slots(D) + [pltpu.VMEM((HALF, D), F32), pltpu.VMEM((HALF, D), BF)]
    scratch += SCATTER_SEMS + GATHER_SEMS * 2 + SPREAD_SEMS * 2
    args = (p.reshape(slots), rows, cot, gate_up_part, down_part)
    resid, all_m, all_g, w_gu, w_down = call(
        forward_kernel,
        3,
        "forward_exchange",
        args,
        [HBM, VMEM, HBM, HBM, HBM],
        outs,
        [VMEM] + [HBM] * 4,
        scratch,
    )
    return (
        resid,
        all_m.reshape(ROWS, D),
        all_g.reshape(ROWS, D),
        w_gu.reshape(D, 1024),
        w_down.reshape(D, 512),
    )


def backward_kernel(*refs):
    ins, outs, slots_a, slots_b, slots_c, others, sems_a, sems_b, sems_c, gather, osems = split(
        refs, 5, 4, 4, 4, 4, 3, 5, 5, 3, 5, 3
    )
    pm_ref, pd_ref, resid_ref, cot_ref, mg_ref = ins
    g_resid, all_r, block_out, m_sum = outs
    total, low, out_low = others
    greet(members() + across())
    t = lax.axis_index("t")
    state_a = scatter_start(pm_ref, slots_a, sems_a)
    state_c = reduce_start(mg_ref, slots_c, sems_c)
    sent_a = scatter_send(state_a, slots_a, sems_a)
    state_b = scatter_start(pd_ref, slots_b, sems_b)
    scatter_total(state_a, sent_a, slots_a, total)
    resid = resid_ref[...]
    inverse = scale_rows(resid)
    grad = cot_ref[...].astype(F32) + norm_back(resid * inverse, inverse, total[...])
    g_resid[...] = grad
    low[...] = grad.astype(BF)
    tokens = gather_start(low, all_r, gather)
    sent_b = scatter_send(state_b, slots_b, sems_b)
    reduce_pass(state_c, slots_c, sems_c)
    gather_finish(tokens, all_r, gather)
    scatter_total(state_b, sent_b, slots_b, total)
    out_low[...] = (resid_ref[...] + total[...]).astype(BF)
    osend, orecv, local = osems
    copies = [
        pltpu.make_async_copy(out_low, block_out.at[t], local),
        remote(out_low, block_out.at[t], osend, orecv, other_core()),
    ]
    for c in copies:
        c.start()
    reduce_total(state_c, slots_c, m_sum)
    finish(copies)


def backward_exchange(pm, pd, resid, cot, grads):
    slots = (MEMBERS, 2, HALF, D)
    outs = [
        ((HALF, D), F32),
        (slots, BF),
        ((2, HALF, D), BF),
        ((256, 1536), BF),
    ]
    scratch = scatter_slots(D) * 2 + reduce_slots(1536)
    scratch += [pltpu.VMEM((HALF, D), F32), pltpu.VMEM((HALF, D), BF), pltpu.VMEM((HALF, D), BF)]
    scratch += SCATTER_SEMS * 2 + REDUCE_SEMS + GATHER_SEMS + [DMA, DMA, DMA]
    args = (pm.reshape(slots), pd.reshape(slots), resid, cot, grads.reshape(2, 4, 256, 1536))
    g_resid, all_r, block_out, m_sum = call(
        backward_kernel,
        4,
        "backward_exchange",
        args,
        [HBM, HBM, VMEM, VMEM, HBM],
        outs,
        [VMEM, HBM, HBM, VMEM],
        scratch,
    )
    return g_resid, all_r.reshape(ROWS, D), block_out.reshape(2 * HALF, D), m_sum


def key_grads_kernel(*refs):
    ins, outs, buffers, sems, deal = split(refs, 2, 2, 2, 3, 3)
    p_ref, m_ref = ins
    out_ref, dealt = outs
    mine, land = buffers
    lsem, send, recv = sems
    greet(members()[1:] + across()[1:])
    x = lax.axis_index("x")
    own = pltpu.make_async_copy(p_ref.at[x], mine, lsem)
    own.start()
    copies = []
    for i, s in enumerate(TURNS):
        c = remote(
            p_ref.at[place(("x",), (s,))], land.at[i], send.at[i], recv.at[i], peer(("x",), (s,))
        )
        c.start()
        copies.append(c)
    deals = deal_start(m_ref, dealt, deal)
    own.wait()
    out_ref[...] = mine[...].astype(F32)
    for i in range(3):
        copies[i].wait()
        out_ref[...] += land[i].astype(F32)
    finish(deals)


def exchange_key_grads(p, m_sum):
    outs = [((ROWS, 128), F32), ((MEMBERS, 32, 1536), BF)]
    scratch = [pltpu.VMEM((ROWS, 128), BF), pltpu.VMEM((3, ROWS, 128), BF)]
    scratch += [DMA, DMA((3,)), DMA((3,))] + DEAL_SEMS
    args = (p.reshape(4, ROWS, 128), m_sum.reshape(MEMBERS, 32, 1536))
    return call(
        key_grads_kernel, 5, "exchange_key_grads", args, [HBM] * 2, outs, [VMEM, HBM], scratch
    )


def last_kernel(*refs):
    ins, outs, slots_a, slots_c, others, sems_a, sems_c, deal, osems = split(
        refs, 4, 2, 4, 4, 3, 5, 3, 3, 3
    )
    p_ref, rows_ref, g_resid, ag_ref = ins
    input_grad, dealt = outs
    total, grad, a_sum = others
    greet(members() + across())
    t = lax.axis_index("t")
    state_a = scatter_start(p_ref, slots_a, sems_a)
    state_c = reduce_start(ag_ref, slots_c, sems_c)
    sent_a = scatter_send(state_a, slots_a, sems_a)
    reduce_pass(state_c, slots_c, sems_c)
    scatter_total(state_a, sent_a, slots_a, total)
    rows = rows_ref[...]
    inverse = scale_rows(rows)
    grad[...] = g_resid[...] + norm_back(rows * inverse, inverse, total[...])
    osend, orecv, local = osems
    copies = [
        pltpu.make_async_copy(grad, input_grad.at[t], local),
        remote(grad, input_grad.at[t], osend, orecv, other_core()),
    ]
    for c in copies:
        c.start()
    reduce_total(state_c, slots_c, a_sum)
    finish(deal_start(a_sum.reshape(MEMBERS, 32, 384), dealt, deal) + copies)


def last_exchange(p, rows, g_resid, grads):
    slots = (MEMBERS, 2, HALF, D)
    outs = [((2, HALF, D), F32), ((MEMBERS, 32, 384), BF)]
    scratch = scatter_slots(D) + reduce_slots(384)
    scratch += [pltpu.VMEM((HALF, D), F32), pltpu.VMEM((HALF, D), F32), pltpu.VMEM((256, 384), BF)]
    scratch += SCATTER_SEMS + REDUCE_SEMS + DEAL_SEMS + [DMA, DMA, DMA]
    args = (p.reshape(slots), rows, g_resid, grads.reshape(2, 4, 256, 384))
    input_grad, dealt = call(
        last_kernel, 6, "last_exchange", args, [HBM, VMEM, VMEM, HBM], outs, [HBM, HBM], scratch
    )
    return input_grad.reshape(2 * HALF, D), dealt


def abt(left, right):
    return lax.dot_general(left, right, (((1,), (1,)), ((), ())), preferred_element_type=F32)


def atb(left, right):
    return lax.dot_general(left, right, (((0,), (0,)), ((), ())), preferred_element_type=F32)


def attend_kernel(lo_ref, hi_ref, q_ref, kv_ref, kvt_ref, qi_ref, st_ref, o_ref, lse_ref):
    i = pl.program_id(0)
    q = q_ref[...]
    row, start = qi_ref[...], st_ref[...]
    wide = q.shape[0]

    def step(j, carry):
        top, total, acc = carry
        base = pl.multiple_of(j * KB, KB)
        s = abt(kv_ref[pl.ds(base, KB), :], q)
        key = base + lax.broadcasted_iota(jnp.int32, (KB, wide), 0)
        s = jnp.where((key <= row) & (key >= start), s, -1e30)
        new_top = jnp.maximum(top, jnp.max(s, axis=0, keepdims=True))
        p = jnp.exp(s - new_top)
        fade = jnp.exp(top - new_top)
        total = total * fade + jnp.sum(p, axis=0, keepdims=True)
        acc = acc * fade + jnp.dot(
            kvt_ref[:, pl.ds(base, KB)], p.astype(BF), preferred_element_type=F32
        )
        return (new_top, total, acc)

    init = (
        jnp.full((1, wide), -1e30, F32),
        jnp.zeros((1, wide), F32),
        jnp.zeros((2 * HEAD_DIM, wide), F32),
    )
    top, total, acc = lax.fori_loop(lo_ref[i], hi_ref[i], step, init)
    o_ref[...] = acc / total
    lse_ref[...] = top + jnp.log(total)


def attend_back_kernel(
    lo_ref, hi_ref, q_ref, g_ref, kv_ref, kvt_ref, qi_ref, st_ref, lse_ref, dot_ref, dq_ref, dkv_ref, acc_ref
):
    i = pl.program_id(0)
    q, g = q_ref[...], g_ref[...]
    row, start, lse, row_dot = qi_ref[...], st_ref[...], lse_ref[...], dot_ref[...]
    wide = q.shape[0]

    @pl.when(i == 0)
    def _():
        acc_ref[...] = jnp.zeros_like(acc_ref)

    def step(j, dq):
        base = pl.multiple_of(j * KB, KB)
        kv = kv_ref[pl.ds(base, KB), :]
        s = abt(kv, q)
        key = base + lax.broadcasted_iota(jnp.int32, (KB, wide), 0)
        s = jnp.where((key <= row) & (key >= start), s, -1e30)
        p = jnp.exp(s - lse)
        ds = (p * (abt(kv, g) - row_dot)).astype(BF)
        acc_ref[pl.ds(base, KB), :] += jnp.dot(ds, q, preferred_element_type=F32) + jnp.dot(
            p.astype(BF), g, preferred_element_type=F32
        )
        return dq + jnp.dot(kvt_ref[:, pl.ds(base, KB)], ds, preferred_element_type=F32)

    dq_ref[...] = lax.fori_loop(
        lo_ref[i], hi_ref[i], step, jnp.zeros((2 * HEAD_DIM, wide), F32)
    )

    @pl.when(i == pl.num_programs(0) - 1)
    def _():
        dkv_ref[...] = acc_ref[...].astype(BF)


def whole(shape):
    return pl.BlockSpec(shape, lambda i: (0,) * len(shape))


def block(rows, columns):
    return pl.BlockSpec((None, rows, columns), lambda i: (i, 0, 0))


BLOCKS = ROWS // QB
WIDE = 2 * QB
SCALARS = pl.BlockSpec(memory_space=pltpu.SMEM)


def attend(lo, hi, q, kv, kvt, row, start):
    return pl.pallas_call(
        attend_kernel,
        grid=(BLOCKS,),
        out_shape=[
            jax.ShapeDtypeStruct((BLOCKS, 128, WIDE), F32),
            jax.ShapeDtypeStruct((BLOCKS, 1, WIDE), F32),
        ],
        in_specs=[
            SCALARS,
            SCALARS,
            block(WIDE, 128),
            whole((LENGTH, 128)),
            whole((128, LENGTH)),
            block(1, WIDE),
            block(1, WIDE),
        ],
        out_specs=[block(128, WIDE), block(1, WIDE)],
        compiler_params=pltpu.CompilerParams(vmem_limit_bytes=48 * 2**20),
        cost_estimate=pl.CostEstimate(
            flops=2_000_000_000, bytes_accessed=60_000_000, transcendentals=4_000_000
        ),
        name="attend",
    )(lo, hi, q, kv, kvt, row, start)


def attend_back(lo, hi, q, g, kv, kvt, row, start, lse, row_dot):
    return pl.pallas_call(
        attend_back_kernel,
        grid=(BLOCKS,),
        out_shape=[
            jax.ShapeDtypeStruct((BLOCKS, 128, WIDE), F32),
            jax.ShapeDtypeStruct((LENGTH, 128), BF),
        ],
        in_specs=[
            SCALARS,
            SCALARS,
            block(WIDE, 128),
            block(WIDE, 128),
            whole((LENGTH, 128)),
            whole((128, LENGTH)),
            block(1, WIDE),
            block(1, WIDE),
            block(1, WIDE),
            block(1, WIDE),
        ],
        out_specs=[block(128, WIDE), whole((LENGTH, 128))],
        scratch_shapes=[pltpu.VMEM((LENGTH, 128), F32)],
        compiler_params=pltpu.CompilerParams(vmem_limit_bytes=48 * 2**20),
        cost_estimate=pl.CostEstimate(
            flops=5_000_000_000, bytes_accessed=120_000_000, transcendentals=4_000_000
        ),
        name="attend_back",
    )(lo, hi, q, g, kv, kvt, row, start, lse, row_dot)


def swap_cores(x):
    return lax.ppermute(x, "t", [(0, 1), (1, 0)])


def rope_frequency():
    half_size = HEAD_DIM // 2
    base_freq = 500000.0 ** (-(jnp.arange(half_size, dtype=F32) * 2.0 / HEAD_DIM))
    wavelength = 2.0 * math.pi / base_freq
    smooth = (8192.0 / wavelength - 1.0) / 3.0
    blended = (1.0 - smooth) * base_freq / 32.0 + smooth * base_freq
    return jnp.where(
        wavelength < 2048.0, base_freq, jnp.where(wavelength > 8192.0, base_freq / 32.0, blended)
    )


def rotate(values, cos_tab, sin_tab):
    rows = values.shape[0]
    v = values.reshape(rows, -1, 2, HEAD_DIM // 2)
    a, b = v[:, :, 0], v[:, :, 1]
    c, s = cos_tab[:, None, :], sin_tab[:, None, :]
    return jnp.stack([a * c - b * s, b * c + a * s], axis=2).reshape(rows, -1)


def adamw(weight, first_moment, second_moment, gradient, step_rate):
    first_new = 0.9 * first_moment + 0.1 * gradient
    second_new = 0.95 * second_moment + 0.05 * gradient * gradient
    corrected = first_new / (1.0 - 0.9**STEP) / (jnp.sqrt(second_new / (1.0 - 0.95**STEP)) + 1e-08)
    return (first_new, second_new, weight - step_rate * (corrected + 0.1 * weight))


def slots(w, columns):
    return w.reshape(w.shape[0], -1, columns).transpose(1, 0, 2)


def unslots(g):
    return g.transpose(1, 0, 2).reshape(g.shape[1], -1)


def heads_apart(x):
    return x.reshape(BLOCKS, QB, 2, HEAD_DIM).transpose(0, 2, 1, 3).reshape(BLOCKS, WIDE, HEAD_DIM)


def heads_beside(x):
    return x.reshape(BLOCKS, HEAD_DIM, 2, QB).transpose(0, 3, 2, 1).reshape(ROWS, 2 * HEAD_DIM)


def body(
    tokens,
    segments,
    cotangent,
    query_weight,
    key_weight,
    value_weight,
    output_weight,
    gate_weight,
    up_weight,
    down_weight,
    norm_gain_pair,
    query_first,
    key_first,
    value_first,
    output_first,
    gate_first,
    up_first,
    down_first,
    gains_first,
    query_second,
    key_second,
    value_second,
    output_second,
    gate_second,
    up_second,
    down_second,
    gains_second,
):
    t = lax.axis_index("t")
    x_place = lax.axis_index("x")

    gains = norm_gain_pair.astype(BF).astype(F32)
    gain_a, gain_m = gains[0][:, None], gains[1][:, None]
    low = lambda w: w.astype(BF).astype(F32)
    fold = lambda g, w: (g * low(w)).astype(BF)
    twice = lambda w: jnp.repeat(slots(w, HEAD_DIM), 2, axis=0)
    qkv_slots = jnp.concatenate(
        [
            slots(fold(gain_a, query_weight), 128),
            twice(fold(gain_a, key_weight)),
            twice(fold(gain_a, value_weight)),
        ],
        axis=2,
    )
    out_slots = slots(output_weight.astype(BF).T, 128)
    gate_up_slots = jnp.concatenate(
        [slots(fold(gain_m, gate_weight), 512), slots(fold(gain_m, up_weight), 512)], axis=2
    )
    down_slots = slots(down_weight.astype(BF).T, 512)

    rows = lax.dynamic_slice_in_dim(tokens[0], t * HALF, HALF, 0).astype(F32)
    unit_a = rows * scale_rows(rows)
    all_a, seg, w_qkv, w_out = first_exchange(
        unit_a.astype(BF), jnp.broadcast_to(segments, (8, 128)), qkv_slots, out_slots
    )
    segment = seg[:, :, 0, :].reshape(LENGTH)
    index = jnp.arange(LENGTH, dtype=jnp.int32)
    previous = jnp.concatenate([jnp.full((1,), -1, jnp.int32), segment[:-1]])
    starts = lax.cummax(jnp.where(segment != previous, index, 0), axis=0)
    first_row = x_place * ROWS
    own_start = lax.dynamic_slice_in_dim(starts, first_row, ROWS, 0)
    own_index = first_row + jnp.arange(ROWS, dtype=jnp.int32)
    angles = (own_index - own_start).astype(F32)[:, None] * rope_frequency()[None, :]
    cos_tab, sin_tab = jnp.cos(angles), jnp.sin(angles)
    lo = own_start.reshape(BLOCKS, QB)[:, 0] // KB
    hi = (first_row + (jnp.arange(BLOCKS, dtype=jnp.int32) + 1) * QB + KB - 1) // KB
    by_block = lambda v: jnp.concatenate([v.reshape(BLOCKS, 1, QB)] * 2, axis=2)
    row_ids, row_starts = by_block(own_index), by_block(own_start)

    qkv = jnp.dot(all_a, w_qkv, preferred_element_type=F32)
    rotated = rotate(qkv[:, :192], cos_tab, sin_tab).astype(BF)
    kv_own = jnp.concatenate([rotated[:, 128:], qkv[:, 192:].astype(BF)], axis=1)
    kv, gate_up_part, down_part = exchange_keys(kv_own, gate_up_slots, down_slots)
    kvt = kv.T
    scale = HEAD_DIM ** (-0.5)
    q_low = heads_apart(rotated[:, :128])
    nothing = jnp.zeros_like(q_low)
    q_wide = jnp.concatenate([q_low * jnp.asarray(scale, BF), nothing], axis=2)
    o_cols, lse = attend(lo, hi, q_wide, kv, kvt, row_ids, row_starts)
    o_full = heads_beside(o_cols[:, HEAD_DIM:])
    o_low = o_full.astype(BF)

    cot_half = lax.dynamic_slice_in_dim(cotangent[0], t * HALF, HALF, 0)
    resid, all_m, all_g, w_gate_up, w_down = forward_exchange(
        abt(o_low, w_out).astype(BF), rows, cot_half, gate_up_part, down_part
    )
    gate_up = jnp.dot(all_m, w_gate_up, preferred_element_type=F32)
    gate, up = gate_up[:, :512], gate_up[:, 512:]
    sig = jax.nn.sigmoid(gate)
    silu = gate * sig
    act = (silu * up).astype(BF)

    g_act = jnp.dot(all_g, w_down, preferred_element_type=F32)
    g_gate = g_act * up * sig * (1.0 + gate * (1.0 - sig))
    g_up = g_act * silu
    g_gate_up = jnp.concatenate([g_gate, g_up], axis=1).astype(BF)
    mlp_grad = jnp.concatenate([atb(all_m, g_gate_up), atb(all_g, act)], axis=1).astype(BF)
    g_resid, all_r, block_out, mlp_part = backward_exchange(
        abt(g_gate_up, w_gate_up).astype(BF),
        abt(act, w_down).astype(BF),
        resid,
        cot_half,
        mlp_grad,
    )

    g_o = jnp.dot(all_r, w_out, preferred_element_type=F32).astype(BF)
    row_dot = (
        (o_full * g_o.astype(F32))
        .reshape(BLOCKS, QB, 2, HEAD_DIM)
        .sum(axis=3)
        .transpose(0, 2, 1)
        .reshape(BLOCKS, 1, WIDE)
    )
    g_wide = jnp.concatenate([nothing, heads_apart(g_o)], axis=2)
    dq_cols, dkv = attend_back(
        lo, hi, q_wide, g_wide, kv, kvt, row_ids, row_starts, lse, row_dot
    )
    g_kv, mlp_dealt = exchange_key_grads(dkv, mlp_part)
    g_q = heads_beside(dq_cols[:, :HEAD_DIM]) * scale
    g_turned = rotate(jnp.concatenate([g_q, g_kv[:, :HEAD_DIM]], axis=1), cos_tab, -sin_tab)
    g_qkv = jnp.concatenate([g_turned, g_kv[:, HEAD_DIM:]], axis=1).astype(BF)
    attn_grad = jnp.concatenate([atb(all_a, g_qkv), atb(all_r, o_low)], axis=1).astype(BF)
    input_grad, attn_dealt = last_exchange(
        abt(g_qkv, w_qkv).astype(BF), rows, g_resid, attn_grad
    )
    mlp_sum, attn_sum = mlp_dealt.astype(F32), attn_dealt.astype(F32)

    pairs = lambda g: unslots(g.reshape(4, 2, 32, HEAD_DIM).sum(axis=1))
    q_sum = unslots(attn_sum[:, :, :128])
    k_sum = pairs(attn_sum[:, :, 128:192])
    v_sum = pairs(attn_sum[:, :, 192:256])
    gate_sum = unslots(mlp_sum[:, :, :512])
    up_sum = unslots(mlp_sum[:, :, 512:1024])
    dots = lambda g, w: jnp.sum(g * low(w), axis=1)
    gains_half = jnp.stack(
        [
            dots(q_sum, query_weight) + dots(k_sum, key_weight) + dots(v_sum, value_weight),
            dots(gate_sum, gate_weight) + dots(up_sum, up_weight),
        ],
        axis=0,
    )
    gains_grad = gains_half + swap_cores(gains_half)
    query_grad, key_grad, value_grad = gain_a * q_sum, gain_a * k_sum, gain_a * v_sum
    gate_grad, up_grad = gain_m * gate_sum, gain_m * up_sum
    output_grad = unslots(attn_sum[:, :, 256:]).T
    down_grad = unslots(mlp_sum[:, :, 1024:]).T
    wide_rate = 2.0 * D ** (-0.5)
    outs = [block_out[None], input_grad[None]]
    for weight, first, second, grad, rate in (
        (query_weight, query_first, query_second, query_grad, wide_rate),
        (key_weight, key_first, key_second, key_grad, wide_rate),
        (value_weight, value_first, value_second, value_grad, wide_rate),
        (output_weight, output_first, output_second, output_grad, 2.0 * (4 * HEAD_DIM) ** (-0.5)),
        (gate_weight, gate_first, gate_second, gate_grad, wide_rate),
        (up_weight, up_first, up_second, up_grad, wide_rate),
        (down_weight, down_first, down_second, down_grad, 2.0 * FF ** (-0.5)),
        (norm_gain_pair, gains_first, gains_second, gains_grad, 1.5),
    ):
        outs.append(grad)
        outs.extend(adamw(weight, first, second, grad, rate))
    return tuple(outs)


def solution(mesh):
    split = Mesh(
        mesh.devices.reshape(tuple(SIZES.values())), tuple(SIZES)
    )
    heads = ("x", "z", "yl")
    every = ("dp", "x", "z", "yl")
    acts = P("dp", heads, None)
    rows_cut = P(every, "t")
    columns_cut = P("t", every)
    gains = P(None, every)
    weights = (rows_cut,) * 3 + (columns_cut,) + (rows_cut,) * 2 + (columns_cut, gains)
    in_specs = (acts, P("dp", heads), acts) + weights * 3
    out_specs = (acts, acts) + tuple(spec for spec in weights for _ in range(4))
    return jax.shard_map(
        body, mesh=split, in_specs=in_specs, out_specs=out_specs, check_vma=False
    )
```

```python
import functools
import itertools
import math

import jax
import jax.numpy as jnp
from jax import lax
from jax.experimental import pallas as pl
from jax.experimental.pallas import tpu as pltpu
from jax.sharding import Mesh
from jax.sharding import PartitionSpec as P

D = 2048
FF = 8192
HEADS = 32
KV_HEADS = 8
HEAD_DIM = 64
STEP = 10
EPS = 1e-05

SIZES = {"dp": 2, "x": 4, "z": 4, "yl": 2, "t": 2}
GROUP = ("z", "yl")
CROSS = ("dp", "x")
MEMBERS = 8
HALF = 64
ROWS = 1024
LENGTH = 4096
DOC_MOST = 2048
QB = 256
KB = 512
BLOCKS = ROWS // QB
WIDE = 2 * QB
BF = jnp.bfloat16
F32 = jnp.float32


def shifts(axes):
    return list(itertools.product(*[range(SIZES[a]) for a in axes]))


def place(axes, shift, sign=1):
    index = 0
    for a, s in zip(axes, shift):
        index = index * SIZES[a] + lax.rem(
            lax.axis_index(a) + (s if sign > 0 else SIZES[a] - s), SIZES[a]
        )
    return index


def peer(axes, shift):
    return {
        a: lax.rem(lax.axis_index(a) + s, SIZES[a]) for a, s in zip(axes, shift) if s
    }


def other_core():
    return {"t": 1 - lax.axis_index("t")}


def hail(devices):
    for device in devices:
        pl.semaphore_signal(
            pltpu.get_barrier_semaphore(),
            inc=1,
            device_id=device,
            device_id_type=pl.DeviceIdType.MESH,
        )


def await_all(devices):
    pl.semaphore_wait(pltpu.get_barrier_semaphore(), len(devices))


def greet(devices):
    hail(devices)
    await_all(devices)


def remote(src, dst, send, recv, device):
    return pltpu.make_async_remote_copy(
        src_ref=src,
        dst_ref=dst,
        send_sem=send,
        recv_sem=recv,
        device_id=device,
        device_id_type=pl.DeviceIdType.MESH,
    )


def abt(left, right):
    return lax.dot_general(left, right, (((1,), (1,)), ((), ())), preferred_element_type=F32)


def atb(left, right):
    return lax.dot_general(left, right, (((0,), (0,)), ((), ())), preferred_element_type=F32)


DMA = pltpu.SemaphoreType.DMA
HBM = pl.BlockSpec(memory_space=pl.ANY)
VMEM = pl.BlockSpec(memory_space=pltpu.VMEM)
MOVES = shifts(GROUP)[1:]
TURNS = (1, 3, 2)


def members():
    return [other_core()] + [peer(GROUP, s) for s in MOVES]


def across():
    return [peer(("dp",), (1,))] + [peer(("x",), (s,)) for s in TURNS]


def finish(copies):
    for c in copies:
        c.wait()


INSIDE = ("yl", "z")
ACROSS = ("dp", "x")


def ring_places(axes):
    pair, ring = axes
    p, q = lax.axis_index(pair), lax.axis_index(ring)
    mate, up, down = {pair: 1 - p}, {ring: lax.rem(q + 1, 4)}, {ring: lax.rem(q + 3, 4)}
    return p, q, mate, up, down


RING_GATHER_SEMS = [DMA((9,)), DMA((9,)), DMA]


class RingGather:
    def __init__(self, x_ref, slot, rows, axes, sems, arrived=None):
        self.x_ref, self.slot, self.half, self.axes = x_ref, slot, rows // 2, axes
        self.ssem, self.rsem, self.local = sems
        self.copies = {}
        self.arrived = arrived if arrived is not None else lambda part: None
        p, q, mate, up, down = ring_places(axes)
        self.own = pltpu.make_async_copy(x_ref, slot(p, q), self.local)
        self.own.start()
        for k, to in enumerate((mate, up, down)):
            self.go(k, x_ref, slot(p, q), to)

    def go(self, k, src, dst, to):
        c = remote(src, dst, self.ssem.at[k], self.rsem.at[k], to)
        c.start()
        self.copies[k] = c

    def part(self, p, q, which=None):
        ref = self.slot(p, q)
        return ref if which is None else ref.at[pl.ds(which * self.half, self.half)]

    def pass_mate(self):
        p, q, _, up, down = ring_places(self.axes)
        self.copies[0].wait_recv()
        part = self.part(1 - p, q)
        self.go(3, part, part, up)
        self.go(4, part, part, down)
        self.arrived(part)

    def pass_ring(self, column):
        p, q, _, up, down = ring_places(self.axes)
        p = p if column == 0 else 1 - p
        at = 1 if column == 0 else 3
        for i, (step, to) in enumerate(((3, up), (1, down))):
            self.copies[at + i].wait_recv()
            there = lax.rem(q + step, 4)
            part = self.part(p, there, i)
            self.go(5 + 2 * column + i, part, part, to)
            self.arrived(self.part(p, there))

    def finish(self):
        p, q, _, _, _ = ring_places(self.axes)
        far = lax.rem(q + 2, 4)
        for column, p in enumerate((p, 1 - p)):
            for i in range(2):
                self.copies[5 + 2 * column + i].wait_recv()
            self.arrived(self.part(p, far))
        self.own.wait()
        for c in self.copies.values():
            c.wait_send()


TOKEN_GATHER_SEMS = RING_GATHER_SEMS + [DMA((8,)), DMA((8,))]


class TokenGather(RingGather):
    def __init__(self, x_ref, out_ref, sems):
        t = lax.axis_index("t")
        self.passed, self.tsend, self.trecv = [], sems[3], sems[4]
        slot = lambda p, q: out_ref.at[2 * q + p, t]
        super().__init__(x_ref, slot, HALF, INSIDE, sems[:3], self.to_core)
        p, q, _, _, _ = ring_places(INSIDE)
        self.to_core(slot(p, q), x_ref)

    def to_core(self, part, src=None):
        k = len(self.passed)
        c = remote(part if src is None else src, part, self.tsend.at[k], self.trecv.at[k], other_core())
        c.start()
        self.passed.append(c)

    def finish(self):
        super().finish()
        finish(self.passed)


def add_rows(out_ref, terms, rows, step_rows):
    def step(r, carry):
        at = pl.ds(pl.multiple_of(r * step_rows, step_rows), step_rows)
        total = terms[0][at, :].astype(F32)
        for term in terms[1:]:
            total = total + term[at, :].astype(F32)
        out_ref[at, :] = total.astype(out_ref.dtype)
        return carry

    lax.fori_loop(0, rows // step_rows, step, 0)


RING_SCATTER_SEMS = [DMA((13,)), DMA((13,))]


def ring_scatter_slots(rows, wide):
    half = rows // 2
    return [
        pltpu.VMEM((2, half, wide), BF),
        pltpu.VMEM((2, half, wide), BF),
        pltpu.VMEM((2, rows, wide), BF),
        pltpu.VMEM((2, rows, wide), BF),
        pltpu.VMEM((rows, wide), BF),
    ]


class RingScatter:
    def __init__(self, rows, axes, slots, sems):
        self.rows, self.half, self.axes = rows, rows // 2, axes
        self.far_up, self.far_down, self.from_down, self.from_up, self.back = slots
        self.ssem, self.rsem = sems
        self.copies = {}

    def go(self, k, src, dst, to):
        c = remote(src, dst, self.ssem.at[k], self.rsem.at[k], to)
        c.start()
        self.copies[k] = c

    def part(self, p, q, at):
        return self.held(p, q).at[at]

    def halves(self):
        return pl.ds(0, self.half), pl.ds(self.half, self.half)

    def add(self, out_ref, terms, rows):
        add_rows(out_ref, terms, rows, 16)

    def send_far(self, p):
        _, _, _, up, down = ring_places(self.axes)
        first, second = self.halves()
        self.go(2 * p, self.part(p, 2, first), self.far_up.at[p], up)
        self.go(2 * p + 1, self.part(p, 2, second), self.far_down.at[p], down)

    def send_near(self, p):
        _, _, _, up, down = ring_places(self.axes)
        first, second = self.halves()
        self.go(4 + 2 * p, self.part(p, 1, second), self.from_down.at[p, second], up)
        self.go(5 + 2 * p, self.part(p, 3, first), self.from_up.at[p, first], down)

    def send_joined(self, p):
        _, _, _, up, down = ring_places(self.axes)
        first, second = self.halves()
        self.copies[2 * p].wait_recv()
        part = self.part(p, 1, first)
        self.add(part, [part, self.far_up.at[p]], self.half)
        self.go(8 + 2 * p, part, self.from_down.at[p, first], up)
        self.copies[2 * p + 1].wait_recv()
        part = self.part(p, 3, second)
        self.add(part, [part, self.far_down.at[p]], self.half)
        self.go(9 + 2 * p, part, self.from_up.at[p, second], down)

    def arrivals(self, p):
        for k in (4 + 2 * p, 5 + 2 * p, 8 + 2 * p, 9 + 2 * p):
            self.copies[k].wait_recv()

    def send_mate(self):
        _, _, mate, _, _ = ring_places(self.axes)
        self.arrivals(1)
        part = self.held(1, 0)
        self.add(part, [part, self.from_down.at[1], self.from_up.at[1]], self.rows)
        self.go(12, part, self.back, mate)

    def total(self, out_ref):
        self.arrivals(0)
        self.copies[12].wait_recv()
        self.add(
            out_ref,
            [self.held(0, 0), self.from_down.at[0], self.from_up.at[0], self.back],
            self.rows,
        )
        for c in self.copies.values():
            c.wait_send()


TOKEN_SCATTER_SEMS = RING_SCATTER_SEMS + [DMA((4, 2)), DMA((4, 2))]


def token_scatter_slots():
    return ring_scatter_slots(HALF, D) + [pltpu.VMEM((4, 2, HALF, D), BF)]


STAGE = pltpu.VMEM((4, 2, 2, HALF, D), BF)


class TokenScatter(RingScatter):
    def __init__(self, a_ref, w_ref, slots, stage, sems):
        super().__init__(HALF, INSIDE, slots[:5], sems[:2])
        self.a_ref, self.w_ref = a_ref, w_ref
        self.stage, self.theirs = stage, slots[5]
        self.tsend, self.trecv = sems[2:]
        self.swaps = {}

    def pair_place(self, p):
        own = lax.axis_index("yl")
        return own if p == 0 else 1 - own

    def held(self, p, q):
        return self.stage.at[q, self.pair_place(p), lax.axis_index("t")]

    def make(self, q):
        row = lax.rem(lax.axis_index("z") + q, 4) * 256
        a = self.a_ref[pl.ds(pl.multiple_of(row, 256), 256), :]

        def step(n, carry):
            at = pl.ds(pl.multiple_of(n * 512, 512), 512)
            product = abt(a, self.w_ref[at, :]).astype(BF)
            self.stage[q, :, :, :, at] = product.reshape(2, 2, HALF, 512)
            return carry

        lax.fori_loop(0, D // 512, step, 0)

    def swap(self, q):
        t = lax.axis_index("t")
        for p in (1, 0):
            at = self.pair_place(p)
            c = remote(
                self.stage.at[q, at, 1 - t],
                self.theirs.at[q, at],
                self.tsend.at[q, p],
                self.trecv.at[q, p],
                other_core(),
            )
            c.start()
            self.swaps[q, p] = c

    def pair(self, p, q):
        self.swaps[q, p].wait_recv()
        part = self.held(p, q)
        self.add(part, [part, self.theirs.at[q, self.pair_place(p)]], HALF)

    def total(self, out_ref):
        super().total(out_ref)
        for c in self.swaps.values():
            c.wait_send()

    def steps(self, started=False):
        if not started:
            self.make(2)
            self.swap(2)
        self.make(1)
        self.swap(1)
        yield
        self.pair(1, 2)
        self.send_far(1)
        self.pair(0, 2)
        self.send_far(0)
        self.make(3)
        self.swap(3)
        yield
        for q in (1, 3):
            self.pair(1, q)
            self.pair(0, q)
        self.send_near(1)
        self.send_near(0)
        self.make(0)
        self.swap(0)
        yield
        self.send_joined(1)
        self.send_joined(0)
        yield
        self.pair(1, 0)
        self.pair(0, 0)
        yield
        self.send_mate()
        yield


BY_NEED = [(1, 2), (0, 2), (1, 1), (1, 3), (0, 1), (0, 3), (1, 0), (0, 0)]


def grad_scatter_slots(wide):
    return ring_scatter_slots(256, wide) + [pltpu.VMEM((2, 4, 256, wide), BF)]


COLUMNS = pltpu.VMEM((2, 2, ROWS, 256), BF)


class GradScatter(RingScatter):
    def __init__(self, pairs, slots, columns, sems):
        super().__init__(256, ACROSS, slots[:5], sems[:2])
        self.pairs, self.blocks, self.columns, self.lsem = pairs, slots[5], columns, sems[2]
        self.loads = {}
        self.done = 0
        self.load(0)
        self.load(1)

    def held(self, p, q):
        return self.blocks.at[p, q]

    def load(self, k):
        p, q = BY_NEED[k]
        dp, x = lax.axis_index("dp"), lax.axis_index("x")
        row = (dp if p == 0 else 1 - dp) * 4 + lax.rem(x + q, 4)
        at = pl.ds(pl.multiple_of(row * 256, 256), 256)
        for i, (x_ref, _) in enumerate(self.pairs):
            c = pltpu.make_async_copy(
                x_ref.at[:, at], self.columns.at[k % 2, i], self.lsem.at[k % 2, i]
            )
            c.start()
            self.loads[k, i] = c

    def make(self):
        k = self.done
        p, q = BY_NEED[k]
        start = 0
        for i, (_, g_ref) in enumerate(self.pairs):
            self.loads[k, i].wait()
            wide = g_ref.shape[1]
            self.blocks[p, q, :, start : start + wide] = atb(
                self.columns[k % 2, i], g_ref[...]
            ).astype(BF)
            start += wide
        self.done = k + 1
        if k + 2 < len(BY_NEED):
            self.load(k + 2)

    def steps(self):
        self.make()
        self.send_far(1)
        yield
        self.make()
        self.send_far(0)
        yield
        self.make()
        self.make()
        self.send_near(1)
        yield
        self.make()
        self.make()
        self.send_near(0)
        yield
        self.send_joined(1)
        self.send_joined(0)
        yield
        self.make()
        yield
        self.make()
        yield
        self.send_mate()
        yield


GRAD_SCATTER_SEMS = RING_SCATTER_SEMS + [DMA((2, 2))]


def weight_gather(x_ref, out_ref, sems):
    return RingGather(x_ref, lambda p, q: out_ref.at[p, q], 256, ACROSS, sems)


DEAL_SEMS = [DMA((7,)), DMA((7,)), DMA]


def deal_start(x_ref, out_ref, sems):
    send, recv, local = sems
    me = place(GROUP, (0, 0))
    own = pltpu.make_async_copy(x_ref.at[me], out_ref.at[me], local)
    own.start()
    copies = []
    for i, s in enumerate(MOVES):
        c = remote(
            x_ref.at[place(GROUP, s)], out_ref.at[me], send.at[i], recv.at[i], peer(GROUP, s)
        )
        c.start()
        copies.append(c)
    return [own] + copies


def split(refs, *counts):
    parts, at = [], 0
    for count in counts:
        parts.append(refs[at : at + count])
        at += count
    assert at == len(refs)
    return parts


def scale_rows(x):
    return lax.rsqrt(jnp.mean(x * x, axis=1, keepdims=True) + EPS)


def norm_back(unit, inverse, grad):
    return inverse * (grad - unit * jnp.mean(grad * unit, axis=1, keepdims=True))


def call(kernel, collective_id, name, args, in_specs, outs, out_specs, scratch):
    sent = 60_000_000
    return pl.pallas_call(
        kernel,
        out_shape=[jax.ShapeDtypeStruct(s, d) for s, d in outs],
        in_specs=in_specs,
        out_specs=out_specs,
        scratch_shapes=scratch,
        compiler_params=pltpu.CompilerParams(
            collective_id=collective_id, has_side_effects=True, vmem_limit_bytes=60 * 2**20
        ),
        cost_estimate=pl.CostEstimate(flops=0, bytes_accessed=sent, transcendentals=0),
        name=name,
    )(*args)


def first_kernel(*refs):
    ins, outs, dealt, gather, deal_a, deal_b, ring_a, ring_b, seg_sems = split(
        refs, 4, 4, 2, 5, 3, 3, 3, 3, 5
    )
    x_ref, seg_ref, qkv_ref, wo_ref = ins
    all_ref, seg_out, w_qkv, w_out = outs
    part_a, part_b = dealt
    ssend, srecv, xsend, xrecv, slocal = seg_sems
    greet(members() + across())
    deals = deal_start(qkv_ref, part_a, deal_a) + deal_start(wo_ref, part_b, deal_b)
    me, x = place(GROUP, (0, 0)), lax.axis_index("x")
    seg_own = pltpu.make_async_copy(seg_ref, seg_out.at[x, me], slocal)
    seg_own.start()
    seg_copies = [seg_own]
    for i, s in enumerate(MOVES):
        c = remote(seg_ref, seg_out.at[x, me], ssend.at[i], srecv.at[i], peer(GROUP, s))
        c.start()
        seg_copies.append(c)
    tokens = TokenGather(x_ref, all_ref, gather)
    finish(deals)
    weights = [
        weight_gather(part_a.reshape(256, 256), w_qkv, ring_a),
        weight_gather(part_b.reshape(256, 128), w_out, ring_b),
    ]
    finish(seg_copies)
    crossed = []
    for i, to in enumerate(across()[1:]):
        c = remote(seg_out.at[x], seg_out.at[x], xsend.at[i], xrecv.at[i], to)
        c.start()
        crossed.append(c)
    everything = [tokens] + weights
    for g in everything:
        g.pass_mate()
    for g in everything:
        g.pass_ring(0)
    for g in everything:
        g.pass_ring(1)
    for g in everything:
        g.finish()
    finish(crossed)


def first_exchange(unit, segments, qkv_slots, out_slots):
    outs = [
        ((MEMBERS, 2, HALF, D), BF),
        ((4, MEMBERS, 8, 128), jnp.int32),
        ((2, 4, 256, 256), BF),
        ((2, 4, 256, 128), BF),
    ]
    scratch = [pltpu.VMEM((MEMBERS, 32, 256), BF), pltpu.VMEM((MEMBERS, 32, 128), BF)]
    scratch += TOKEN_GATHER_SEMS + DEAL_SEMS * 2 + RING_GATHER_SEMS * 2
    scratch += [DMA((7,)), DMA((7,)), DMA((3,)), DMA((3,)), DMA]
    args = (unit, segments, qkv_slots, out_slots)
    tokens, seg, w_qkv, w_out = call(
        first_kernel, 1, "first_exchange", args, [HBM] * 4, outs, [HBM] * 4, scratch
    )
    return tokens.reshape(ROWS, D), seg, w_qkv.reshape(D, 256), w_out.reshape(D, 128)


def attend_block(q_ref, kv_ref, kvt_ref, start_ref, o_ref, lse_ref, low_ref, b):
    x = lax.axis_index("x")
    at = pl.ds(pl.multiple_of(b * QB, QB), QB)
    first = x * ROWS + b * QB
    q = jnp.concatenate([q_ref[0, :, at], q_ref[1, :, at]], axis=1)
    own = first + lax.broadcasted_iota(jnp.int32, (1, QB), 1)
    row = jnp.concatenate([own, own], axis=1)
    start = start_ref[:, at]
    start = jnp.concatenate([start, start], axis=1)

    def step(j, carry):
        top, total, acc = carry
        base = pl.multiple_of(j * KB, KB)
        s = jnp.dot(kv_ref[pl.ds(base, KB), :], q, preferred_element_type=F32)
        key = base + lax.broadcasted_iota(jnp.int32, (KB, WIDE), 0)
        s = jnp.where((key <= row) & (key >= start), s, -1e30)
        new_top = jnp.maximum(top, jnp.max(s, axis=0, keepdims=True))
        p = jnp.exp(s - new_top)
        fade = jnp.exp(top - new_top)
        total = total * fade + jnp.sum(p, axis=0, keepdims=True)
        acc = acc * fade + jnp.dot(
            kvt_ref[:, pl.ds(base, KB)], p.astype(BF), preferred_element_type=F32
        )
        return (new_top, total, acc)

    init = (
        jnp.full((1, WIDE), -1e30, F32),
        jnp.zeros((1, WIDE), F32),
        jnp.zeros((2 * HEAD_DIM, WIDE), F32),
    )
    low = lax.max(first - (DOC_MOST - 1), 0) // KB
    high = (first + QB + KB - 1) // KB
    top, total, acc = lax.fori_loop(low, high, step, init)
    o = acc[HEAD_DIM:] / total
    lse = top + jnp.log(total)
    for h in range(2):
        o_ref[h, :, at] = o[:, h * QB : (h + 1) * QB]
        lse_ref[h : h + 1, at] = lse[:, h * QB : (h + 1) * QB]
    beside = jnp.concatenate([o[:, :QB], o[:, QB:]], axis=0)
    low_ref[at, :] = beside.T.astype(BF)


def forward_kernel(*refs):
    ins, outs, slots, others, sems, gather, rings, keys, deals = split(
        refs, 8, 10, 6, 5, 4, 10, 6, 3, 6
    )
    q_ref, start_ref, wo_ref, rows_ref, kv_own, cot_ref, gu_ref, down_ref = ins
    resid_ref, all_m, all_g, w_gu, w_down, kv_ref, kvt_ref, o_ref, lse_ref, low_ref = outs
    stage, total, unit, gu_part, down_part = others
    ksend, krecv, klocal = keys
    devices = members() + across()
    greet(devices)
    x, z = lax.axis_index("x"), lax.axis_index("z")
    own_keys = kv_ref.at[pl.ds(pl.multiple_of(x * ROWS, ROWS), ROWS)]
    key_copies = [pltpu.make_async_copy(kv_own, own_keys, klocal)]
    key_copies[0].start()
    for i, to in enumerate(across()[1:]):
        c = remote(kv_own, own_keys, ksend.at[i], krecv.at[i], to)
        c.start()
        key_copies.append(c)
    dealt = deal_start(gu_ref, gu_part, deals[:3]) + deal_start(down_ref, down_part, deals[3:])
    cots = TokenGather(cot_ref, all_g, gather[:5])
    finish(dealt)
    finish(key_copies)
    weights = [
        weight_gather(gu_part.reshape(256, 1024), w_gu, rings[:3]),
        weight_gather(down_part.reshape(256, 512), w_down, rings[3:]),
    ]

    def turn(c, carry):
        at = pl.ds(pl.multiple_of(c * KB, KB), KB)
        kvt_ref[:, at] = kv_ref[at, :].T
        return carry

    lax.fori_loop(0, LENGTH // KB, turn, 0)
    sums = TokenScatter(low_ref, wo_ref, slots, stage, sems)

    def attend(q):
        b = lax.rem(z + q, 4)
        attend_block(q_ref, kv_ref, kvt_ref, start_ref, o_ref, lse_ref, low_ref, b)
        sums.make(q)
        sums.swap(q)

    attend(2)
    cots.pass_mate()
    attend(1)
    sums.pair(1, 2)
    sums.send_far(1)
    sums.pair(0, 2)
    sums.send_far(0)
    cots.pass_ring(0)
    attend(3)
    for q in (1, 3):
        sums.pair(1, q)
        sums.pair(0, q)
    sums.send_near(1)
    sums.send_near(0)
    attend(0)
    sums.send_joined(1)
    sums.send_joined(0)
    for g in weights:
        g.pass_mate()
    sums.pair(1, 0)
    sums.pair(0, 0)
    cots.pass_ring(1)
    sums.send_mate()
    for g in weights:
        g.pass_ring(0)
    sums.total(total)
    resid = rows_ref[...] + total[...]
    resid_ref[...] = resid
    unit[...] = (resid * scale_rows(resid)).astype(BF)
    tokens = TokenGather(unit, all_m, gather[5:])
    tokens.pass_mate()
    for g in weights:
        g.pass_ring(1)
    tokens.pass_ring(0)
    tokens.pass_ring(1)
    for g in [cots, tokens] + weights:
        g.finish()


def forward_exchange(q, starts, w_out, rows, kv, cot, gate_up_slots, down_slots):
    slots = (MEMBERS, 2, HALF, D)
    outs = [
        ((HALF, D), F32),
        (slots, BF),
        (slots, BF),
        ((2, 4, 256, 1024), BF),
        ((2, 4, 256, 512), BF),
        ((LENGTH, 128), BF),
        ((128, LENGTH), BF),
        ((2, HEAD_DIM, ROWS), F32),
        ((2, ROWS), F32),
        ((ROWS, 128), BF),
    ]
    scratch = token_scatter_slots() + [
        STAGE,
        pltpu.VMEM((HALF, D), F32),
        pltpu.VMEM((HALF, D), BF),
        pltpu.VMEM((MEMBERS, 32, 1024), BF),
        pltpu.VMEM((MEMBERS, 32, 512), BF),
    ]
    scratch += TOKEN_SCATTER_SEMS + TOKEN_GATHER_SEMS * 2 + RING_GATHER_SEMS * 2
    scratch += [DMA((3,)), DMA((3,)), DMA] + DEAL_SEMS * 2
    args = (q, starts, w_out, rows, kv, cot, gate_up_slots, down_slots)
    resid, all_m, all_g, w_gu, w_down, kv, kvt, o, lse, o_low = call(
        forward_kernel,
        3,
        "forward_exchange",
        args,
        [VMEM] * 4 + [HBM] * 4,
        outs,
        [VMEM] + [HBM] * 4 + [VMEM] * 5,
        scratch,
    )
    return (
        resid,
        all_m.reshape(ROWS, D),
        all_g.reshape(ROWS, D),
        w_gu.reshape(D, 1024),
        w_down.reshape(D, 512),
        kv,
        kvt,
        o,
        lse,
        o_low,
    )


def turn_back(v, cos_tab, sin_tab):
    a, b = v[: HEAD_DIM // 2], v[HEAD_DIM // 2 :]
    return jnp.concatenate([a * cos_tab + b * sin_tab, b * cos_tab - a * sin_tab], axis=0)


def attend_back_block(q_ref, kv_ref, kvt_ref, start_ref, o_ref, lse_ref, g, acc_ref, b):
    at = pl.ds(pl.multiple_of(b * QB, QB), QB)
    first = lax.axis_index("x") * ROWS + b * QB
    q = jnp.concatenate([q_ref[0, :, at], q_ref[1, :, at]], axis=1)
    own = first + lax.broadcasted_iota(jnp.int32, (1, QB), 1)
    row = jnp.concatenate([own, own], axis=1)
    start = start_ref[:, at]
    start = jnp.concatenate([start, start], axis=1)
    lse = jnp.concatenate([lse_ref[0:1, at], lse_ref[1:2, at]], axis=1)
    beside = jnp.concatenate([g[:HEAD_DIM], g[HEAD_DIM:]], axis=1)
    o = jnp.concatenate([o_ref[0, :, at], o_ref[1, :, at]], axis=1)
    row_dot = jnp.sum(o * beside.astype(F32), axis=0, keepdims=True)
    g_wide = jnp.concatenate([jnp.zeros_like(beside), beside], axis=0)

    def step(j, dq):
        base = pl.multiple_of(j * KB, KB)
        kv = kv_ref[pl.ds(base, KB), :]
        s = jnp.dot(kv, q, preferred_element_type=F32)
        key = base + lax.broadcasted_iota(jnp.int32, (KB, WIDE), 0)
        s = jnp.where((key <= row) & (key >= start), s, -1e30)
        p = jnp.exp(s - lse)
        g_p = jnp.dot(kv, g_wide, preferred_element_type=F32)
        g_s = (p * (g_p - row_dot)).astype(BF)
        acc_ref[pl.ds(base, KB), :] += abt(g_s, q) + abt(p.astype(BF), g_wide)
        return dq + jnp.dot(kvt_ref[:, pl.ds(base, KB)], g_s, preferred_element_type=F32)

    low = lax.max(first - (DOC_MOST - 1), 0) // KB
    high = (first + QB + KB - 1) // KB
    return lax.fori_loop(low, high, step, jnp.zeros((2 * HEAD_DIM, WIDE), F32))


def backward_kernel(*refs):
    ins, outs, slots, mids, others, keys, sems, gsems, gather, ksems, csems, deals = split(
        refs, 21, 5, 18, 12, 12, 4, 12, 6, 5, 4, 7, 6
    )
    (
        g_ref, act_ref, wgu_ref, wdown_ref, resid_ref, cot_ref, wot_ref, q_ref, kv_ref, kvt_ref,
        start_ref, o_ref, lse_ref, low_ref, cos_ref, sin_ref, wqkv_ref, rows_ref,
        all_m, all_g, all_a,
    ) = ins
    input_grad, block_out, m_dealt, a_dealt, all_r = outs
    stage, columns, total, grad, g_resid, low, out_low, m_sum, a_sum, chunk, g_qkv, key_sum = others
    acc_ref, key_low, key_land, key_own = keys
    devices = members() + across()
    hail(devices)
    t, x = lax.axis_index("t"), lax.axis_index("x")
    sums = TokenScatter(g_ref, wgu_ref, slots[:6], stage, sems[:4])
    grads = GradScatter([(all_m, g_ref), (all_g, act_ref)], mids[:6], columns, gsems[:3])
    sums.make(2)
    await_all(devices)
    sums.swap(2)
    sum_steps, grad_steps = sums.steps(started=True), grads.steps()
    next(sum_steps)
    next(grad_steps)
    next(sum_steps)
    next(sum_steps)
    next(grad_steps)
    next(sum_steps)
    next(grad_steps)
    next(sum_steps)
    next(grad_steps)
    next(sum_steps)
    next(grad_steps)
    sums.total(total)
    resid = resid_ref[...]
    inverse = scale_rows(resid)
    back = cot_ref[...].astype(F32) + norm_back(resid * inverse, inverse, total[...])
    g_resid[...] = back
    low[...] = back.astype(BF)
    tokens = TokenGather(low, all_r, gather)
    acc_ref[...] = jnp.zeros_like(acc_ref)
    next(grad_steps)
    tokens.pass_mate()
    tokens.pass_ring(0)
    tokens.pass_ring(1)
    next(grad_steps)
    tokens.finish()

    downs = TokenScatter(act_ref, wdown_ref, slots[6:12], stage, sems[4:8])
    down_steps = downs.steps()

    def attend(b):
        for c in range(2):
            for core in range(2):
                at = pl.ds((2 * c + core) * HALF, HALF)
                copy = pltpu.make_async_copy(
                    all_r.at[2 * b + c, core], chunk.at[at], ksems[3].at[2 * c + core]
                )
                copy.start()
        for c in range(2):
            for core in range(2):
                at = pl.ds((2 * c + core) * HALF, HALF)
                pltpu.make_async_copy(
                    all_r.at[2 * b + c, core], chunk.at[at], ksems[3].at[2 * c + core]
                ).wait()
        g = abt(wot_ref[...], chunk[...]).astype(BF)
        dq = attend_back_block(
            q_ref, kv_ref, kvt_ref, start_ref, o_ref, lse_ref, g, acc_ref, b
        )
        dq = dq[:HEAD_DIM] * HEAD_DIM ** (-0.5)
        at = pl.ds(b * QB, QB)
        c, s = cos_ref[:, at], sin_ref[:, at]
        turned = jnp.concatenate(
            [turn_back(dq[:, :QB], c, s), turn_back(dq[:, QB:], c, s)], axis=0
        )
        g_qkv[at, :128] = turned.T.astype(BF)

    attend(0)
    next(down_steps)
    next(down_steps)
    attend(1)
    next(down_steps)
    attend(2)
    next(down_steps)
    next(grad_steps)
    attend(3)

    def lower(i, carry):
        at = pl.ds(pl.multiple_of(i * KB, KB), KB)
        key_low[at, :] = acc_ref[at, :].astype(BF)
        return carry

    lax.fori_loop(0, LENGTH // KB, lower, 0)
    key_copies = []
    for i, s in enumerate(TURNS):
        there = pl.ds(pl.multiple_of(lax.rem(x + s, 4) * ROWS, ROWS), ROWS)
        c = remote(
            key_low.at[there],
            key_land.at[i],
            ksems[0].at[i],
            ksems[1].at[i],
            peer(("x",), (s,)),
        )
        c.start()
        key_copies.append(c)
    next(down_steps)
    next(down_steps)
    grads.total(m_sum)
    m_deal = deal_start(m_sum.reshape(MEMBERS, 32, 1536), m_dealt, deals[:3])
    downs.total(total)
    out_low[...] = (resid_ref[...] + total[...]).astype(BF)
    copies = [
        pltpu.make_async_copy(out_low, block_out.at[t], csems[2]),
        remote(out_low, block_out.at[t], csems[0], csems[1], other_core()),
    ]
    for c in copies:
        c.start()
    for c in key_copies:
        c.wait()
    own = pl.ds(pl.multiple_of(x * ROWS, ROWS), ROWS)
    add_rows(key_sum, [acc_ref.at[own]] + [key_land.at[i] for i in range(3)], ROWS, 256)
    for b in range(BLOCKS):
        at = pl.ds(b * QB, QB)
        v = key_sum[at, :].T
        k = turn_back(v[:HEAD_DIM], cos_ref[:, at], sin_ref[:, at])
        g_qkv[at, 128:] = jnp.concatenate([k, v[HEAD_DIM:]], axis=0).T.astype(BF)

    last = TokenScatter(g_qkv, wqkv_ref, slots[12:], stage, sems[8:])
    attn = GradScatter(
        [(all_a, g_qkv), (all_r.reshape(ROWS, D), low_ref)], mids[6:], columns, gsems[3:]
    )
    last_steps, attn_steps = last.steps(), attn.steps()
    next(last_steps)
    next(attn_steps)
    next(last_steps)
    next(last_steps)
    next(attn_steps)
    next(attn_steps)
    next(last_steps)
    next(attn_steps)
    next(last_steps)
    next(attn_steps)
    next(last_steps)
    next(attn_steps)
    next(attn_steps)
    next(attn_steps)
    last.total(total)
    rows = rows_ref[...]
    inverse = scale_rows(rows)
    grad[...] = g_resid[...] + norm_back(rows * inverse, inverse, total[...])
    more = [
        pltpu.make_async_copy(grad, input_grad.at[t], csems[5]),
        remote(grad, input_grad.at[t], csems[3], csems[4], other_core()),
    ]
    for c in more:
        c.start()
    attn.total(a_sum)
    a_deal = deal_start(a_sum.reshape(MEMBERS, 32, 384), a_dealt, deals[3:])
    finish(copies + more + m_deal + a_deal)


def backward_exchange(*args):
    outs = [
        ((2, HALF, D), F32),
        ((2, HALF, D), BF),
        ((MEMBERS, 32, 1536), BF),
        ((MEMBERS, 32, 384), BF),
        ((MEMBERS, 2, HALF, D), BF),
    ]
    wide, low = pltpu.VMEM((HALF, D), F32), pltpu.VMEM((HALF, D), BF)
    scratch = token_scatter_slots() * 3 + grad_scatter_slots(1536) + grad_scatter_slots(384)
    scratch += [STAGE, COLUMNS, wide, wide, wide, low, low]
    scratch += [
        pltpu.VMEM((256, 1536), BF),
        pltpu.VMEM((256, 384), BF),
        pltpu.VMEM((256, D), BF),
        pltpu.VMEM((ROWS, 256), BF),
        pltpu.VMEM((ROWS, 128), F32),
        pltpu.VMEM((LENGTH, 128), F32),
        pltpu.VMEM((LENGTH, 128), BF),
        pltpu.VMEM((3, ROWS, 128), BF),
        pltpu.VMEM((8, 128), F32),
    ]
    scratch += TOKEN_SCATTER_SEMS * 3 + GRAD_SCATTER_SEMS * 2 + TOKEN_GATHER_SEMS
    scratch += [DMA((3,)), DMA((3,)), DMA, DMA((4,))] + [DMA] * 7 + DEAL_SEMS * 2
    input_grad, block_out, m_dealt, a_dealt, _ = call(
        backward_kernel,
        4,
        "backward_exchange",
        args,
        [VMEM] * 18 + [HBM] * 3,
        outs,
        [HBM] * 5,
        scratch,
    )
    return input_grad.reshape(2 * HALF, D), block_out.reshape(2 * HALF, D), m_dealt, a_dealt


def rope_frequency():
    half_size = HEAD_DIM // 2
    base_freq = 500000.0 ** (-(jnp.arange(half_size, dtype=F32) * 2.0 / HEAD_DIM))
    wavelength = 2.0 * math.pi / base_freq
    smooth = (8192.0 / wavelength - 1.0) / 3.0
    blended = (1.0 - smooth) * base_freq / 32.0 + smooth * base_freq
    return jnp.where(
        wavelength < 2048.0, base_freq, jnp.where(wavelength > 8192.0, base_freq / 32.0, blended)
    )


def swap_cores(x):
    return lax.ppermute(x, "t", [(0, 1), (1, 0)])


def rotate(values, cos_tab, sin_tab):
    v = values.reshape(-1, 2, HEAD_DIM // 2, values.shape[1])
    a, b = v[:, 0], v[:, 1]
    return jnp.stack([a * cos_tab - b * sin_tab, b * cos_tab + a * sin_tab], axis=1).reshape(
        values.shape
    )


def adamw(weight, first_moment, second_moment, gradient, step_rate):
    first_new = 0.9 * first_moment + 0.1 * gradient
    second_new = 0.95 * second_moment + 0.05 * gradient * gradient
    corrected = first_new / (1.0 - 0.9**STEP) / (jnp.sqrt(second_new / (1.0 - 0.95**STEP)) + 1e-08)
    return (first_new, second_new, weight - step_rate * (corrected + 0.1 * weight))


def slots(w, columns):
    return w.reshape(w.shape[0], -1, columns).transpose(1, 0, 2)


def unslots(g):
    return g.transpose(1, 0, 2).reshape(g.shape[1], -1)


def body(
    tokens,
    segments,
    cotangent,
    query_weight,
    key_weight,
    value_weight,
    output_weight,
    gate_weight,
    up_weight,
    down_weight,
    norm_gain_pair,
    query_first,
    key_first,
    value_first,
    output_first,
    gate_first,
    up_first,
    down_first,
    gains_first,
    query_second,
    key_second,
    value_second,
    output_second,
    gate_second,
    up_second,
    down_second,
    gains_second,
):
    t = lax.axis_index("t")
    x_place = lax.axis_index("x")

    gains = norm_gain_pair.astype(BF).astype(F32)
    gain_a, gain_m = gains[0][:, None], gains[1][:, None]
    low = lambda w: w.astype(BF).astype(F32)
    fold = lambda g, w: (g * low(w)).astype(BF)
    twice = lambda w: jnp.repeat(slots(w, HEAD_DIM), 2, axis=0)
    qkv_slots = jnp.concatenate(
        [
            slots(fold(gain_a, query_weight), 128),
            twice(fold(gain_a, key_weight)),
            twice(fold(gain_a, value_weight)),
        ],
        axis=2,
    )
    out_slots = slots(output_weight.astype(BF).T, 128)
    gate_up_slots = jnp.concatenate(
        [slots(fold(gain_m, gate_weight), 512), slots(fold(gain_m, up_weight), 512)], axis=2
    )
    down_slots = slots(down_weight.astype(BF).T, 512)

    rows = lax.dynamic_slice_in_dim(tokens[0], t * HALF, HALF, 0).astype(F32)
    unit_a = rows * scale_rows(rows)
    all_a, seg, w_qkv, w_out = first_exchange(
        unit_a.astype(BF), jnp.broadcast_to(segments, (8, 128)), qkv_slots, out_slots
    )
    segment = seg[:, :, 0, :].reshape(LENGTH)
    index = jnp.arange(LENGTH, dtype=jnp.int32)
    previous = jnp.concatenate([jnp.full((1,), -1, jnp.int32), segment[:-1]])
    starts = lax.cummax(jnp.where(segment != previous, index, 0), axis=0)
    first_row = x_place * ROWS
    own_start = lax.dynamic_slice_in_dim(starts, first_row, ROWS, 0)
    own_index = first_row + jnp.arange(ROWS, dtype=jnp.int32)
    angles = rope_frequency()[:, None] * (own_index - own_start).astype(F32)[None, :]
    cos_tab, sin_tab = jnp.cos(angles), jnp.sin(angles)
    qkv = lax.dot_general(
        w_qkv, all_a, (((0,), (1,)), ((), ())), preferred_element_type=F32
    )
    rotated = rotate(qkv[:192], cos_tab, sin_tab).astype(BF)
    kv_own = jnp.concatenate([rotated[128:], qkv[192:].astype(BF)], axis=0).T
    scale = HEAD_DIM ** (-0.5)
    q_low = rotated[:128].reshape(2, HEAD_DIM, ROWS) * jnp.asarray(scale, BF)
    nothing = jnp.zeros_like(q_low)
    q_wide = jnp.concatenate([q_low, nothing], axis=1)
    cot_half = lax.dynamic_slice_in_dim(cotangent[0], t * HALF, HALF, 0)
    resid, all_m, all_g, w_gate_up, w_down, kv, kvt, o_full, lse, o_low = forward_exchange(
        q_wide, own_start[None], w_out, rows, kv_own, cot_half, gate_up_slots, down_slots
    )
    gate_up = jnp.dot(all_m, w_gate_up, preferred_element_type=F32)
    gate, up = gate_up[:, :512], gate_up[:, 512:]
    sig = jax.nn.sigmoid(gate)
    silu = gate * sig
    act = (silu * up).astype(BF)

    g_act = jnp.dot(all_g, w_down, preferred_element_type=F32)
    g_gate = g_act * up * sig * (1.0 + gate * (1.0 - sig))
    g_up = g_act * silu
    g_gate_up = jnp.concatenate([g_gate, g_up], axis=1).astype(BF)
    input_grad, block_out, mlp_dealt, attn_dealt = backward_exchange(
        g_gate_up,
        act,
        w_gate_up,
        w_down,
        resid,
        cot_half,
        w_out.T,
        q_wide,
        kv,
        kvt,
        own_start[None],
        o_full,
        lse,
        o_low,
        cos_tab,
        sin_tab,
        w_qkv,
        rows,
        all_m,
        all_g,
        all_a,
    )
    mlp_sum, attn_sum = mlp_dealt.astype(F32), attn_dealt.astype(F32)

    pairs = lambda g: unslots(g.reshape(4, 2, 32, HEAD_DIM).sum(axis=1))
    q_sum = unslots(attn_sum[:, :, :128])
    k_sum = pairs(attn_sum[:, :, 128:192])
    v_sum = pairs(attn_sum[:, :, 192:256])
    gate_sum = unslots(mlp_sum[:, :, :512])
    up_sum = unslots(mlp_sum[:, :, 512:1024])
    dots = lambda g, w: jnp.sum(g * low(w), axis=1)
    gains_half = jnp.stack(
        [
            dots(q_sum, query_weight) + dots(k_sum, key_weight) + dots(v_sum, value_weight),
            dots(gate_sum, gate_weight) + dots(up_sum, up_weight),
        ],
        axis=0,
    )
    gains_grad = gains_half + swap_cores(gains_half)
    query_grad, key_grad, value_grad = gain_a * q_sum, gain_a * k_sum, gain_a * v_sum
    gate_grad, up_grad = gain_m * gate_sum, gain_m * up_sum
    output_grad = unslots(attn_sum[:, :, 256:]).T
    down_grad = unslots(mlp_sum[:, :, 1024:]).T
    wide_rate = 2.0 * D ** (-0.5)
    outs = [block_out[None], input_grad[None]]
    for weight, first, second, grad, rate in (
        (query_weight, query_first, query_second, query_grad, wide_rate),
        (key_weight, key_first, key_second, key_grad, wide_rate),
        (value_weight, value_first, value_second, value_grad, wide_rate),
        (output_weight, output_first, output_second, output_grad, 2.0 * (4 * HEAD_DIM) ** (-0.5)),
        (gate_weight, gate_first, gate_second, gate_grad, wide_rate),
        (up_weight, up_first, up_second, up_grad, wide_rate),
        (down_weight, down_first, down_second, down_grad, 2.0 * FF ** (-0.5)),
        (norm_gain_pair, gains_first, gains_second, gains_grad, 1.5),
    ):
        outs.append(grad)
        outs.extend(adamw(weight, first, second, grad, rate))
    return tuple(outs)


def solution(mesh):
    split = Mesh(
        mesh.devices.reshape(tuple(SIZES.values())), tuple(SIZES)
    )
    heads = ("x", "z", "yl")
    every = ("dp", "x", "z", "yl")
    acts = P("dp", heads, None)
    rows_cut = P(every, "t")
    columns_cut = P("t", every)
    gains = P(None, every)
    weights = (rows_cut,) * 3 + (columns_cut,) + (rows_cut,) * 2 + (columns_cut, gains)
    in_specs = (acts, P("dp", heads), acts) + weights * 3
    out_specs = (acts, acts) + tuple(spec for spec in weights for _ in range(4))
    return jax.shard_map(
        body, mesh=split, in_specs=in_specs, out_specs=out_specs, check_vma=False
    )
```

```python
import functools
import itertools
import math

import jax
import jax.numpy as jnp
import numpy as np
from jax import lax
from jax.experimental import pallas as pl
from jax.experimental.pallas import tpu as pltpu
from jax.sharding import Mesh
from jax.sharding import PartitionSpec as P

D = 2048
FF = 8192
HEADS = 32
KV_HEADS = 8
HEAD_DIM = 64
STEP = 10
EPS = 1e-05

SIZES = {"dp": 2, "x": 4, "z": 4, "yl": 2, "t": 2}
GROUP = ("z", "yl")
CROSS = ("dp", "x")
MEMBERS = 8
HALF = 64
ROWS = 1024
LENGTH = 4096
DOC_MOST = 2048
DOCS = 10
QB = 256
KB = 512
BLOCKS = ROWS // QB
WIDE = 2 * QB
BF = jnp.bfloat16
F32 = jnp.float32


def shifts(axes):
    return list(itertools.product(*[range(SIZES[a]) for a in axes]))


def place(axes, shift, sign=1):
    index = 0
    for a, s in zip(axes, shift):
        index = index * SIZES[a] + lax.rem(
            lax.axis_index(a) + (s if sign > 0 else SIZES[a] - s), SIZES[a]
        )
    return index


def peer(axes, shift):
    return {
        a: lax.rem(lax.axis_index(a) + s, SIZES[a]) for a, s in zip(axes, shift) if s
    }


def other_core():
    return {"t": 1 - lax.axis_index("t")}


def hail(devices):
    for device in devices:
        pl.semaphore_signal(
            pltpu.get_barrier_semaphore(),
            inc=1,
            device_id=device,
            device_id_type=pl.DeviceIdType.MESH,
        )


def await_all(devices):
    pl.semaphore_wait(pltpu.get_barrier_semaphore(), len(devices))


def greet(devices):
    hail(devices)
    await_all(devices)


def remote(src, dst, send, recv, device):
    return pltpu.make_async_remote_copy(
        src_ref=src,
        dst_ref=dst,
        send_sem=send,
        recv_sem=recv,
        device_id=device,
        device_id_type=pl.DeviceIdType.MESH,
    )


def abt(left, right):
    return lax.dot_general(left, right, (((1,), (1,)), ((), ())), preferred_element_type=F32)


def atb(left, right):
    return lax.dot_general(left, right, (((0,), (0,)), ((), ())), preferred_element_type=F32)


DMA = pltpu.SemaphoreType.DMA
HBM = pl.BlockSpec(memory_space=pl.ANY)
VMEM = pl.BlockSpec(memory_space=pltpu.VMEM)
MOVES = shifts(GROUP)[1:]
TURNS = (1, 3, 2)


def members():
    return [other_core()] + [peer(GROUP, s) for s in MOVES]


def across():
    return [peer(("dp",), (1,))] + [peer(("x",), (s,)) for s in TURNS]


def finish(copies):
    for c in copies:
        c.wait()


INSIDE = ("yl", "z")
ACROSS = ("dp", "x")


def ring_places(axes):
    pair, ring = axes
    p, q = lax.axis_index(pair), lax.axis_index(ring)
    mate, up, down = {pair: 1 - p}, {ring: lax.rem(q + 1, 4)}, {ring: lax.rem(q + 3, 4)}
    return p, q, mate, up, down


RING_GATHER_SEMS = [DMA((9,)), DMA((9,)), DMA]


class RingGather:
    def __init__(self, x_ref, slot, rows, axes, sems, arrived=None):
        self.x_ref, self.slot, self.half, self.axes = x_ref, slot, rows // 2, axes
        self.ssem, self.rsem, self.local = sems
        self.copies = {}
        self.arrived = arrived if arrived is not None else lambda part: None
        p, q, mate, up, down = ring_places(axes)
        self.own = pltpu.make_async_copy(x_ref, slot(p, q), self.local)
        self.own.start()
        for k, to in enumerate((mate, up, down)):
            self.go(k, x_ref, slot(p, q), to)

    def go(self, k, src, dst, to):
        c = remote(src, dst, self.ssem.at[k], self.rsem.at[k], to)
        c.start()
        self.copies[k] = c

    def part(self, p, q, which=None):
        ref = self.slot(p, q)
        return ref if which is None else ref.at[pl.ds(which * self.half, self.half)]

    def wait_own(self):
        if self.own is not None:
            self.own.wait()
            self.own = None

    def pass_mate(self):
        p, q, _, up, down = ring_places(self.axes)
        self.copies[0].wait_recv()
        part = self.part(1 - p, q)
        self.go(3, part, part, up)
        self.go(4, part, part, down)
        self.arrived(part)

    def pass_ring(self, column):
        p, q, _, up, down = ring_places(self.axes)
        p = p if column == 0 else 1 - p
        at = 1 if column == 0 else 3
        for i, (step, to) in enumerate(((3, up), (1, down))):
            self.copies[at + i].wait_recv()
            there = lax.rem(q + step, 4)
            part = self.part(p, there, i)
            self.go(5 + 2 * column + i, part, part, to)
            self.arrived(self.part(p, there))

    def finish(self):
        p, q, _, _, _ = ring_places(self.axes)
        far = lax.rem(q + 2, 4)
        for column, p in enumerate((p, 1 - p)):
            for i in range(2):
                self.copies[5 + 2 * column + i].wait_recv()
            self.arrived(self.part(p, far))
        self.wait_own()
        for c in self.copies.values():
            c.wait_send()


TOKEN_GATHER_SEMS = RING_GATHER_SEMS + [DMA((8,)), DMA((8,))]


class TokenGather(RingGather):
    def __init__(self, x_ref, out_ref, sems):
        t = lax.axis_index("t")
        self.passed, self.had, self.tsend, self.trecv = [], set(), sems[3], sems[4]
        slot = lambda p, q: out_ref.at[2 * q + p, t]
        super().__init__(x_ref, slot, HALF, INSIDE, sems[:3], self.to_core)
        p, q, _, _, _ = ring_places(INSIDE)
        self.to_core(slot(p, q), x_ref)

    def to_core(self, part, src=None):
        k = len(self.passed)
        c = remote(part if src is None else src, part, self.tsend.at[k], self.trecv.at[k], other_core())
        c.start()
        self.passed.append(c)

    def have(self, *ks):
        for k in ks:
            if k not in self.had:
                self.passed[k].wait_recv()
                self.had.add(k)

    def finish(self):
        super().finish()
        self.have(*range(8))
        for c in self.passed:
            c.wait_send()


def add_rows(out_ref, terms, rows, step_rows):
    def step(r, carry):
        at = pl.ds(pl.multiple_of(r * step_rows, step_rows), step_rows)
        total = terms[0][at, :].astype(F32)
        for term in terms[1:]:
            total = total + term[at, :].astype(F32)
        out_ref[at, :] = total.astype(out_ref.dtype)
        return carry

    lax.fori_loop(0, rows // step_rows, step, 0)


RING_SCATTER_SEMS = [DMA((13,)), DMA((13,))]


def ring_scatter_slots(rows, wide):
    half = rows // 2
    return [
        pltpu.VMEM((2, half, wide), BF),
        pltpu.VMEM((2, half, wide), BF),
        pltpu.VMEM((2, rows, wide), BF),
        pltpu.VMEM((2, rows, wide), BF),
        pltpu.VMEM((rows, wide), BF),
    ]


class RingScatter:
    def __init__(self, rows, axes, slots, sems):
        self.rows, self.half, self.axes = rows, rows // 2, axes
        self.far_up, self.far_down, self.from_down, self.from_up, self.back = slots
        self.ssem, self.rsem = sems
        self.copies = {}

    def go(self, k, src, dst, to):
        c = remote(src, dst, self.ssem.at[k], self.rsem.at[k], to)
        c.start()
        self.copies[k] = c

    def part(self, p, q, at):
        return self.held(p, q).at[at]

    def halves(self):
        return pl.ds(0, self.half), pl.ds(self.half, self.half)

    def add(self, out_ref, terms, rows):
        add_rows(out_ref, terms, rows, 16)

    def send_far(self, p):
        _, _, _, up, down = ring_places(self.axes)
        first, second = self.halves()
        self.go(2 * p, self.part(p, 2, first), self.far_up.at[p], up)
        self.go(2 * p + 1, self.part(p, 2, second), self.far_down.at[p], down)

    def send_near(self, p):
        _, _, _, up, down = ring_places(self.axes)
        first, second = self.halves()
        self.go(4 + 2 * p, self.part(p, 1, second), self.from_down.at[p, second], up)
        self.go(5 + 2 * p, self.part(p, 3, first), self.from_up.at[p, first], down)

    def send_joined(self, p):
        _, _, _, up, down = ring_places(self.axes)
        first, second = self.halves()
        self.copies[2 * p].wait_recv()
        part = self.part(p, 1, first)
        self.add(part, [part, self.far_up.at[p]], self.half)
        self.go(8 + 2 * p, part, self.from_down.at[p, first], up)
        self.copies[2 * p + 1].wait_recv()
        part = self.part(p, 3, second)
        self.add(part, [part, self.far_down.at[p]], self.half)
        self.go(9 + 2 * p, part, self.from_up.at[p, second], down)

    def arrivals(self, p):
        for k in (4 + 2 * p, 5 + 2 * p, 8 + 2 * p, 9 + 2 * p):
            self.copies[k].wait_recv()

    def send_mate(self):
        _, _, mate, _, _ = ring_places(self.axes)
        self.arrivals(1)
        part = self.held(1, 0)
        self.add(part, [part, self.from_down.at[1], self.from_up.at[1]], self.rows)
        self.go(12, part, self.back, mate)

    def total(self, out_ref):
        self.arrivals(0)
        self.copies[12].wait_recv()
        self.add(
            out_ref,
            [self.held(0, 0), self.from_down.at[0], self.from_up.at[0], self.back],
            self.rows,
        )
        for c in self.copies.values():
            c.wait_send()


TOKEN_SCATTER_SEMS = RING_SCATTER_SEMS + [DMA((4, 2)), DMA((4, 2))]


def token_scatter_slots():
    return ring_scatter_slots(HALF, D) + [pltpu.VMEM((4, 2, HALF, D), BF)]


STAGE = pltpu.VMEM((4, 2, 2, HALF, D), BF)


class TokenScatter(RingScatter):
    def __init__(self, a_ref, w_ref, slots, stage, sems):
        super().__init__(HALF, INSIDE, slots[:5], sems[:2])
        self.a_ref, self.w_ref = a_ref, w_ref
        self.stage, self.theirs = stage, slots[5]
        self.tsend, self.trecv = sems[2:]
        self.swaps = {}

    def pair_place(self, p):
        own = lax.axis_index("yl")
        return own if p == 0 else 1 - own

    def held(self, p, q):
        return self.stage.at[q, self.pair_place(p), lax.axis_index("t")]

    def make(self, q):
        row = lax.rem(lax.axis_index("z") + q, 4) * 256
        a = self.a_ref[pl.ds(pl.multiple_of(row, 256), 256), :]

        def step(n, carry):
            at = pl.ds(pl.multiple_of(n * 512, 512), 512)
            product = abt(a, self.w_ref[at, :]).astype(BF)
            self.stage[q, :, :, :, at] = product.reshape(2, 2, HALF, 512)
            return carry

        lax.fori_loop(0, D // 512, step, 0)

    def swap(self, q):
        t = lax.axis_index("t")
        for p in (1, 0):
            at = self.pair_place(p)
            c = remote(
                self.stage.at[q, at, 1 - t],
                self.theirs.at[q, at],
                self.tsend.at[q, p],
                self.trecv.at[q, p],
                other_core(),
            )
            c.start()
            self.swaps[q, p] = c

    def pair(self, p, q):
        self.swaps[q, p].wait_recv()
        part = self.held(p, q)
        self.add(part, [part, self.theirs.at[q, self.pair_place(p)]], HALF)

    def total(self, out_ref):
        super().total(out_ref)
        for c in self.swaps.values():
            c.wait_send()

    def pair_ring(self, q):
        self.pair(1, q)
        self.pair(0, q)

    def fill(self, *qs):
        for q in qs:
            self.make(q)
            self.swap(q)


BY_NEED = [(1, 2), (0, 2), (1, 1), (1, 3), (0, 1), (0, 3), (1, 0), (0, 0)]


def grad_scatter_slots(wide):
    return ring_scatter_slots(256, wide) + [pltpu.VMEM((2, 4, 256, wide), BF)]


COLUMNS = pltpu.VMEM((2, 2, ROWS, 256), BF)


class GradScatter(RingScatter):
    def __init__(self, pairs, slots, columns, sems):
        super().__init__(256, ACROSS, slots[:5], sems[:2])
        self.pairs, self.blocks, self.columns, self.lsem = pairs, slots[5], columns, sems[2]
        self.loads = {}
        self.done = 0
        self.load(0)
        self.load(1)

    def held(self, p, q):
        return self.blocks.at[p, q]

    def load(self, k):
        p, q = BY_NEED[k]
        dp, x = lax.axis_index("dp"), lax.axis_index("x")
        row = (dp if p == 0 else 1 - dp) * 4 + lax.rem(x + q, 4)
        at = pl.ds(pl.multiple_of(row * 256, 256), 256)
        for i, (x_ref, _) in enumerate(self.pairs):
            c = pltpu.make_async_copy(
                x_ref.at[:, at], self.columns.at[k % 2, i], self.lsem.at[k % 2, i]
            )
            c.start()
            self.loads[k, i] = c

    def make(self):
        k = self.done
        p, q = BY_NEED[k]
        start = 0
        for i, (_, g_ref) in enumerate(self.pairs):
            self.loads[k, i].wait()
            wide = g_ref.shape[1]
            self.blocks[p, q, :, start : start + wide] = atb(
                self.columns[k % 2, i], g_ref[...]
            ).astype(BF)
            start += wide
        self.done = k + 1
        if k + 2 < len(BY_NEED):
            self.load(k + 2)

def both(method):
    method(1)
    method(0)


def scatter_both(sums, grads, devices=None):
    sums.make(2)
    if devices is not None:
        await_all(devices)
    sums.swap(2)
    grads.make()
    grads.send_far(1)
    sums.pair(1, 2)
    sums.send_far(1)
    sums.pair(0, 2)
    sums.send_far(0)
    sums.fill(1, 3)
    sums.pair(1, 1)
    sums.pair(1, 3)
    sums.send_near(1)
    sums.send_joined(1)
    grads.make()
    grads.send_far(0)
    sums.pair(0, 1)
    sums.pair(0, 3)
    sums.send_near(0)
    sums.fill(0)
    sums.send_joined(0)
    grads.make()
    grads.make()
    grads.send_near(1)
    sums.pair_ring(0)
    sums.send_mate()
    grads.send_joined(1)
    grads.make()
    grads.make()
    grads.send_near(0)
    grads.make()
    grads.make()


GRAD_SCATTER_SEMS = RING_SCATTER_SEMS + [DMA((2, 2))]


def weight_gather(x_ref, out_ref, sems):
    return RingGather(x_ref, lambda p, q: out_ref.at[p, q], 256, ACROSS, sems)


DEAL_SEMS = [DMA((7,)), DMA((7,)), DMA]


def deal_start(x_ref, out_ref, sems):
    send, recv, local = sems
    me = place(GROUP, (0, 0))
    own = pltpu.make_async_copy(x_ref.at[me], out_ref.at[me], local)
    own.start()
    copies = []
    for i, s in enumerate(MOVES):
        c = remote(
            x_ref.at[place(GROUP, s)], out_ref.at[me], send.at[i], recv.at[i], peer(GROUP, s)
        )
        c.start()
        copies.append(c)
    return [own] + copies


def deal_columns(x_ref, out_ref, at, wide, sems):
    send, recv, local = sems
    me = place(GROUP, (0, 0))
    slot = lambda c: x_ref.at[:, pl.ds(pl.multiple_of(c * wide, wide), wide)]
    there = out_ref.at[me, :, pl.ds(at, wide)]
    own = pltpu.make_async_copy(slot(me), there, local)
    own.start()
    copies = []
    for i, s in enumerate(MOVES):
        c = remote(slot(place(GROUP, s)), there, send.at[i], recv.at[i], peer(GROUP, s))
        c.start()
        copies.append(c)
    return [own] + copies


def own_half(ref):
    return pl.ds(pl.multiple_of(lax.axis_index("t") * HALF, HALF), HALF)


def fold(gain, weight):
    return (gain * weight.astype(BF).astype(F32)).astype(BF)


def split(refs, *counts):
    parts, at = [], 0
    for count in counts:
        parts.append(refs[at : at + count])
        at += count
    assert at == len(refs)
    return parts


def scale_rows(x):
    return lax.rsqrt(jnp.mean(x * x, axis=1, keepdims=True) + EPS)


def norm_back(unit, inverse, grad):
    return inverse * (grad - unit * jnp.mean(grad * unit, axis=1, keepdims=True))


def call(kernel, collective_id, name, args, in_specs, outs, out_specs, scratch):
    sent = 60_000_000
    return pl.pallas_call(
        kernel,
        out_shape=[jax.ShapeDtypeStruct(s, d) for s, d in outs],
        in_specs=in_specs,
        out_specs=out_specs,
        scratch_shapes=scratch,
        compiler_params=pltpu.CompilerParams(
            collective_id=collective_id, has_side_effects=True, vmem_limit_bytes=60 * 2**20
        ),
        cost_estimate=pl.CostEstimate(flops=0, bytes_accessed=sent, transcendentals=0),
        name=name,
    )(*args)


def turn_back(v, cos_tab, sin_tab):
    a, b = v[: HEAD_DIM // 2], v[HEAD_DIM // 2 :]
    return jnp.concatenate([a * cos_tab + b * sin_tab, b * cos_tab - a * sin_tab], axis=0)


def key_blocks(b, rel):
    x = lax.axis_index("x")
    first = x * ROWS + b * QB
    chunk = (x - rel) * (ROWS // KB)
    low = lax.max(lax.max(first - (DOC_MOST - 1), 0) // KB, chunk)
    high = lax.min((first + QB + KB - 1) // KB, chunk + ROWS // KB)
    return low, high


def mask_scores(s, base, start, b, rel):
    key = base + lax.broadcasted_iota(jnp.int32, s.shape, 0)
    allowed = key >= start
    if rel == 0:
        first = lax.axis_index("x") * ROWS + b * QB
        own = first + lax.broadcasted_iota(jnp.int32, (1, QB), 1)
        allowed = allowed & (key <= jnp.concatenate([own, own], axis=1))
    return jnp.where(allowed, s, -1e30)


def block_lanes(b):
    return pl.ds(pl.multiple_of(b * QB, QB), QB)


def beside_lanes(ref, b):
    at = block_lanes(b)
    return jnp.concatenate([ref[0, :, at], ref[1, :, at]], axis=1)


def twice_lanes(ref, b):
    v = ref[:, block_lanes(b)]
    return jnp.concatenate([v, v], axis=1)


def attend_part(q_ref, kv_ref, kvt_ref, start_ref, top_ref, total_ref, acc_ref, b, rel):
    q, start = beside_lanes(q_ref, b), twice_lanes(start_ref, b)

    def step(j, carry):
        top, total, acc = carry
        base = pl.multiple_of(j * KB, KB)
        s = jnp.dot(kv_ref[pl.ds(base, KB), :], q, preferred_element_type=F32)
        s = mask_scores(s, base, start, b, rel)
        new_top = jnp.maximum(top, jnp.max(s, axis=0, keepdims=True))
        p = jnp.exp(s - new_top)
        fade = jnp.exp(top - new_top)
        total = total * fade + jnp.sum(p, axis=0, keepdims=True)
        acc = acc * fade + jnp.dot(
            kvt_ref[:, pl.ds(base, KB)], p.astype(BF), preferred_element_type=F32
        )
        return (new_top, total, acc)

    if rel == 0:
        init = (
            jnp.full((1, WIDE), -1e30, F32),
            jnp.zeros((1, WIDE), F32),
            jnp.zeros((2 * HEAD_DIM, WIDE), F32),
        )
    else:
        init = (top_ref[b], total_ref[b], acc_ref[b])
    low, high = key_blocks(b, rel)
    top_ref[b], total_ref[b], acc_ref[b] = lax.fori_loop(low, high, step, init)


def attend_end(top_ref, total_ref, acc_ref, o_ref, lse_ref, low_ref, b):
    at = block_lanes(b)
    total = total_ref[b]
    o = acc_ref[b][HEAD_DIM:] / total
    lse = top_ref[b] + jnp.log(total)
    for h in range(2):
        o_ref[h, :, at] = o[:, h * QB : (h + 1) * QB]
        lse_ref[h : h + 1, at] = lse[:, h * QB : (h + 1) * QB]
    beside = jnp.concatenate([o[:, :QB], o[:, QB:]], axis=0)
    low_ref[at, :] = beside.T.astype(BF)


def load_block(all_ref, chunk, sems, b):
    pieces = []
    for c in range(2):
        for core in range(2):
            at = pl.ds((2 * c + core) * HALF, HALF)
            copy = pltpu.make_async_copy(
                all_ref.at[2 * b + c, core], chunk.at[at], sems.at[2 * c + core]
            )
            copy.start()
            pieces.append(copy)
    finish(pieces)


def document_starts(seg_ref):
    every = seg_ref[...].reshape(LENGTH * 8 // 128, 128)
    x = lax.axis_index("x")
    own = jnp.concatenate([seg_ref[x, g, 0:1, :] for g in range(MEMBERS)], axis=1)
    starts = jnp.zeros((1, ROWS), F32)
    for d in range(DOCS - 1):
        same = jnp.where(every == d, 1.0, 0.0)
        count = jnp.sum(jnp.sum(same, axis=0, keepdims=True), axis=1, keepdims=True) * 0.125
        starts = starts + jnp.where(own > d, count, 0.0)
    return starts.astype(jnp.int32)


def forward_kernel(*refs):
    ins, outs, slots, others, sems, gather, rings, keys, deals, seg_sems, lsems = split(
        refs, 12, 17, 6, 22, 4, 15, 12, 3, 15, 5, 2
    )
    (
        tokens_ref, seg_ref, gains_ref, freq_ref, wq_ref, wk_ref, wv_ref, wo_ref, cot_ref,
        gate_ref, up_ref, down_ref,
    ) = ins
    (
        resid_ref, all_m, all_g, w_gu, w_down, kv_ref, kvt_ref, o_ref, lse_ref, low_ref,
        all_a, w_qkv, w_out, w_out_turned, q_ref, tables, start_ref,
    ) = outs
    (
        stage, total, unit, gu_part, down_part, *states, qkv_part, wo_part, seg_all, w_turned,
        chunk, qkv_slots, wo_slots, seg_own, raw, gate_low, up_low, down_low, unit_a, _,
    ) = others
    cos_ref, sin_ref = tables.at[0], tables.at[1]
    ksend, krecv, klocal = keys
    ssend, srecv, xsend, xrecv, slocal = seg_sems
    devices = members() + across()
    hail(devices)
    fetches = []
    for i, ref in enumerate((gate_ref, up_ref, down_ref)):
        c = pltpu.make_async_copy(ref, raw.at[i], lsems[1].at[i])
        c.start()
        fetches.append(c)
    x, z = lax.axis_index("x"), lax.axis_index("z")
    me = place(GROUP, (0, 0))
    gain_a, gain_m = gains_ref[0][:, 0:1], gains_ref[1][:, 0:1]
    wq, wk, wv = (fold(gain_a, ref[...]) for ref in (wq_ref, wk_ref, wv_ref))
    wo = wo_ref[...].astype(BF)
    for c in range(MEMBERS):
        head = slice(c // 2 * HEAD_DIM, (c // 2 + 1) * HEAD_DIM)
        qkv_slots[c] = jnp.concatenate(
            [wq[:, c * 128 : (c + 1) * 128], wk[:, head], wv[:, head]], axis=1
        )
        wo_slots[c] = wo[:, c * 128 : (c + 1) * 128]
    rows = tokens_ref[own_half(tokens_ref), :].astype(F32)
    unit_a[...] = (rows * scale_rows(rows)).astype(BF)
    seg_own[...] = jnp.broadcast_to(seg_ref[...], (8, 128))
    await_all(devices)

    early = deal_start(qkv_slots, qkv_part, deals[9:12]) + deal_start(wo_slots, wo_part, deals[12:])
    tokens = TokenGather(unit_a, all_a, gather[10:])
    seg_copies = [pltpu.make_async_copy(seg_own, seg_all.at[x, me], slocal)]
    seg_copies[0].start()
    for i, s in enumerate(MOVES):
        c = remote(seg_own, seg_all.at[x, me], ssend.at[i], srecv.at[i], peer(GROUP, s))
        c.start()
        seg_copies.append(c)
    finish(early)
    attn_weights = [
        weight_gather(qkv_part.reshape(256, 256), w_qkv, rings[6:9]),
        weight_gather(wo_part.reshape(256, 128), w_out, rings[9:]),
    ]
    finish(seg_copies)
    crossed = []
    for i, to in enumerate(across()[1:]):
        c = remote(seg_all.at[x], seg_all.at[x], xsend.at[i], xrecv.at[i], to)
        c.start()
        crossed.append(c)
    everything = [tokens] + attn_weights
    for g in everything:
        g.pass_mate()
    for g in everything:
        g.pass_ring(0)
    finish(crossed)
    starts = document_starts(seg_all)
    start_ref[...] = starts
    own = x * ROWS + lax.broadcasted_iota(jnp.int32, (1, ROWS), 1)
    angles = freq_ref[:, 0:1] * (own - starts).astype(F32)
    cos_ref[...] = jnp.cos(angles)
    sin_ref[...] = jnp.sin(angles)
    for c in fetches:
        c.wait()
    gate_low[...] = fold(gain_m, raw[0])
    up_low[...] = fold(gain_m, raw[1])
    down_low[...] = raw[2].astype(BF)
    for g in everything:
        g.pass_ring(1)
    for g in attn_weights:
        g.finish()
    for r in range(8):
        at = slice(r * 256, (r + 1) * 256)
        w_turned[:, at] = w_qkv[r // 4, r % 4].T
        w_out_turned[:, at] = w_out[r // 4, r % 4].T

    def project(b):
        load_block(all_a, chunk, lsems[0], b)
        qkv = abt(w_turned[...], chunk[...])
        at = block_lanes(b)
        c, s = cos_ref[:, at], -sin_ref[:, at]
        zeros = jnp.zeros((HEAD_DIM, QB), BF)
        for h in range(2):
            q = turn_back(qkv[h * HEAD_DIM : (h + 1) * HEAD_DIM], c, s)
            q_ref[h, :, at] = jnp.concatenate([(q * HEAD_DIM ** (-0.5)).astype(BF), zeros], axis=0)
        k = turn_back(qkv[128:192], c, s)
        kv = jnp.concatenate([k, qkv[192:]], axis=0)
        here = pl.ds(pl.multiple_of(x * ROWS + b * QB, QB), QB)
        kvt_ref[:, here] = kv.astype(BF)
        kv_ref[here, :] = kv.T.astype(BF)

    tokens.wait_own()
    tokens.have(0, 1)
    project(z)
    tokens.have(2, 4)
    project(lax.rem(z + 3, 4))
    tokens.have(3, 5)
    project(lax.rem(z + 1, 4))
    tokens.finish()
    dealt = deal_columns(gate_low, gu_part, 0, 512, deals[:3])
    dealt += deal_columns(up_low, gu_part, 512, 512, deals[3:6])
    dealt += deal_columns(down_low, down_part, 0, 512, deals[6:9])
    project(lax.rem(z + 2, 4))

    own_keys = kv_ref.at[pl.ds(pl.multiple_of(x * ROWS, ROWS), ROWS)]
    key_copies = []
    for i in range(2):
        c = remote(own_keys, own_keys, ksend.at[i], krecv.at[i], peer(("x",), (i + 1,)))
        c.start()
        key_copies.append(c)
    cots = TokenGather(cot_ref.at[own_half(cot_ref)], all_g, gather[:5])

    def turn(rel):
        base = lax.rem(x + 4 - rel, 4) * ROWS
        for c in range(ROWS // KB):
            at = pl.ds(pl.multiple_of(base + c * KB, KB), KB)
            kvt_ref[:, at] = kv_ref[at, :].T

    def part(b, rel):
        attend_part(q_ref, kv_ref, kvt_ref, start_ref, *states, b, rel)

    for b in range(BLOCKS):
        part(b, 0)
    key_copies[0].wait_recv()
    turn(1)
    for b in range(BLOCKS):
        part(b, 1)
    finish(dealt)
    cots.pass_mate()
    key_copies[1].wait_recv()
    for c in key_copies:
        c.wait_send()
    weights = [
        weight_gather(gu_part.reshape(256, 1024), w_gu, rings[:3]),
        weight_gather(down_part.reshape(256, 512), w_down, rings[3:6]),
    ]
    turn(2)
    sums = TokenScatter(low_ref, w_out.reshape(D, 128), slots, stage, sems)

    def attend(q):
        b = lax.rem(z + q, 4)
        part(b, 2)
        attend_end(*states, o_ref, lse_ref, low_ref, b)
        sums.make(q)
        sums.swap(q)

    attend(2)
    attend(1)
    sums.pair(1, 2)
    sums.send_far(1)
    sums.pair(0, 2)
    sums.send_far(0)
    attend(3)
    for p in (1, 0):
        sums.pair(p, 1)
        sums.pair(p, 3)
        sums.send_near(p)
        sums.send_joined(p)
    attend(0)
    sums.pair_ring(0)
    sums.send_mate()
    cots.pass_ring(0)
    for g in weights:
        g.pass_mate()
    cots.pass_ring(1)
    for g in weights:
        g.pass_ring(0)
    sums.total(total)
    resid = tokens_ref[own_half(tokens_ref), :].astype(F32) + total[...]
    resid_ref[...] = resid
    unit[...] = (resid * scale_rows(resid)).astype(BF)
    tokens = TokenGather(unit, all_m, gather[5:10])
    tokens.pass_mate()
    for g in weights:
        g.pass_ring(1)
    tokens.pass_ring(0)
    tokens.pass_ring(1)
    for g in [cots, tokens] + weights:
        g.finish()


def forward_exchange(*args):
    slots = (MEMBERS, 2, HALF, D)
    outs = [
        ((HALF, D), F32),
        (slots, BF),
        (slots, BF),
        ((2, 4, 256, 1024), BF),
        ((2, 4, 256, 512), BF),
        ((LENGTH, 128), BF),
        ((128, LENGTH), BF),
        ((2, HEAD_DIM, ROWS), F32),
        ((2, ROWS), F32),
        ((ROWS, 128), BF),
        (slots, BF),
        ((2, 4, 256, 256), BF),
        ((2, 4, 256, 128), BF),
        ((128, D), BF),
        ((2, 128, ROWS), BF),
        ((2, HEAD_DIM // 2, ROWS), F32),
        ((1, ROWS), jnp.int32),
    ]
    scratch = token_scatter_slots() + [
        STAGE,
        pltpu.VMEM((HALF, D), F32),
        pltpu.VMEM((HALF, D), BF),
        pltpu.VMEM((MEMBERS, 32, 1024), BF),
        pltpu.VMEM((MEMBERS, 32, 512), BF),
        pltpu.VMEM((BLOCKS, 1, WIDE), F32),
        pltpu.VMEM((BLOCKS, 1, WIDE), F32),
        pltpu.VMEM((BLOCKS, 2 * HEAD_DIM, WIDE), F32),
        pltpu.VMEM((MEMBERS, 32, 256), BF),
        pltpu.VMEM((MEMBERS, 32, 128), BF),
        pltpu.VMEM((4, MEMBERS, 8, 128), jnp.int32),
        pltpu.VMEM((256, D), BF),
        pltpu.VMEM((256, D), BF),
        pltpu.VMEM((MEMBERS, 32, 256), BF),
        pltpu.VMEM((MEMBERS, 32, 128), BF),
        pltpu.VMEM((8, 128), jnp.int32),
        pltpu.VMEM((3, 32, 4096), F32),
        pltpu.VMEM((32, 4096), BF),
        pltpu.VMEM((32, 4096), BF),
        pltpu.VMEM((32, 4096), BF),
        pltpu.VMEM((HALF, D), BF),
        pltpu.VMEM((8, 128), F32),
    ]
    scratch += TOKEN_SCATTER_SEMS + TOKEN_GATHER_SEMS * 3 + RING_GATHER_SEMS * 4
    scratch += [DMA((2,)), DMA((2,)), DMA] + DEAL_SEMS * 5
    scratch += [DMA((7,)), DMA((7,)), DMA((3,)), DMA((3,)), DMA, DMA((4,)), DMA((3,))]
    (
        resid, all_m, all_g, w_gu, w_down, kv, kvt, o, lse, o_low, all_a, w_qkv, _, w_out, q,
        tables, starts,
    ) = call(
        forward_kernel,
        1,
        "forward_exchange",
        args,
        [VMEM] * 8 + [HBM] * 4,
        outs,
        [VMEM] + [HBM] * 4 + [VMEM] * 5 + [HBM] + [VMEM] * 6,
        scratch,
    )
    return (
        resid,
        all_m.reshape(ROWS, D),
        all_g.reshape(ROWS, D),
        w_gu.reshape(D, 1024),
        w_down.reshape(D, 512),
        kv,
        kvt,
        o,
        lse,
        o_low,
        all_a.reshape(ROWS, D),
        w_qkv.reshape(D, 256),
        w_out,
        q,
        tables,
        starts,
    )


def attend_back_part(q_ref, kv_ref, kvt_ref, start_ref, lse_ref, g_ref, dot_ref, dq_ref, acc_ref, b, rel):
    q, start, g, row_dot = beside_lanes(q_ref, b), twice_lanes(start_ref, b), g_ref[b], dot_ref[b]
    at = block_lanes(b)
    lse = jnp.concatenate([lse_ref[0:1, at], lse_ref[1:2, at]], axis=1)

    def step(j, dq):
        base = pl.multiple_of(j * KB, KB)
        kv = kv_ref[pl.ds(base, KB), :]
        s = jnp.dot(kv, q, preferred_element_type=F32)
        p = jnp.exp(mask_scores(s, base, start, b, rel) - lse)
        g_p = jnp.dot(kv, g, preferred_element_type=F32)
        g_s = (p * (g_p - row_dot)).astype(BF)
        acc_ref[pl.ds(base, KB), :] += abt(g_s, q) + abt(p.astype(BF), g)
        return dq + jnp.dot(kvt_ref[:, pl.ds(base, KB)], g_s, preferred_element_type=F32)

    low, high = key_blocks(b, rel)
    dq = jnp.zeros((2 * HEAD_DIM, WIDE), F32) if rel == 2 else dq_ref[b]
    dq_ref[b] = lax.fori_loop(low, high, step, dq)


def backward_kernel(*refs):
    ins, outs, slots, mids, others, keys, sems, gsems, gather, ksems, csems, deals = split(
        refs, 20, 5, 18, 12, 12, 6, 12, 6, 5, 4, 7, 6
    )
    (
        g_ref, act_ref, wgu_ref, wdown_ref, resid_ref, cot_ref, wot_ref, q_ref, kv_ref, kvt_ref,
        start_ref, o_ref, lse_ref, low_ref, tables, wqkv_ref, tokens_ref,
        all_m, all_g, all_a,
    ) = ins
    cos_ref, sin_ref = tables.at[0], tables.at[1]
    input_grad, block_out, m_dealt, a_dealt, all_r = outs
    stage, columns, total, grad, g_resid, low, out_low, m_sum, a_sum, chunk, g_qkv, key_sum = others
    acc_ref, key_low, key_land, gw_ref, dot_ref, dq_ref = keys
    devices = members() + across()
    hail(devices)
    t, x = lax.axis_index("t"), lax.axis_index("x")
    sums = TokenScatter(g_ref, wgu_ref, slots[:6], stage, sems[:4])
    grads = GradScatter([(all_m, g_ref), (all_g, act_ref)], mids[:6], columns, gsems[:3])
    scatter_both(sums, grads, devices)
    grads.send_joined(0)
    sums.total(total)
    resid = resid_ref[...]
    inverse = scale_rows(resid)
    back = cot_ref[own_half(cot_ref), :].astype(F32) + norm_back(resid * inverse, inverse, total[...])
    g_resid[...] = back
    low[...] = back.astype(BF)
    tokens = TokenGather(low, all_r, gather)

    downs = TokenScatter(act_ref, wdown_ref, slots[6:12], stage, sems[4:8])

    def lead(b):
        load_block(all_r, chunk, ksems[3], b)
        g = abt(wot_ref[...], chunk[...]).astype(BF)
        beside = jnp.concatenate([g[:HEAD_DIM], g[HEAD_DIM:]], axis=1)
        o = beside_lanes(o_ref, b)
        dot_ref[b] = jnp.sum(o * beside.astype(F32), axis=0, keepdims=True)
        gw_ref[b] = jnp.concatenate([jnp.zeros_like(beside), beside], axis=0)

    def part(b, rel):
        attend_back_part(
            q_ref, kv_ref, kvt_ref, start_ref, lse_ref, gw_ref, dot_ref, dq_ref, acc_ref, b, rel
        )

    def end(b):
        dq = dq_ref[b][:HEAD_DIM] * HEAD_DIM ** (-0.5)
        at = block_lanes(b)
        c, s = cos_ref[:, at], sin_ref[:, at]
        turned = jnp.concatenate(
            [turn_back(dq[:, :QB], c, s), turn_back(dq[:, QB:], c, s)], axis=0
        )
        g_qkv[at, :128] = turned.T.astype(BF)

    key_copies = []

    def send_keys(rel):
        i = rel - 1
        s = 4 - rel
        there = pl.multiple_of(lax.rem(x + s, 4) * ROWS, ROWS)
        add_rows(key_low.at[i], [acc_ref.at[pl.ds(there, ROWS)]], ROWS, 256)
        c = remote(
            key_low.at[i], key_land.at[i], ksems[0].at[i], ksems[1].at[i], peer(("x",), (s,))
        )
        c.start()
        key_copies.append(c)

    z = lax.axis_index("z")
    acc_ref[...] = jnp.zeros_like(acc_ref)
    downs.fill(2, 1)
    tokens.pass_mate()
    tokens.pass_ring(0)
    tokens.wait_own()
    tokens.have(0, 1)
    lead(z)
    downs.fill(3, 0)
    for q in (2, 1, 3):
        downs.pair_ring(q)
    tokens.pass_ring(1)
    grads.send_mate()
    tokens.have(2, 4)
    lead(lax.rem(z + 3, 4))
    tokens.have(3, 5)
    lead(lax.rem(z + 1, 4))
    tokens.finish()
    both(downs.send_far)
    both(downs.send_near)
    lead(lax.rem(z + 2, 4))
    for b in range(BLOCKS):
        part(b, 2)
    send_keys(2)
    both(downs.send_joined)
    downs.pair_ring(0)
    for b in range(BLOCKS):
        part(b, 1)
    send_keys(1)
    downs.send_mate()
    grads.total(m_sum)
    m_deal = deal_start(m_sum.reshape(MEMBERS, 32, 1536), m_dealt, deals[:3])
    for b in range(BLOCKS):
        part(b, 0)
        end(b)
    downs.total(total)
    out_low[...] = (resid_ref[...] + total[...]).astype(BF)
    copies = [
        pltpu.make_async_copy(out_low, block_out.at[t], csems[2]),
        remote(out_low, block_out.at[t], csems[0], csems[1], other_core()),
    ]
    for c in copies:
        c.start()
    for c in key_copies:
        c.wait()
    own = pl.ds(pl.multiple_of(x * ROWS, ROWS), ROWS)
    add_rows(key_sum, [acc_ref.at[own]] + [key_land.at[i] for i in range(2)], ROWS, 256)
    for b in range(BLOCKS):
        at = pl.ds(b * QB, QB)
        v = key_sum[at, :].T
        k = turn_back(v[:HEAD_DIM], cos_ref[:, at], sin_ref[:, at])
        g_qkv[at, 128:] = jnp.concatenate([k, v[HEAD_DIM:]], axis=0).T.astype(BF)

    last = TokenScatter(g_qkv, wqkv_ref, slots[12:], stage, sems[8:])
    attn = GradScatter(
        [(all_a, g_qkv), (all_r.reshape(ROWS, D), low_ref)], mids[6:], columns, gsems[3:]
    )
    scatter_both(last, attn)
    attn.send_mate()
    attn.send_joined(0)
    attn.total(a_sum)
    a_deal = deal_start(a_sum.reshape(MEMBERS, 32, 384), a_dealt, deals[3:])
    last.total(total)
    rows = tokens_ref[own_half(tokens_ref), :].astype(F32)
    inverse = scale_rows(rows)
    grad[...] = g_resid[...] + norm_back(rows * inverse, inverse, total[...])
    more = [
        pltpu.make_async_copy(grad, input_grad.at[t], csems[5]),
        remote(grad, input_grad.at[t], csems[3], csems[4], other_core()),
    ]
    for c in more:
        c.start()
    finish(copies + more + m_deal + a_deal)


def backward_exchange(*args):
    outs = [
        ((2, HALF, D), F32),
        ((2, HALF, D), BF),
        ((MEMBERS, 32, 1536), BF),
        ((MEMBERS, 32, 384), BF),
        ((MEMBERS, 2, HALF, D), BF),
    ]
    wide, low = pltpu.VMEM((HALF, D), F32), pltpu.VMEM((HALF, D), BF)
    scratch = token_scatter_slots() * 3 + grad_scatter_slots(1536) + grad_scatter_slots(384)
    scratch += [STAGE, COLUMNS, wide, wide, wide, low, low]
    scratch += [
        pltpu.VMEM((256, 1536), BF),
        pltpu.VMEM((256, 384), BF),
        pltpu.VMEM((256, D), BF),
        pltpu.VMEM((ROWS, 256), BF),
        pltpu.VMEM((ROWS, 128), F32),
        pltpu.VMEM((LENGTH, 128), F32),
        pltpu.VMEM((2, ROWS, 128), BF),
        pltpu.VMEM((2, ROWS, 128), BF),
        pltpu.VMEM((BLOCKS, 2 * HEAD_DIM, WIDE), BF),
        pltpu.VMEM((BLOCKS, 1, WIDE), F32),
        pltpu.VMEM((BLOCKS, 2 * HEAD_DIM, WIDE), F32),
    ]
    scratch += TOKEN_SCATTER_SEMS * 3 + GRAD_SCATTER_SEMS * 2 + TOKEN_GATHER_SEMS
    scratch += [DMA((2,)), DMA((2,)), DMA, DMA((4,))] + [DMA] * 7 + DEAL_SEMS * 2
    input_grad, block_out, m_dealt, a_dealt, _ = call(
        backward_kernel,
        4,
        "backward_exchange",
        args,
        [VMEM] * 17 + [HBM] * 3,
        outs,
        [HBM] * 5,
        scratch,
    )
    return input_grad.reshape(2 * HALF, D), block_out.reshape(2 * HALF, D), m_dealt, a_dealt


def rope_frequency():
    base_freq = 500000.0 ** (-(np.arange(HEAD_DIM // 2) * 2.0 / HEAD_DIM))
    wavelength = 2.0 * math.pi / base_freq
    smooth = (8192.0 / wavelength - 1.0) / 3.0
    blended = (1.0 - smooth) * base_freq / 32.0 + smooth * base_freq
    frequency = np.where(
        wavelength < 2048.0, base_freq, np.where(wavelength > 8192.0, base_freq / 32.0, blended)
    )
    return np.repeat(frequency.astype(np.float32)[:, None], 128, axis=1)


def swap_cores(x):
    return lax.ppermute(x, "t", [(0, 1), (1, 0)])


def adamw(weight, first_moment, second_moment, gradient, step_rate):
    first_new = 0.9 * first_moment + 0.1 * gradient
    second_new = 0.95 * second_moment + 0.05 * gradient * gradient
    corrected = first_new / (1.0 - 0.9**STEP) / (jnp.sqrt(second_new / (1.0 - 0.95**STEP)) + 1e-08)
    return (first_new, second_new, weight - step_rate * (corrected + 0.1 * weight))


def slots(w, columns):
    return w.reshape(w.shape[0], -1, columns).transpose(1, 0, 2)


def unslots(g):
    return g.transpose(1, 0, 2).reshape(g.shape[1], -1)


def body(
    tokens,
    segments,
    cotangent,
    query_weight,
    key_weight,
    value_weight,
    output_weight,
    gate_weight,
    up_weight,
    down_weight,
    norm_gain_pair,
    query_first,
    key_first,
    value_first,
    output_first,
    gate_first,
    up_first,
    down_first,
    gains_first,
    query_second,
    key_second,
    value_second,
    output_second,
    gate_second,
    up_second,
    down_second,
    gains_second,
):
    gains = norm_gain_pair.astype(BF).astype(F32)
    gain_a, gain_m = gains[0][:, None], gains[1][:, None]
    low = lambda w: w.astype(BF).astype(F32)
    (
        resid,
        all_m,
        all_g,
        w_gate_up,
        w_down,
        kv,
        kvt,
        o_full,
        lse,
        o_low,
        all_a,
        w_qkv,
        w_out,
        q_wide,
        tables,
        starts,
    ) = forward_exchange(
        tokens[0],
        segments,
        jnp.broadcast_to(gains[:, :, None], (2, 32, 128)),
        jnp.asarray(rope_frequency()),
        query_weight,
        key_weight,
        value_weight,
        output_weight.T,
        cotangent[0],
        gate_weight,
        up_weight,
        down_weight.T,
    )
    gate_up = jnp.dot(all_m, w_gate_up, preferred_element_type=F32)
    gate, up = gate_up[:, :512], gate_up[:, 512:]
    sig = jax.nn.sigmoid(gate)
    silu = gate * sig
    act = (silu * up).astype(BF)

    g_act = jnp.dot(all_g, w_down, preferred_element_type=F32)
    g_gate = g_act * up * sig * (1.0 + gate * (1.0 - sig))
    g_up = g_act * silu
    g_gate_up = jnp.concatenate([g_gate, g_up], axis=1).astype(BF)
    input_grad, block_out, mlp_dealt, attn_dealt = backward_exchange(
        g_gate_up,
        act,
        w_gate_up,
        w_down,
        resid,
        cotangent[0],
        w_out,
        q_wide,
        kv,
        kvt,
        starts,
        o_full,
        lse,
        o_low,
        tables,
        w_qkv,
        tokens[0],
        all_m,
        all_g,
        all_a,
    )
    mlp_sum, attn_sum = mlp_dealt.astype(F32), attn_dealt.astype(F32)

    pairs = lambda g: unslots(g.reshape(4, 2, 32, HEAD_DIM).sum(axis=1))
    q_sum = unslots(attn_sum[:, :, :128])
    k_sum = pairs(attn_sum[:, :, 128:192])
    v_sum = pairs(attn_sum[:, :, 192:256])
    gate_sum = unslots(mlp_sum[:, :, :512])
    up_sum = unslots(mlp_sum[:, :, 512:1024])
    dots = lambda g, w: jnp.sum(g * low(w), axis=1)
    gains_half = jnp.stack(
        [
            dots(q_sum, query_weight) + dots(k_sum, key_weight) + dots(v_sum, value_weight),
            dots(gate_sum, gate_weight) + dots(up_sum, up_weight),
        ],
        axis=0,
    )
    gains_grad = gains_half + swap_cores(gains_half)
    query_grad, key_grad, value_grad = gain_a * q_sum, gain_a * k_sum, gain_a * v_sum
    gate_grad, up_grad = gain_m * gate_sum, gain_m * up_sum
    output_grad = unslots(attn_sum[:, :, 256:]).T
    down_grad = unslots(mlp_sum[:, :, 1024:]).T
    wide_rate = 2.0 * D ** (-0.5)
    outs = [block_out[None], input_grad[None]]
    for weight, first, second, grad, rate in (
        (query_weight, query_first, query_second, query_grad, wide_rate),
        (key_weight, key_first, key_second, key_grad, wide_rate),
        (value_weight, value_first, value_second, value_grad, wide_rate),
        (output_weight, output_first, output_second, output_grad, 2.0 * (4 * HEAD_DIM) ** (-0.5)),
        (gate_weight, gate_first, gate_second, gate_grad, wide_rate),
        (up_weight, up_first, up_second, up_grad, wide_rate),
        (down_weight, down_first, down_second, down_grad, 2.0 * FF ** (-0.5)),
        (norm_gain_pair, gains_first, gains_second, gains_grad, 1.5),
    ):
        outs.append(grad)
        outs.extend(adamw(weight, first, second, grad, rate))
    return tuple(outs)


def solution(mesh):
    split = Mesh(
        mesh.devices.reshape(tuple(SIZES.values())), tuple(SIZES)
    )
    heads = ("x", "z", "yl")
    every = ("dp", "x", "z", "yl")
    acts = P("dp", heads, None)
    rows_cut = P(every, "t")
    columns_cut = P("t", every)
    gains = P(None, every)
    weights = (rows_cut,) * 3 + (columns_cut,) + (rows_cut,) * 2 + (columns_cut, gains)
    in_specs = (acts, P("dp", heads), acts) + weights * 3
    out_specs = (acts, acts) + tuple(spec for spec in weights for _ in range(4))
    return jax.shard_map(
        body, mesh=split, in_specs=in_specs, out_specs=out_specs, check_vma=False
    )
```

```python
import functools
import itertools
import math

import jax
import jax.numpy as jnp
import numpy as np
from jax import lax
from jax.experimental import pallas as pl
from jax.experimental.pallas import tpu as pltpu
from jax.sharding import Mesh
from jax.sharding import PartitionSpec as P

D = 2048
FF = 8192
HEADS = 32
KV_HEADS = 8
HEAD_DIM = 64
STEP = 10
EPS = 1e-05

SIZES = {"dp": 2, "x": 4, "z": 4, "yl": 2, "t": 2}
GROUP = ("z", "yl")
CROSS = ("dp", "x")
MEMBERS = 8
HALF = 64
ROWS = 1024
LENGTH = 4096
DOC_MOST = 2048
DOCS = 10
QB = 256
KB = 512
BLOCKS = ROWS // QB
WIDE = 2 * QB
BF = jnp.bfloat16
F32 = jnp.float32


def shifts(axes):
    return list(itertools.product(*[range(SIZES[a]) for a in axes]))


def place(axes, shift, sign=1):
    index = 0
    for a, s in zip(axes, shift):
        index = index * SIZES[a] + lax.rem(
            lax.axis_index(a) + (s if sign > 0 else SIZES[a] - s), SIZES[a]
        )
    return index


def peer(axes, shift):
    return {
        a: lax.rem(lax.axis_index(a) + s, SIZES[a]) for a, s in zip(axes, shift) if s
    }


def other_core():
    return {"t": 1 - lax.axis_index("t")}


def hail(devices):
    for device in devices:
        pl.semaphore_signal(
            pltpu.get_barrier_semaphore(),
            inc=1,
            device_id=device,
            device_id_type=pl.DeviceIdType.MESH,
        )


def await_all(devices):
    pl.semaphore_wait(pltpu.get_barrier_semaphore(), len(devices))


def greet(devices):
    hail(devices)
    await_all(devices)


def remote(src, dst, send, recv, device):
    return pltpu.make_async_remote_copy(
        src_ref=src,
        dst_ref=dst,
        send_sem=send,
        recv_sem=recv,
        device_id=device,
        device_id_type=pl.DeviceIdType.MESH,
    )


def abt(left, right):
    return lax.dot_general(left, right, (((1,), (1,)), ((), ())), preferred_element_type=F32)


def atb(left, right):
    return lax.dot_general(left, right, (((0,), (0,)), ((), ())), preferred_element_type=F32)


DMA = pltpu.SemaphoreType.DMA
HBM = pl.BlockSpec(memory_space=pl.ANY)
VMEM = pl.BlockSpec(memory_space=pltpu.VMEM)
MOVES = shifts(GROUP)[1:]
TURNS = (1, 3, 2)


def members():
    return [other_core()] + [peer(GROUP, s) for s in MOVES]


def across():
    return [peer(("dp",), (1,))] + [peer(("x",), (s,)) for s in TURNS]


def finish(copies):
    for c in copies:
        c.wait()


INSIDE = ("yl", "z")
ACROSS = ("dp", "x")


def ring_places(axes):
    pair, ring = axes
    p, q = lax.axis_index(pair), lax.axis_index(ring)
    mate, up, down = {pair: 1 - p}, {ring: lax.rem(q + 1, 4)}, {ring: lax.rem(q + 3, 4)}
    return p, q, mate, up, down


RING_GATHER_SEMS = [DMA((9,)), DMA((9,)), DMA]


class RingGather:
    def __init__(self, x_ref, slot, rows, axes, sems, arrived=None):
        self.x_ref, self.slot, self.half, self.axes = x_ref, slot, rows // 2, axes
        self.ssem, self.rsem, self.local = sems
        self.copies = {}
        self.arrived = arrived if arrived is not None else lambda part: None
        p, q, mate, up, down = ring_places(axes)
        self.own = pltpu.make_async_copy(x_ref, slot(p, q), self.local)
        self.own.start()
        for k, to in enumerate((mate, up, down)):
            self.go(k, x_ref, slot(p, q), to)

    def go(self, k, src, dst, to):
        c = remote(src, dst, self.ssem.at[k], self.rsem.at[k], to)
        c.start()
        self.copies[k] = c

    def part(self, p, q, which=None):
        ref = self.slot(p, q)
        return ref if which is None else ref.at[pl.ds(which * self.half, self.half)]

    def wait_own(self):
        if self.own is not None:
            self.own.wait()
            self.own = None

    def pass_mate(self):
        p, q, _, up, down = ring_places(self.axes)
        self.copies[0].wait_recv()
        part = self.part(1 - p, q)
        self.go(3, part, part, up)
        self.go(4, part, part, down)
        self.arrived(part)

    def pass_ring(self, column):
        p, q, _, up, down = ring_places(self.axes)
        p = p if column == 0 else 1 - p
        at = 1 if column == 0 else 3
        for i, (step, to) in enumerate(((3, up), (1, down))):
            self.copies[at + i].wait_recv()
            there = lax.rem(q + step, 4)
            part = self.part(p, there, i)
            self.go(5 + 2 * column + i, part, part, to)
            self.arrived(self.part(p, there))

    def finish(self):
        p, q, _, _, _ = ring_places(self.axes)
        far = lax.rem(q + 2, 4)
        for column, p in enumerate((p, 1 - p)):
            for i in range(2):
                self.copies[5 + 2 * column + i].wait_recv()
            self.arrived(self.part(p, far))
        self.wait_own()
        for c in self.copies.values():
            c.wait_send()


TOKEN_GATHER_SEMS = RING_GATHER_SEMS + [DMA((8,)), DMA((8,))]


class TokenGather(RingGather):
    def __init__(self, x_ref, out_ref, sems):
        t = lax.axis_index("t")
        self.passed, self.had, self.tsend, self.trecv = [], set(), sems[3], sems[4]
        slot = lambda p, q: out_ref.at[2 * q + p, t]
        super().__init__(x_ref, slot, HALF, INSIDE, sems[:3], self.to_core)
        p, q, _, _, _ = ring_places(INSIDE)
        self.to_core(slot(p, q), x_ref)

    def to_core(self, part, src=None):
        k = len(self.passed)
        c = remote(part if src is None else src, part, self.tsend.at[k], self.trecv.at[k], other_core())
        c.start()
        self.passed.append(c)

    def have(self, *ks):
        for k in ks:
            if k not in self.had:
                self.passed[k].wait_recv()
                self.had.add(k)

    def finish(self):
        super().finish()
        self.have(*range(8))
        for c in self.passed:
            c.wait_send()


def add_rows(out_ref, terms, rows, step_rows):
    def step(r, carry):
        at = pl.ds(pl.multiple_of(r * step_rows, step_rows), step_rows)
        total = terms[0][at, :].astype(F32)
        for term in terms[1:]:
            total = total + term[at, :].astype(F32)
        out_ref[at, :] = total.astype(out_ref.dtype)
        return carry

    lax.fori_loop(0, rows // step_rows, step, 0)


RING_SCATTER_SEMS = [DMA((13,)), DMA((13,))]


def ring_scatter_slots(rows, wide):
    half = rows // 2
    return [
        pltpu.VMEM((2, half, wide), BF),
        pltpu.VMEM((2, half, wide), BF),
        pltpu.VMEM((2, rows, wide), BF),
        pltpu.VMEM((2, rows, wide), BF),
        pltpu.VMEM((rows, wide), BF),
    ]


class RingScatter:
    def __init__(self, rows, axes, slots, sems):
        self.rows, self.half, self.axes = rows, rows // 2, axes
        self.far_up, self.far_down, self.from_down, self.from_up, self.back = slots
        self.ssem, self.rsem = sems
        self.copies = {}

    def go(self, k, src, dst, to):
        c = remote(src, dst, self.ssem.at[k], self.rsem.at[k], to)
        c.start()
        self.copies[k] = c

    def part(self, p, q, at):
        return self.held(p, q).at[at]

    def halves(self):
        return pl.ds(0, self.half), pl.ds(self.half, self.half)

    def add(self, out_ref, terms, rows):
        add_rows(out_ref, terms, rows, 16)

    def send_far(self, p):
        _, _, _, up, down = ring_places(self.axes)
        first, second = self.halves()
        self.go(2 * p, self.part(p, 2, first), self.far_up.at[p], up)
        self.go(2 * p + 1, self.part(p, 2, second), self.far_down.at[p], down)

    def send_near(self, p):
        _, _, _, up, down = ring_places(self.axes)
        first, second = self.halves()
        self.go(4 + 2 * p, self.part(p, 1, second), self.from_down.at[p, second], up)
        self.go(5 + 2 * p, self.part(p, 3, first), self.from_up.at[p, first], down)

    def send_joined(self, p):
        _, _, _, up, down = ring_places(self.axes)
        first, second = self.halves()
        self.copies[2 * p].wait_recv()
        part = self.part(p, 1, first)
        self.add(part, [part, self.far_up.at[p]], self.half)
        self.go(8 + 2 * p, part, self.from_down.at[p, first], up)
        self.copies[2 * p + 1].wait_recv()
        part = self.part(p, 3, second)
        self.add(part, [part, self.far_down.at[p]], self.half)
        self.go(9 + 2 * p, part, self.from_up.at[p, second], down)

    def arrivals(self, p):
        for k in (4 + 2 * p, 5 + 2 * p, 8 + 2 * p, 9 + 2 * p):
            self.copies[k].wait_recv()

    def send_mate(self):
        _, _, mate, _, _ = ring_places(self.axes)
        self.arrivals(1)
        part = self.held(1, 0)
        self.add(part, [part, self.from_down.at[1], self.from_up.at[1]], self.rows)
        self.go(12, part, self.back, mate)

    def total(self, out_ref):
        self.arrivals(0)
        self.copies[12].wait_recv()
        self.add(
            out_ref,
            [self.held(0, 0), self.from_down.at[0], self.from_up.at[0], self.back],
            self.rows,
        )
        for c in self.copies.values():
            c.wait_send()


TOKEN_SCATTER_SEMS = RING_SCATTER_SEMS + [DMA((4, 2)), DMA((4, 2))]


def token_scatter_slots():
    return ring_scatter_slots(HALF, D) + [pltpu.VMEM((4, 2, HALF, D), BF)]


STAGE = pltpu.VMEM((4, 2, 2, HALF, D), BF)


class TokenScatter(RingScatter):
    def __init__(self, a_ref, w_ref, slots, stage, sems):
        super().__init__(HALF, INSIDE, slots[:5], sems[:2])
        self.a_ref, self.w_ref = a_ref, w_ref
        self.stage, self.theirs = stage, slots[5]
        self.tsend, self.trecv = sems[2:]
        self.swaps = {}

    def pair_place(self, p):
        own = lax.axis_index("yl")
        return own if p == 0 else 1 - own

    def held(self, p, q):
        return self.stage.at[q, self.pair_place(p), lax.axis_index("t")]

    def make(self, q):
        row = lax.rem(lax.axis_index("z") + q, 4) * 256
        a = self.a_ref[pl.ds(pl.multiple_of(row, 256), 256), :]

        def step(n, carry):
            at = pl.ds(pl.multiple_of(n * 512, 512), 512)
            product = abt(a, self.w_ref[at, :]).astype(BF)
            self.stage[q, :, :, :, at] = product.reshape(2, 2, HALF, 512)
            return carry

        lax.fori_loop(0, D // 512, step, 0)

    def swap(self, q):
        t = lax.axis_index("t")
        for p in (1, 0):
            at = self.pair_place(p)
            c = remote(
                self.stage.at[q, at, 1 - t],
                self.theirs.at[q, at],
                self.tsend.at[q, p],
                self.trecv.at[q, p],
                other_core(),
            )
            c.start()
            self.swaps[q, p] = c

    def pair(self, p, q):
        self.swaps[q, p].wait_recv()
        part = self.held(p, q)
        self.add(part, [part, self.theirs.at[q, self.pair_place(p)]], HALF)

    def total(self, out_ref):
        super().total(out_ref)
        for c in self.swaps.values():
            c.wait_send()

    def pair_ring(self, q):
        self.pair(1, q)
        self.pair(0, q)

    def fill(self, *qs):
        for q in qs:
            self.make(q)
            self.swap(q)


BY_NEED = [(1, 2), (0, 2), (1, 1), (1, 3), (0, 1), (0, 3), (1, 0), (0, 0)]


def grad_scatter_slots(wide):
    return ring_scatter_slots(256, wide) + [pltpu.VMEM((2, 4, 256, wide), BF)]


COLUMNS = pltpu.VMEM((2, 2, ROWS, 256), BF)


class GradScatter(RingScatter):
    def __init__(self, pairs, slots, columns, sems):
        super().__init__(256, ACROSS, slots[:5], sems[:2])
        self.pairs, self.blocks, self.columns, self.lsem = pairs, slots[5], columns, sems[2]
        self.loads = {}
        self.done = 0
        self.load(0)
        self.load(1)

    def held(self, p, q):
        return self.blocks.at[p, q]

    def load(self, k):
        p, q = BY_NEED[k]
        dp, x = lax.axis_index("dp"), lax.axis_index("x")
        row = (dp if p == 0 else 1 - dp) * 4 + lax.rem(x + q, 4)
        at = pl.ds(pl.multiple_of(row * 256, 256), 256)
        for i, (x_ref, _) in enumerate(self.pairs):
            c = pltpu.make_async_copy(
                x_ref.at[:, at], self.columns.at[k % 2, i], self.lsem.at[k % 2, i]
            )
            c.start()
            self.loads[k, i] = c

    def make(self):
        k = self.done
        p, q = BY_NEED[k]
        start = 0
        for i, (_, g_ref) in enumerate(self.pairs):
            self.loads[k, i].wait()
            wide = g_ref.shape[1]
            self.blocks[p, q, :, start : start + wide] = atb(
                self.columns[k % 2, i], g_ref[...]
            ).astype(BF)
            start += wide
        self.done = k + 1
        if k + 2 < len(BY_NEED):
            self.load(k + 2)

def both(method):
    method(1)
    method(0)


def scatter_both(sums, grads, devices=None):
    sums.make(2)
    if devices is not None:
        await_all(devices)
    sums.swap(2)
    grads.make()
    grads.send_far(1)
    sums.pair(1, 2)
    sums.send_far(1)
    sums.pair(0, 2)
    sums.send_far(0)
    sums.fill(1, 3)
    sums.pair(1, 1)
    sums.pair(1, 3)
    sums.send_near(1)
    sums.send_joined(1)
    grads.make()
    grads.send_far(0)
    sums.pair(0, 1)
    sums.pair(0, 3)
    sums.send_near(0)
    sums.fill(0)
    sums.send_joined(0)
    grads.make()
    grads.make()
    grads.send_near(1)
    sums.pair_ring(0)
    sums.send_mate()
    grads.send_joined(1)
    grads.make()
    grads.make()
    grads.send_near(0)
    grads.make()
    grads.make()


GRAD_SCATTER_SEMS = RING_SCATTER_SEMS + [DMA((2, 2))]


def weight_gather(x_ref, out_ref, sems):
    return RingGather(x_ref, lambda p, q: out_ref.at[p, q], 256, ACROSS, sems)


DEAL_SEMS = [DMA((7,)), DMA((7,)), DMA]


def deal_start(x_ref, out_ref, sems):
    send, recv, local = sems
    me = place(GROUP, (0, 0))
    own = pltpu.make_async_copy(x_ref.at[me], out_ref.at[me], local)
    own.start()
    copies = []
    for i, s in enumerate(MOVES):
        c = remote(
            x_ref.at[place(GROUP, s)], out_ref.at[me], send.at[i], recv.at[i], peer(GROUP, s)
        )
        c.start()
        copies.append(c)
    return [own] + copies


def deal_columns(x_ref, out_ref, at, wide, sems):
    send, recv, local = sems
    me = place(GROUP, (0, 0))
    slot = lambda c: x_ref.at[:, pl.ds(pl.multiple_of(c * wide, wide), wide)]
    there = out_ref.at[me, :, pl.ds(at, wide)]
    own = pltpu.make_async_copy(slot(me), there, local)
    own.start()
    copies = []
    for i, s in enumerate(MOVES):
        c = remote(slot(place(GROUP, s)), there, send.at[i], recv.at[i], peer(GROUP, s))
        c.start()
        copies.append(c)
    return [own] + copies


def own_half(ref):
    return pl.ds(pl.multiple_of(lax.axis_index("t") * HALF, HALF), HALF)


def fold(gain, weight):
    return (gain * weight.astype(BF).astype(F32)).astype(BF)


def split(refs, *counts):
    parts, at = [], 0
    for count in counts:
        parts.append(refs[at : at + count])
        at += count
    assert at == len(refs)
    return parts


def scale_rows(x):
    return lax.rsqrt(jnp.mean(x * x, axis=1, keepdims=True) + EPS)


def norm_back(unit, inverse, grad):
    return inverse * (grad - unit * jnp.mean(grad * unit, axis=1, keepdims=True))


def call(kernel, collective_id, name, args, in_specs, outs, out_specs, scratch):
    sent = 60_000_000
    return pl.pallas_call(
        kernel,
        out_shape=[jax.ShapeDtypeStruct(s, d) for s, d in outs],
        in_specs=in_specs,
        out_specs=out_specs,
        scratch_shapes=scratch,
        compiler_params=pltpu.CompilerParams(
            collective_id=collective_id, has_side_effects=True, vmem_limit_bytes=60 * 2**20
        ),
        cost_estimate=pl.CostEstimate(flops=0, bytes_accessed=sent, transcendentals=0),
        name=name,
    )(*args)


def turn_back(v, cos_tab, sin_tab):
    a, b = v[: HEAD_DIM // 2], v[HEAD_DIM // 2 :]
    return jnp.concatenate([a * cos_tab + b * sin_tab, b * cos_tab - a * sin_tab], axis=0)


def key_blocks(b, rel):
    x = lax.axis_index("x")
    first = x * ROWS + b * QB
    chunk = (x - rel) * (ROWS // KB)
    low = lax.max(lax.max(first - (DOC_MOST - 1), 0) // KB, chunk)
    high = lax.min((first + QB + KB - 1) // KB, chunk + ROWS // KB)
    return low, high


def mask_scores(s, base, start, b, rel):
    key = base + lax.broadcasted_iota(jnp.int32, s.shape, 0)
    allowed = key >= start
    if rel == 0:
        first = lax.axis_index("x") * ROWS + b * QB
        own = first + lax.broadcasted_iota(jnp.int32, (1, QB), 1)
        allowed = allowed & (key <= jnp.concatenate([own, own], axis=1))
    return jnp.where(allowed, s, -1e30)


def block_lanes(b):
    return pl.ds(pl.multiple_of(b * QB, QB), QB)


def beside_lanes(ref, b):
    at = block_lanes(b)
    return jnp.concatenate([ref[0, :, at], ref[1, :, at]], axis=1)


def twice_lanes(ref, b):
    v = ref[:, block_lanes(b)]
    return jnp.concatenate([v, v], axis=1)


def attend_part(q_ref, kv_ref, kvt_ref, start_ref, top_ref, total_ref, acc_ref, b, rel):
    q, start = beside_lanes(q_ref, b), twice_lanes(start_ref, b)

    def step(j, carry):
        top, total, acc = carry
        base = pl.multiple_of(j * KB, KB)
        s = jnp.dot(kv_ref[pl.ds(base, KB), :], q, preferred_element_type=F32)
        s = mask_scores(s, base, start, b, rel)
        new_top = jnp.maximum(top, jnp.max(s, axis=0, keepdims=True))
        p = jnp.exp(s - new_top)
        fade = jnp.exp(top - new_top)
        total = total * fade + jnp.sum(p, axis=0, keepdims=True)
        acc = acc * fade + jnp.dot(
            kvt_ref[:, pl.ds(base, KB)], p.astype(BF), preferred_element_type=F32
        )
        return (new_top, total, acc)

    if rel == 0:
        init = (
            jnp.full((1, WIDE), -1e30, F32),
            jnp.zeros((1, WIDE), F32),
            jnp.zeros((2 * HEAD_DIM, WIDE), F32),
        )
    else:
        init = (top_ref[b], total_ref[b], acc_ref[b])
    low, high = key_blocks(b, rel)
    top_ref[b], total_ref[b], acc_ref[b] = lax.fori_loop(low, high, step, init)


def attend_end(top_ref, total_ref, acc_ref, o_ref, lse_ref, low_ref, b):
    at = block_lanes(b)
    total = total_ref[b]
    o = acc_ref[b][HEAD_DIM:] / total
    lse = top_ref[b] + jnp.log(total)
    for h in range(2):
        o_ref[h, :, at] = o[:, h * QB : (h + 1) * QB]
        lse_ref[h : h + 1, at] = lse[:, h * QB : (h + 1) * QB]
    beside = jnp.concatenate([o[:, :QB], o[:, QB:]], axis=0)
    low_ref[at, :] = beside.T.astype(BF)


def start_block(all_ref, chunk, sems, b):
    pieces = []
    for c in range(2):
        for core in range(2):
            at = pl.ds((2 * c + core) * HALF, HALF)
            copy = pltpu.make_async_copy(
                all_ref.at[2 * b + c, core], chunk.at[at], sems.at[2 * c + core]
            )
            copy.start()
            pieces.append(copy)
    return pieces


def load_block(all_ref, chunk, sems, b):
    finish(start_block(all_ref, chunk, sems, b))


def document_starts(seg_ref):
    every = seg_ref[...].reshape(LENGTH * 8 // 128, 128)
    x = lax.axis_index("x")
    own = jnp.concatenate([seg_ref[x, g, 0:1, :] for g in range(MEMBERS)], axis=1)
    starts = jnp.zeros((1, ROWS), F32)
    for d in range(DOCS - 1):
        same = jnp.where(every == d, 1.0, 0.0)
        count = jnp.sum(jnp.sum(same, axis=0, keepdims=True), axis=1, keepdims=True) * 0.125
        starts = starts + jnp.where(own > d, count, 0.0)
    return starts.astype(jnp.int32)


def forward_kernel(*refs):
    ins, outs, slots, others, sems, gather, rings, keys, deals, seg_sems, lsems = split(
        refs, 12, 19, 6, 22, 4, 15, 12, 3, 15, 5, 3
    )
    (
        tokens_ref, seg_ref, gains_ref, freq_ref, wq_ref, wk_ref, wv_ref, wo_ref, cot_ref,
        gate_ref, up_ref, down_ref,
    ) = ins
    (
        resid_ref, all_m, all_g, w_gu, w_down, kv_ref, kvt_ref, o_ref, lse_ref, low_ref,
        all_a, w_qkv, w_out, w_out_turned, q_ref, tables, start_ref, g_ref, act_ref,
    ) = outs
    (
        stage, total, unit, gu_part, down_part, *states, qkv_part, wo_part, seg_all, w_turned,
        chunk, qkv_slots, wo_slots, seg_own, raw, gate_low, up_low, down_low, unit_a, pairs,
    ) = others
    cos_ref, sin_ref = tables.at[0], tables.at[1]
    ksend, krecv, klocal = keys
    ssend, srecv, xsend, xrecv, slocal = seg_sems
    devices = members() + across()
    hail(devices)
    fetches = []
    for i, ref in enumerate((gate_ref, up_ref, down_ref)):
        c = pltpu.make_async_copy(ref, raw.at[i], lsems[1].at[i])
        c.start()
        fetches.append(c)
    x, z = lax.axis_index("x"), lax.axis_index("z")
    me = place(GROUP, (0, 0))
    gain_a, gain_m = gains_ref[0][:, 0:1], gains_ref[1][:, 0:1]
    wq, wk, wv = (fold(gain_a, ref[...]) for ref in (wq_ref, wk_ref, wv_ref))
    wo = wo_ref[...].astype(BF)
    for c in range(MEMBERS):
        head = slice(c // 2 * HEAD_DIM, (c // 2 + 1) * HEAD_DIM)
        qkv_slots[c] = jnp.concatenate(
            [wq[:, c * 128 : (c + 1) * 128], wk[:, head], wv[:, head]], axis=1
        )
        wo_slots[c] = wo[:, c * 128 : (c + 1) * 128]
    rows = tokens_ref[own_half(tokens_ref), :].astype(F32)
    unit_a[...] = (rows * scale_rows(rows)).astype(BF)
    seg_own[...] = jnp.broadcast_to(seg_ref[...], (8, 128))
    await_all(devices)

    early = deal_start(qkv_slots, qkv_part, deals[9:12]) + deal_start(wo_slots, wo_part, deals[12:])
    tokens = TokenGather(unit_a, all_a, gather[10:])
    seg_copies = [pltpu.make_async_copy(seg_own, seg_all.at[x, me], slocal)]
    seg_copies[0].start()
    for i, s in enumerate(MOVES):
        c = remote(seg_own, seg_all.at[x, me], ssend.at[i], srecv.at[i], peer(GROUP, s))
        c.start()
        seg_copies.append(c)
    finish(early)
    qkv_weights = weight_gather(qkv_part.reshape(256, 256), w_qkv, rings[6:9])
    out_weights = weight_gather(wo_part.reshape(256, 128), w_out, rings[9:])
    finish(seg_copies)
    crossed = []
    for i, to in enumerate(across()[1:]):
        c = remote(seg_all.at[x], seg_all.at[x], xsend.at[i], xrecv.at[i], to)
        c.start()
        crossed.append(c)
    everything = [tokens, qkv_weights]
    for g in everything:
        g.pass_mate()
    for g in everything:
        g.pass_ring(0)
    finish(crossed)
    starts = document_starts(seg_all)
    start_ref[...] = starts
    own = x * ROWS + lax.broadcasted_iota(jnp.int32, (1, ROWS), 1)
    angles = freq_ref[:, 0:1] * (own - starts).astype(F32)
    cos_ref[...] = jnp.cos(angles)
    sin_ref[...] = jnp.sin(angles)
    for c in fetches:
        c.wait()
    gate_low[...] = fold(gain_m, raw[0])
    up_low[...] = fold(gain_m, raw[1])
    down_low[...] = raw[2].astype(BF)
    for g in everything:
        g.pass_ring(1)
    dealt = deal_columns(gate_low, gu_part, 0, 512, deals[:3])
    dealt += deal_columns(up_low, gu_part, 512, 512, deals[3:6])
    dealt += deal_columns(down_low, down_part, 0, 512, deals[6:9])
    out_weights.pass_mate()
    out_weights.pass_ring(0)
    out_weights.pass_ring(1)
    qkv_weights.finish()
    for r in range(8):
        w_turned[:, r * 256 : (r + 1) * 256] = w_qkv[r // 4, r % 4].T
    key_copies = ([], [])

    def project(b):
        load_block(all_a, chunk, lsems[0], b)
        qkv = abt(w_turned[...], chunk[...])
        at = block_lanes(b)
        c, s = cos_ref[:, at], -sin_ref[:, at]
        zeros = jnp.zeros((HEAD_DIM, QB), BF)
        for h in range(2):
            q = turn_back(qkv[h * HEAD_DIM : (h + 1) * HEAD_DIM], c, s)
            q_ref[h, :, at] = jnp.concatenate([(q * HEAD_DIM ** (-0.5)).astype(BF), zeros], axis=0)
        k = turn_back(qkv[128:192], c, s)
        kv = jnp.concatenate([k, qkv[192:]], axis=0)
        here = pl.ds(pl.multiple_of(x * ROWS + b * QB, QB), QB)
        kvt_ref[:, here] = kv.astype(BF)
        kv_ref[here, :] = kv.T.astype(BF)
        k = len(key_copies[0])
        for i in range(2):
            there = kv_ref.at[here]
            c = remote(there, there, ksend.at[i, k], krecv.at[i, k], peer(("x",), (i + 1,)))
            c.start()
            key_copies[i].append(c)

    tokens.wait_own()
    tokens.have(0, 1)
    project(z)
    tokens.have(2, 4)
    project(lax.rem(z + 3, 4))
    tokens.have(3, 5)
    project(lax.rem(z + 1, 4))
    tokens.finish()
    project(lax.rem(z + 2, 4))

    cots = TokenGather(cot_ref.at[own_half(cot_ref)], all_g, gather[:5])

    def turn(rel):
        base = lax.rem(x + 4 - rel, 4) * ROWS
        for c in range(ROWS // KB):
            at = pl.ds(pl.multiple_of(base + c * KB, KB), KB)
            kvt_ref[:, at] = kv_ref[at, :].T

    def part(b, rel):
        attend_part(q_ref, kv_ref, kvt_ref, start_ref, *states, b, rel)

    for b in range(BLOCKS):
        part(b, 0)
    for c in key_copies[0]:
        c.wait_recv()
    turn(1)
    for b in range(BLOCKS):
        part(b, 1)
    finish(dealt)
    cots.pass_mate()
    for c in key_copies[1]:
        c.wait_recv()
    for c in key_copies[0] + key_copies[1]:
        c.wait_send()
    weights = [
        weight_gather(gu_part.reshape(256, 1024), w_gu, rings[:3]),
        weight_gather(down_part.reshape(256, 512), w_down, rings[3:6]),
    ]
    turn(2)
    out_weights.finish()
    sums = TokenScatter(low_ref, w_out.reshape(D, 128), slots, stage, sems)

    def attend(q):
        b = lax.rem(z + q, 4)
        part(b, 2)
        attend_end(*states, o_ref, lse_ref, low_ref, b)
        sums.make(q)
        sums.swap(q)

    attend(2)
    attend(1)
    sums.pair(1, 2)
    sums.send_far(1)
    sums.pair(0, 2)
    sums.send_far(0)
    attend(3)
    for p in (1, 0):
        sums.pair(p, 1)
        sums.pair(p, 3)
        sums.send_near(p)
        sums.send_joined(p)
    attend(0)
    sums.pair_ring(0)
    for g in weights:
        g.pass_mate()
    sums.send_mate()
    cots.pass_ring(0)
    for g in weights:
        g.pass_ring(0)
    cots.pass_ring(1)
    sums.total(total)
    resid = tokens_ref[own_half(tokens_ref), :].astype(F32) + total[...]
    resid_ref[...] = resid
    unit[...] = (resid * scale_rows(resid)).astype(BF)
    tokens = TokenGather(unit, all_m, gather[5:10])
    tokens.pass_mate()
    for g in weights:
        g.pass_ring(1)
    tokens.pass_ring(0)
    tokens.pass_ring(1)
    for r in range(8):
        w_out_turned[:, r * 256 : (r + 1) * 256] = w_out[r // 4, r % 4].T
    cots.finish()
    tokens.finish()
    order = [lax.rem(z + q, 4) for q in (0, 3, 1, 2)]
    blocks = {}

    def fetch(k):
        for i, ref in enumerate((all_m, all_g)):
            blocks[k, i] = start_block(ref, pairs.at[k % 2, i], lsems[2].at[k % 2, i], order[k])

    fetch(0)
    fetch(1)
    for g in weights:
        g.finish()
    w_gate_up, w_act = w_gu.reshape(D, 1024), w_down.reshape(D, 512)
    for k in range(BLOCKS):
        finish(blocks[k, 0] + blocks[k, 1])
        at = block_lanes(order[k])
        gate_up = jnp.dot(pairs[k % 2, 0], w_gate_up[...], preferred_element_type=F32)
        g_act = jnp.dot(pairs[k % 2, 1], w_act[...], preferred_element_type=F32)
        gate, up = gate_up[:, :512], gate_up[:, 512:]
        sig = 1.0 / (1.0 + jnp.exp(-gate))
        silu = gate * sig
        act_ref[at, :] = (silu * up).astype(BF)
        g_gate = g_act * up * sig * (1.0 + gate * (1.0 - sig))
        g_ref[at, :512] = g_gate.astype(BF)
        g_ref[at, 512:] = (g_act * silu).astype(BF)
        if k + 2 < BLOCKS:
            fetch(k + 2)


def forward_exchange(*args):
    slots = (MEMBERS, 2, HALF, D)
    outs = [
        ((HALF, D), F32),
        (slots, BF),
        (slots, BF),
        ((2, 4, 256, 1024), BF),
        ((2, 4, 256, 512), BF),
        ((LENGTH, 128), BF),
        ((128, LENGTH), BF),
        ((2, HEAD_DIM, ROWS), F32),
        ((2, ROWS), F32),
        ((ROWS, 128), BF),
        (slots, BF),
        ((2, 4, 256, 256), BF),
        ((2, 4, 256, 128), BF),
        ((128, D), BF),
        ((2, 128, ROWS), BF),
        ((2, HEAD_DIM // 2, ROWS), F32),
        ((1, ROWS), jnp.int32),
        ((ROWS, 1024), BF),
        ((ROWS, 512), BF),
    ]
    scratch = token_scatter_slots() + [
        STAGE,
        pltpu.VMEM((HALF, D), F32),
        pltpu.VMEM((HALF, D), BF),
        pltpu.VMEM((MEMBERS, 32, 1024), BF),
        pltpu.VMEM((MEMBERS, 32, 512), BF),
        pltpu.VMEM((BLOCKS, 1, WIDE), F32),
        pltpu.VMEM((BLOCKS, 1, WIDE), F32),
        pltpu.VMEM((BLOCKS, 2 * HEAD_DIM, WIDE), F32),
        pltpu.VMEM((MEMBERS, 32, 256), BF),
        pltpu.VMEM((MEMBERS, 32, 128), BF),
        pltpu.VMEM((4, MEMBERS, 8, 128), jnp.int32),
        pltpu.VMEM((256, D), BF),
        pltpu.VMEM((256, D), BF),
        pltpu.VMEM((MEMBERS, 32, 256), BF),
        pltpu.VMEM((MEMBERS, 32, 128), BF),
        pltpu.VMEM((8, 128), jnp.int32),
        pltpu.VMEM((3, 32, 4096), F32),
        pltpu.VMEM((32, 4096), BF),
        pltpu.VMEM((32, 4096), BF),
        pltpu.VMEM((32, 4096), BF),
        pltpu.VMEM((HALF, D), BF),
        pltpu.VMEM((2, 2, 256, D), BF),
    ]
    scratch += TOKEN_SCATTER_SEMS + TOKEN_GATHER_SEMS * 3 + RING_GATHER_SEMS * 4
    scratch += [DMA((2, 4)), DMA((2, 4)), DMA] + DEAL_SEMS * 5
    scratch += [DMA((7,)), DMA((7,)), DMA((3,)), DMA((3,)), DMA, DMA((4,)), DMA((3,))]
    scratch += [DMA((2, 2, 4))]
    (
        resid, all_m, all_g, w_gu, w_down, kv, kvt, o, lse, o_low, all_a, w_qkv, _, w_out, q,
        tables, starts, g_gate_up, act,
    ) = call(
        forward_kernel,
        1,
        "forward_exchange",
        args,
        [VMEM] * 8 + [HBM] * 4,
        outs,
        [VMEM] + [HBM] * 2 + [VMEM] * 7 + [HBM] + [VMEM] * 8,
        scratch,
    )
    return (
        resid,
        all_m.reshape(ROWS, D),
        all_g.reshape(ROWS, D),
        w_gu.reshape(D, 1024),
        w_down.reshape(D, 512),
        kv,
        kvt,
        o,
        lse,
        o_low,
        all_a.reshape(ROWS, D),
        w_qkv.reshape(D, 256),
        w_out,
        q,
        tables,
        starts,
        g_gate_up,
        act,
    )


def attend_back_part(q_ref, kv_ref, kvt_ref, start_ref, lse_ref, g_ref, dot_ref, dq_ref, acc_ref, b, rel):
    q, start, g, row_dot = beside_lanes(q_ref, b), twice_lanes(start_ref, b), g_ref[b], dot_ref[b]
    at = block_lanes(b)
    lse = jnp.concatenate([lse_ref[0:1, at], lse_ref[1:2, at]], axis=1)

    def step(j, dq):
        base = pl.multiple_of(j * KB, KB)
        kv = kv_ref[pl.ds(base, KB), :]
        s = jnp.dot(kv, q, preferred_element_type=F32)
        p = jnp.exp(mask_scores(s, base, start, b, rel) - lse)
        g_p = jnp.dot(kv, g, preferred_element_type=F32)
        g_s = (p * (g_p - row_dot)).astype(BF)
        acc_ref[pl.ds(base, KB), :] += abt(g_s, q) + abt(p.astype(BF), g)
        return dq + jnp.dot(kvt_ref[:, pl.ds(base, KB)], g_s, preferred_element_type=F32)

    low, high = key_blocks(b, rel)
    dq = jnp.zeros((2 * HEAD_DIM, WIDE), F32) if rel == 2 else dq_ref[b]
    dq_ref[b] = lax.fori_loop(low, high, step, dq)


def backward_kernel(*refs):
    ins, outs, slots, mids, others, keys, sems, gsems, gather, ksems, csems, deals = split(
        refs, 20, 5, 18, 12, 12, 6, 12, 6, 5, 4, 7, 6
    )
    (
        g_ref, act_ref, wgu_ref, wdown_ref, resid_ref, cot_ref, wot_ref, q_ref, kv_ref, kvt_ref,
        start_ref, o_ref, lse_ref, low_ref, tables, wqkv_ref, tokens_ref,
        all_m, all_g, all_a,
    ) = ins
    cos_ref, sin_ref = tables.at[0], tables.at[1]
    input_grad, block_out, m_dealt, a_dealt, all_r = outs
    stage, columns, total, grad, g_resid, low, out_low, m_sum, a_sum, chunk, g_qkv, key_sum = others
    acc_ref, key_low, key_land, gw_ref, dot_ref, dq_ref = keys
    devices = members() + across()
    hail(devices)
    t, x = lax.axis_index("t"), lax.axis_index("x")
    sums = TokenScatter(g_ref, wgu_ref, slots[:6], stage, sems[:4])
    grads = GradScatter([(all_m, g_ref), (all_g, act_ref)], mids[:6], columns, gsems[:3])
    scatter_both(sums, grads, devices)
    grads.send_joined(0)
    sums.total(total)
    resid = resid_ref[...]
    inverse = scale_rows(resid)
    back = cot_ref[own_half(cot_ref), :].astype(F32) + norm_back(resid * inverse, inverse, total[...])
    g_resid[...] = back
    low[...] = back.astype(BF)
    tokens = TokenGather(low, all_r, gather)

    downs = TokenScatter(act_ref, wdown_ref, slots[6:12], stage, sems[4:8])

    def lead(b):
        load_block(all_r, chunk, ksems[3], b)
        g = abt(wot_ref[...], chunk[...]).astype(BF)
        beside = jnp.concatenate([g[:HEAD_DIM], g[HEAD_DIM:]], axis=1)
        o = beside_lanes(o_ref, b)
        dot_ref[b] = jnp.sum(o * beside.astype(F32), axis=0, keepdims=True)
        gw_ref[b] = jnp.concatenate([jnp.zeros_like(beside), beside], axis=0)

    def part(b, rel):
        attend_back_part(
            q_ref, kv_ref, kvt_ref, start_ref, lse_ref, gw_ref, dot_ref, dq_ref, acc_ref, b, rel
        )

    def end(b):
        dq = dq_ref[b][:HEAD_DIM] * HEAD_DIM ** (-0.5)
        at = block_lanes(b)
        c, s = cos_ref[:, at], sin_ref[:, at]
        turned = jnp.concatenate(
            [turn_back(dq[:, :QB], c, s), turn_back(dq[:, QB:], c, s)], axis=0
        )
        g_qkv[at, :128] = turned.T.astype(BF)

    key_copies = []

    def send_keys(rel):
        i = rel - 1
        s = 4 - rel
        there = pl.multiple_of(lax.rem(x + s, 4) * ROWS, ROWS)
        add_rows(key_low.at[i], [acc_ref.at[pl.ds(there, ROWS)]], ROWS, 256)
        c = remote(
            key_low.at[i], key_land.at[i], ksems[0].at[i], ksems[1].at[i], peer(("x",), (s,))
        )
        c.start()
        key_copies.append(c)

    z = lax.axis_index("z")
    acc_ref[...] = jnp.zeros_like(acc_ref)
    downs.fill(2, 1)
    tokens.pass_mate()
    tokens.pass_ring(0)
    tokens.wait_own()
    tokens.have(0, 1)
    lead(z)
    downs.fill(3, 0)
    for q in (2, 1, 3):
        downs.pair_ring(q)
    tokens.pass_ring(1)
    grads.send_mate()
    tokens.have(2, 4)
    lead(lax.rem(z + 3, 4))
    tokens.have(3, 5)
    lead(lax.rem(z + 1, 4))
    tokens.finish()
    both(downs.send_far)
    both(downs.send_near)
    lead(lax.rem(z + 2, 4))
    for b in range(BLOCKS):
        part(b, 2)
    send_keys(2)
    both(downs.send_joined)
    downs.pair_ring(0)
    for b in range(BLOCKS):
        part(b, 1)
    send_keys(1)
    downs.send_mate()
    grads.total(m_sum)
    m_deal = deal_start(m_sum.reshape(MEMBERS, 32, 1536), m_dealt, deals[:3])
    for b in range(BLOCKS):
        part(b, 0)
        end(b)
    downs.total(total)
    out_low[...] = (resid_ref[...] + total[...]).astype(BF)
    copies = [
        pltpu.make_async_copy(out_low, block_out.at[t], csems[2]),
        remote(out_low, block_out.at[t], csems[0], csems[1], other_core()),
    ]
    for c in copies:
        c.start()
    for c in key_copies:
        c.wait()
    own = pl.ds(pl.multiple_of(x * ROWS, ROWS), ROWS)
    add_rows(key_sum, [acc_ref.at[own]] + [key_land.at[i] for i in range(2)], ROWS, 256)
    for b in range(BLOCKS):
        at = pl.ds(b * QB, QB)
        v = key_sum[at, :].T
        k = turn_back(v[:HEAD_DIM], cos_ref[:, at], sin_ref[:, at])
        g_qkv[at, 128:] = jnp.concatenate([k, v[HEAD_DIM:]], axis=0).T.astype(BF)

    last = TokenScatter(g_qkv, wqkv_ref, slots[12:], stage, sems[8:])
    attn = GradScatter(
        [(all_a, g_qkv), (all_r.reshape(ROWS, D), low_ref)], mids[6:], columns, gsems[3:]
    )
    scatter_both(last, attn)
    attn.send_mate()
    attn.send_joined(0)
    attn.total(a_sum)
    a_deal = deal_start(a_sum.reshape(MEMBERS, 32, 384), a_dealt, deals[3:])
    last.total(total)
    rows = tokens_ref[own_half(tokens_ref), :].astype(F32)
    inverse = scale_rows(rows)
    grad[...] = g_resid[...] + norm_back(rows * inverse, inverse, total[...])
    more = [
        pltpu.make_async_copy(grad, input_grad.at[t], csems[5]),
        remote(grad, input_grad.at[t], csems[3], csems[4], other_core()),
    ]
    for c in more:
        c.start()
    finish(copies + more + m_deal + a_deal)


def backward_exchange(*args):
    outs = [
        ((2, HALF, D), F32),
        ((2, HALF, D), BF),
        ((MEMBERS, 32, 1536), BF),
        ((MEMBERS, 32, 384), BF),
        ((MEMBERS, 2, HALF, D), BF),
    ]
    wide, low = pltpu.VMEM((HALF, D), F32), pltpu.VMEM((HALF, D), BF)
    scratch = token_scatter_slots() * 3 + grad_scatter_slots(1536) + grad_scatter_slots(384)
    scratch += [STAGE, COLUMNS, wide, wide, wide, low, low]
    scratch += [
        pltpu.VMEM((256, 1536), BF),
        pltpu.VMEM((256, 384), BF),
        pltpu.VMEM((256, D), BF),
        pltpu.VMEM((ROWS, 256), BF),
        pltpu.VMEM((ROWS, 128), F32),
        pltpu.VMEM((LENGTH, 128), F32),
        pltpu.VMEM((2, ROWS, 128), BF),
        pltpu.VMEM((2, ROWS, 128), BF),
        pltpu.VMEM((BLOCKS, 2 * HEAD_DIM, WIDE), BF),
        pltpu.VMEM((BLOCKS, 1, WIDE), F32),
        pltpu.VMEM((BLOCKS, 2 * HEAD_DIM, WIDE), F32),
    ]
    scratch += TOKEN_SCATTER_SEMS * 3 + GRAD_SCATTER_SEMS * 2 + TOKEN_GATHER_SEMS
    scratch += [DMA((2,)), DMA((2,)), DMA, DMA((4,))] + [DMA] * 7 + DEAL_SEMS * 2
    input_grad, block_out, m_dealt, a_dealt, _ = call(
        backward_kernel,
        4,
        "backward_exchange",
        args,
        [VMEM] * 17 + [HBM] * 3,
        outs,
        [HBM] * 5,
        scratch,
    )
    return input_grad.reshape(2 * HALF, D), block_out.reshape(2 * HALF, D), m_dealt, a_dealt


def rope_frequency():
    base_freq = 500000.0 ** (-(np.arange(HEAD_DIM // 2) * 2.0 / HEAD_DIM))
    wavelength = 2.0 * math.pi / base_freq
    smooth = (8192.0 / wavelength - 1.0) / 3.0
    blended = (1.0 - smooth) * base_freq / 32.0 + smooth * base_freq
    frequency = np.where(
        wavelength < 2048.0, base_freq, np.where(wavelength > 8192.0, base_freq / 32.0, blended)
    )
    return np.repeat(frequency.astype(np.float32)[:, None], 128, axis=1)


def swap_cores(x):
    return lax.ppermute(x, "t", [(0, 1), (1, 0)])


def adamw(weight, first_moment, second_moment, gradient, step_rate):
    first_new = 0.9 * first_moment + 0.1 * gradient
    second_new = 0.95 * second_moment + 0.05 * gradient * gradient
    corrected = first_new / (1.0 - 0.9**STEP) / (jnp.sqrt(second_new / (1.0 - 0.95**STEP)) + 1e-08)
    return (first_new, second_new, weight - step_rate * (corrected + 0.1 * weight))


def slots(w, columns):
    return w.reshape(w.shape[0], -1, columns).transpose(1, 0, 2)


def unslots(g):
    return g.transpose(1, 0, 2).reshape(g.shape[1], -1)


def body(
    tokens,
    segments,
    cotangent,
    query_weight,
    key_weight,
    value_weight,
    output_weight,
    gate_weight,
    up_weight,
    down_weight,
    norm_gain_pair,
    query_first,
    key_first,
    value_first,
    output_first,
    gate_first,
    up_first,
    down_first,
    gains_first,
    query_second,
    key_second,
    value_second,
    output_second,
    gate_second,
    up_second,
    down_second,
    gains_second,
):
    gains = norm_gain_pair.astype(BF).astype(F32)
    gain_a, gain_m = gains[0][:, None], gains[1][:, None]
    low = lambda w: w.astype(BF).astype(F32)
    (
        resid,
        all_m,
        all_g,
        w_gate_up,
        w_down,
        kv,
        kvt,
        o_full,
        lse,
        o_low,
        all_a,
        w_qkv,
        w_out,
        q_wide,
        tables,
        starts,
        g_gate_up,
        act,
    ) = forward_exchange(
        tokens[0],
        segments,
        jnp.broadcast_to(gains[:, :, None], (2, 32, 128)),
        jnp.asarray(rope_frequency()),
        query_weight,
        key_weight,
        value_weight,
        output_weight.T,
        cotangent[0],
        gate_weight,
        up_weight,
        down_weight.T,
    )
    input_grad, block_out, mlp_dealt, attn_dealt = backward_exchange(
        g_gate_up,
        act,
        w_gate_up,
        w_down,
        resid,
        cotangent[0],
        w_out,
        q_wide,
        kv,
        kvt,
        starts,
        o_full,
        lse,
        o_low,
        tables,
        w_qkv,
        tokens[0],
        all_m,
        all_g,
        all_a,
    )
    mlp_sum, attn_sum = mlp_dealt.astype(F32), attn_dealt.astype(F32)

    pairs = lambda g: unslots(g.reshape(4, 2, 32, HEAD_DIM).sum(axis=1))
    q_sum = unslots(attn_sum[:, :, :128])
    k_sum = pairs(attn_sum[:, :, 128:192])
    v_sum = pairs(attn_sum[:, :, 192:256])
    gate_sum = unslots(mlp_sum[:, :, :512])
    up_sum = unslots(mlp_sum[:, :, 512:1024])
    dots = lambda g, w: jnp.sum(g * low(w), axis=1)
    gains_half = jnp.stack(
        [
            dots(q_sum, query_weight) + dots(k_sum, key_weight) + dots(v_sum, value_weight),
            dots(gate_sum, gate_weight) + dots(up_sum, up_weight),
        ],
        axis=0,
    )
    gains_grad = gains_half + swap_cores(gains_half)
    query_grad, key_grad, value_grad = gain_a * q_sum, gain_a * k_sum, gain_a * v_sum
    gate_grad, up_grad = gain_m * gate_sum, gain_m * up_sum
    output_grad = unslots(attn_sum[:, :, 256:]).T
    down_grad = unslots(mlp_sum[:, :, 1024:]).T
    wide_rate = 2.0 * D ** (-0.5)
    outs = [block_out[None], input_grad[None]]
    for weight, first, second, grad, rate in (
        (query_weight, query_first, query_second, query_grad, wide_rate),
        (key_weight, key_first, key_second, key_grad, wide_rate),
        (value_weight, value_first, value_second, value_grad, wide_rate),
        (output_weight, output_first, output_second, output_grad, 2.0 * (4 * HEAD_DIM) ** (-0.5)),
        (gate_weight, gate_first, gate_second, gate_grad, wide_rate),
        (up_weight, up_first, up_second, up_grad, wide_rate),
        (down_weight, down_first, down_second, down_grad, 2.0 * FF ** (-0.5)),
        (norm_gain_pair, gains_first, gains_second, gains_grad, 1.5),
    ):
        outs.append(grad)
        outs.extend(adamw(weight, first, second, grad, rate))
    return tuple(outs)


def solution(mesh):
    split = Mesh(
        mesh.devices.reshape(tuple(SIZES.values())), tuple(SIZES)
    )
    heads = ("x", "z", "yl")
    every = ("dp", "x", "z", "yl")
    acts = P("dp", heads, None)
    rows_cut = P(every, "t")
    columns_cut = P("t", every)
    gains = P(None, every)
    weights = (rows_cut,) * 3 + (columns_cut,) + (rows_cut,) * 2 + (columns_cut, gains)
    in_specs = (acts, P("dp", heads), acts) + weights * 3
    out_specs = (acts, acts) + tuple(spec for spec in weights for _ in range(4))
    return jax.shard_map(
        body, mesh=split, in_specs=in_specs, out_specs=out_specs, check_vma=False
    )
```

```python
import functools
import itertools
import math

import jax
import jax.numpy as jnp
import numpy as np
from jax import lax
from jax.experimental import pallas as pl
from jax.experimental.pallas import tpu as pltpu
from jax.sharding import Mesh
from jax.sharding import PartitionSpec as P

D = 2048
FF = 8192
HEADS = 32
KV_HEADS = 8
HEAD_DIM = 64
STEP = 10
EPS = 1e-05

SIZES = {"dp": 2, "x": 4, "z": 4, "yl": 2, "t": 2}
GROUP = ("z", "yl")
CROSS = ("dp", "x")
MEMBERS = 8
HALF = 64
ROWS = 1024
LENGTH = 4096
DOC_MOST = 2048
DOCS = 10
QB = 256
KB = 512
BLOCKS = ROWS // QB
WIDE = 2 * QB
BF = jnp.bfloat16
F32 = jnp.float32


def shifts(axes):
    return list(itertools.product(*[range(SIZES[a]) for a in axes]))


def place(axes, shift, sign=1):
    index = 0
    for a, s in zip(axes, shift):
        index = index * SIZES[a] + lax.rem(
            lax.axis_index(a) + (s if sign > 0 else SIZES[a] - s), SIZES[a]
        )
    return index


def peer(axes, shift):
    return {
        a: lax.rem(lax.axis_index(a) + s, SIZES[a]) for a, s in zip(axes, shift) if s
    }


def other_core():
    return {"t": 1 - lax.axis_index("t")}


def hail(devices):
    for device in devices:
        pl.semaphore_signal(
            pltpu.get_barrier_semaphore(),
            inc=1,
            device_id=device,
            device_id_type=pl.DeviceIdType.MESH,
        )


def await_all(devices):
    pl.semaphore_wait(pltpu.get_barrier_semaphore(), len(devices))


def greet(devices):
    hail(devices)
    await_all(devices)


def remote(src, dst, send, recv, device):
    return pltpu.make_async_remote_copy(
        src_ref=src,
        dst_ref=dst,
        send_sem=send,
        recv_sem=recv,
        device_id=device,
        device_id_type=pl.DeviceIdType.MESH,
    )


def abt(left, right):
    return lax.dot_general(left, right, (((1,), (1,)), ((), ())), preferred_element_type=F32)


def atb(left, right):
    return lax.dot_general(left, right, (((0,), (0,)), ((), ())), preferred_element_type=F32)


DMA = pltpu.SemaphoreType.DMA
HBM = pl.BlockSpec(memory_space=pl.ANY)
VMEM = pl.BlockSpec(memory_space=pltpu.VMEM)
MOVES = shifts(GROUP)[1:]
TURNS = (1, 3, 2)


def members():
    return [other_core()] + [peer(GROUP, s) for s in MOVES]


def across():
    return [peer(("dp",), (1,))] + [peer(("x",), (s,)) for s in TURNS]


def finish(copies):
    for c in copies:
        c.wait()


INSIDE = ("yl", "z")
ACROSS = ("dp", "x")


def ring_places(axes):
    pair, ring = axes
    p, q = lax.axis_index(pair), lax.axis_index(ring)
    mate, up, down = {pair: 1 - p}, {ring: lax.rem(q + 1, 4)}, {ring: lax.rem(q + 3, 4)}
    return p, q, mate, up, down


RING_GATHER_SEMS = [DMA((9,)), DMA((9,)), DMA]


class RingGather:
    def __init__(self, x_ref, slot, rows, axes, sems, arrived=None):
        self.x_ref, self.slot, self.half, self.axes = x_ref, slot, rows // 2, axes
        self.ssem, self.rsem, self.local = sems
        self.copies = {}
        self.arrived = arrived if arrived is not None else lambda part: None
        p, q, mate, up, down = ring_places(axes)
        self.own = pltpu.make_async_copy(x_ref, slot(p, q), self.local)
        self.own.start()
        for k, to in enumerate((mate, up, down)):
            self.go(k, x_ref, slot(p, q), to)

    def go(self, k, src, dst, to):
        c = remote(src, dst, self.ssem.at[k], self.rsem.at[k], to)
        c.start()
        self.copies[k] = c

    def part(self, p, q, which=None):
        ref = self.slot(p, q)
        return ref if which is None else ref.at[pl.ds(which * self.half, self.half)]

    def wait_own(self):
        if self.own is not None:
            self.own.wait()
            self.own = None

    def pass_mate(self):
        p, q, _, up, down = ring_places(self.axes)
        self.copies[0].wait_recv()
        part = self.part(1 - p, q)
        self.go(3, part, part, up)
        self.go(4, part, part, down)
        self.arrived(part)

    def pass_ring(self, column):
        p, q, _, up, down = ring_places(self.axes)
        p = p if column == 0 else 1 - p
        at = 1 if column == 0 else 3
        for i, (step, to) in enumerate(((3, up), (1, down))):
            self.copies[at + i].wait_recv()
            there = lax.rem(q + step, 4)
            part = self.part(p, there, i)
            self.go(5 + 2 * column + i, part, part, to)
            self.arrived(self.part(p, there))

    def finish(self):
        p, q, _, _, _ = ring_places(self.axes)
        far = lax.rem(q + 2, 4)
        for column, p in enumerate((p, 1 - p)):
            for i in range(2):
                self.copies[5 + 2 * column + i].wait_recv()
            self.arrived(self.part(p, far))
        self.wait_own()
        for c in self.copies.values():
            c.wait_send()


TOKEN_GATHER_SEMS = RING_GATHER_SEMS + [DMA((8,)), DMA((8,))]


class TokenGather(RingGather):
    def __init__(self, x_ref, out_ref, sems):
        t = lax.axis_index("t")
        self.passed, self.had, self.tsend, self.trecv = [], set(), sems[3], sems[4]
        slot = lambda p, q: out_ref.at[2 * q + p, t]
        super().__init__(x_ref, slot, HALF, INSIDE, sems[:3], self.to_core)
        p, q, _, _, _ = ring_places(INSIDE)
        self.to_core(slot(p, q), x_ref)

    def to_core(self, part, src=None):
        k = len(self.passed)
        c = remote(part if src is None else src, part, self.tsend.at[k], self.trecv.at[k], other_core())
        c.start()
        self.passed.append(c)

    def have(self, *ks):
        for k in ks:
            if k not in self.had:
                self.passed[k].wait_recv()
                self.had.add(k)

    def finish(self):
        super().finish()
        self.have(*range(8))
        for c in self.passed:
            c.wait_send()


def add_rows(out_ref, terms, rows, step_rows):
    def step(r, carry):
        at = pl.ds(pl.multiple_of(r * step_rows, step_rows), step_rows)
        total = terms[0][at, :].astype(F32)
        for term in terms[1:]:
            total = total + term[at, :].astype(F32)
        out_ref[at, :] = total.astype(out_ref.dtype)
        return carry

    lax.fori_loop(0, rows // step_rows, step, 0)


RING_SCATTER_SEMS = [DMA((13,)), DMA((13,))]


def ring_scatter_slots(rows, wide):
    half = rows // 2
    return [
        pltpu.VMEM((2, half, wide), BF),
        pltpu.VMEM((2, half, wide), BF),
        pltpu.VMEM((2, rows, wide), BF),
        pltpu.VMEM((2, rows, wide), BF),
        pltpu.VMEM((rows, wide), BF),
    ]


class RingScatter:
    def __init__(self, rows, axes, slots, sems):
        self.rows, self.half, self.axes = rows, rows // 2, axes
        self.far_up, self.far_down, self.from_down, self.from_up, self.back = slots
        self.ssem, self.rsem = sems
        self.copies = {}

    def go(self, k, src, dst, to):
        c = remote(src, dst, self.ssem.at[k], self.rsem.at[k], to)
        c.start()
        self.copies[k] = c

    def part(self, p, q, at):
        return self.held(p, q).at[at]

    def halves(self):
        return pl.ds(0, self.half), pl.ds(self.half, self.half)

    def add(self, out_ref, terms, rows):
        add_rows(out_ref, terms, rows, 16)

    def send_far(self, p):
        _, _, _, up, down = ring_places(self.axes)
        first, second = self.halves()
        self.go(2 * p, self.part(p, 2, first), self.far_up.at[p], up)
        self.go(2 * p + 1, self.part(p, 2, second), self.far_down.at[p], down)

    def send_near(self, p):
        _, _, _, up, down = ring_places(self.axes)
        first, second = self.halves()
        self.go(4 + 2 * p, self.part(p, 1, second), self.from_down.at[p, second], up)
        self.go(5 + 2 * p, self.part(p, 3, first), self.from_up.at[p, first], down)

    def send_joined(self, p):
        _, _, _, up, down = ring_places(self.axes)
        first, second = self.halves()
        self.copies[2 * p].wait_recv()
        part = self.part(p, 1, first)
        self.add(part, [part, self.far_up.at[p]], self.half)
        self.go(8 + 2 * p, part, self.from_down.at[p, first], up)
        self.copies[2 * p + 1].wait_recv()
        part = self.part(p, 3, second)
        self.add(part, [part, self.far_down.at[p]], self.half)
        self.go(9 + 2 * p, part, self.from_up.at[p, second], down)

    def arrivals(self, p):
        for k in (4 + 2 * p, 5 + 2 * p, 8 + 2 * p, 9 + 2 * p):
            self.copies[k].wait_recv()

    def send_mate(self):
        _, _, mate, _, _ = ring_places(self.axes)
        self.arrivals(1)
        part = self.held(1, 0)
        self.add(part, [part, self.from_down.at[1], self.from_up.at[1]], self.rows)
        self.go(12, part, self.back, mate)

    def total(self, out_ref):
        self.arrivals(0)
        self.copies[12].wait_recv()
        self.add(
            out_ref,
            [self.held(0, 0), self.from_down.at[0], self.from_up.at[0], self.back],
            self.rows,
        )
        for c in self.copies.values():
            c.wait_send()


TOKEN_SCATTER_SEMS = RING_SCATTER_SEMS + [DMA((4, 2)), DMA((4, 2))]


def token_scatter_slots():
    return ring_scatter_slots(HALF, D) + [pltpu.VMEM((4, 2, HALF, D), BF)]


STAGE = pltpu.VMEM((4, 2, 2, HALF, D), BF)


class TokenScatter(RingScatter):
    def __init__(self, a_ref, w_ref, slots, stage, sems):
        super().__init__(HALF, INSIDE, slots[:5], sems[:2])
        self.a_ref, self.w_ref = a_ref, w_ref
        self.stage, self.theirs = stage, slots[5]
        self.tsend, self.trecv = sems[2:]
        self.swaps = {}

    def pair_place(self, p):
        own = lax.axis_index("yl")
        return own if p == 0 else 1 - own

    def held(self, p, q):
        return self.stage.at[q, self.pair_place(p), lax.axis_index("t")]

    def make(self, q):
        row = lax.rem(lax.axis_index("z") + q, 4) * 256
        a = self.a_ref[pl.ds(pl.multiple_of(row, 256), 256), :]

        def step(n, carry):
            at = pl.ds(pl.multiple_of(n * 512, 512), 512)
            product = abt(a, self.w_ref[at, :]).astype(BF)
            self.stage[q, :, :, :, at] = product.reshape(2, 2, HALF, 512)
            return carry

        lax.fori_loop(0, D // 512, step, 0)

    def swap(self, q):
        t = lax.axis_index("t")
        for p in (1, 0):
            at = self.pair_place(p)
            c = remote(
                self.stage.at[q, at, 1 - t],
                self.theirs.at[q, at],
                self.tsend.at[q, p],
                self.trecv.at[q, p],
                other_core(),
            )
            c.start()
            self.swaps[q, p] = c

    def pair(self, p, q):
        self.swaps[q, p].wait_recv()
        part = self.held(p, q)
        self.add(part, [part, self.theirs.at[q, self.pair_place(p)]], HALF)

    def total(self, out_ref):
        super().total(out_ref)
        for c in self.swaps.values():
            c.wait_send()

    def pair_ring(self, q):
        self.pair(1, q)
        self.pair(0, q)

    def fill(self, *qs):
        for q in qs:
            self.make(q)
            self.swap(q)


BY_NEED = [(1, 2), (0, 2), (1, 1), (1, 3), (0, 1), (0, 3), (1, 0), (0, 0)]


def grad_scatter_slots(wide):
    return ring_scatter_slots(256, wide) + [pltpu.VMEM((2, 4, 256, wide), BF)]


COLUMNS = pltpu.VMEM((2, 2, ROWS, 256), BF)


class GradScatter(RingScatter):
    def __init__(self, pairs, slots, columns, sems):
        super().__init__(256, ACROSS, slots[:5], sems[:2])
        self.pairs, self.blocks, self.columns, self.lsem = pairs, slots[5], columns, sems[2]
        self.loads = {}
        self.done = 0
        self.load(0)
        self.load(1)

    def held(self, p, q):
        return self.blocks.at[p, q]

    def load(self, k):
        p, q = BY_NEED[k]
        dp, x = lax.axis_index("dp"), lax.axis_index("x")
        row = (dp if p == 0 else 1 - dp) * 4 + lax.rem(x + q, 4)
        at = pl.ds(pl.multiple_of(row * 256, 256), 256)
        for i, (x_ref, _) in enumerate(self.pairs):
            c = pltpu.make_async_copy(
                x_ref.at[:, at], self.columns.at[k % 2, i], self.lsem.at[k % 2, i]
            )
            c.start()
            self.loads[k, i] = c

    def make(self):
        k = self.done
        p, q = BY_NEED[k]
        start = 0
        for i, (_, g_ref) in enumerate(self.pairs):
            self.loads[k, i].wait()
            wide = g_ref.shape[1]
            self.blocks[p, q, :, start : start + wide] = atb(
                self.columns[k % 2, i], g_ref[...]
            ).astype(BF)
            start += wide
        self.done = k + 1
        if k + 2 < len(BY_NEED):
            self.load(k + 2)

def both(method):
    method(1)
    method(0)


def scatter_both(sums, grads, devices=None):
    sums.make(2)
    if devices is not None:
        await_all(devices)
    sums.swap(2)
    grads.make()
    grads.send_far(1)
    sums.pair(1, 2)
    sums.send_far(1)
    sums.pair(0, 2)
    sums.send_far(0)
    sums.fill(1, 3)
    sums.pair(1, 1)
    sums.pair(1, 3)
    sums.send_near(1)
    sums.send_joined(1)
    grads.make()
    grads.send_far(0)
    sums.pair(0, 1)
    sums.pair(0, 3)
    sums.send_near(0)
    sums.fill(0)
    sums.send_joined(0)
    grads.make()
    grads.make()
    grads.send_near(1)
    sums.pair_ring(0)
    sums.send_mate()
    grads.send_joined(1)
    grads.make()
    grads.make()
    grads.send_near(0)
    grads.make()
    grads.make()


GRAD_SCATTER_SEMS = RING_SCATTER_SEMS + [DMA((2, 2))]


def weight_gather(x_ref, out_ref, sems):
    return RingGather(x_ref, lambda p, q: out_ref.at[p, q], 256, ACROSS, sems)


DEAL_SEMS = [DMA((7,)), DMA((7,)), DMA]


def deal_start(x_ref, out_ref, sems):
    send, recv, local = sems
    me = place(GROUP, (0, 0))
    own = pltpu.make_async_copy(x_ref.at[me], out_ref.at[me], local)
    own.start()
    copies = []
    for i, s in enumerate(MOVES):
        c = remote(
            x_ref.at[place(GROUP, s)], out_ref.at[me], send.at[i], recv.at[i], peer(GROUP, s)
        )
        c.start()
        copies.append(c)
    return [own] + copies


def deal_columns(x_ref, out_ref, at, wide, sems):
    send, recv, local = sems
    me = place(GROUP, (0, 0))
    slot = lambda c: x_ref.at[:, pl.ds(pl.multiple_of(c * wide, wide), wide)]
    there = out_ref.at[me, :, pl.ds(at, wide)]
    own = pltpu.make_async_copy(slot(me), there, local)
    own.start()
    copies = []
    for i, s in enumerate(MOVES):
        c = remote(slot(place(GROUP, s)), there, send.at[i], recv.at[i], peer(GROUP, s))
        c.start()
        copies.append(c)
    return [own] + copies


def own_half(ref):
    return pl.ds(pl.multiple_of(lax.axis_index("t") * HALF, HALF), HALF)


def fold(gain, weight):
    return (gain * weight.astype(BF).astype(F32)).astype(BF)


def split(refs, *counts):
    parts, at = [], 0
    for count in counts:
        parts.append(refs[at : at + count])
        at += count
    assert at == len(refs)
    return parts


def scale_rows(x):
    return lax.rsqrt(jnp.mean(x * x, axis=1, keepdims=True) + EPS)


def norm_back(unit, inverse, grad):
    return inverse * (grad - unit * jnp.mean(grad * unit, axis=1, keepdims=True))


def call(kernel, collective_id, name, args, in_specs, outs, out_specs, scratch):
    sent = 60_000_000
    return pl.pallas_call(
        kernel,
        out_shape=[jax.ShapeDtypeStruct(s, d) for s, d in outs],
        in_specs=in_specs,
        out_specs=out_specs,
        scratch_shapes=scratch,
        compiler_params=pltpu.CompilerParams(
            collective_id=collective_id, has_side_effects=True, vmem_limit_bytes=60 * 2**20
        ),
        cost_estimate=pl.CostEstimate(flops=0, bytes_accessed=sent, transcendentals=0),
        name=name,
    )(*args)


def turn_back(v, cos_tab, sin_tab):
    a, b = v[: HEAD_DIM // 2], v[HEAD_DIM // 2 :]
    return jnp.concatenate([a * cos_tab + b * sin_tab, b * cos_tab - a * sin_tab], axis=0)


def key_blocks(b, rel):
    x = lax.axis_index("x")
    first = x * ROWS + b * QB
    chunk = (x - rel) * (ROWS // KB)
    low = lax.max(lax.max(first - (DOC_MOST - 1), 0) // KB, chunk)
    high = lax.min((first + QB + KB - 1) // KB, chunk + ROWS // KB)
    return low, high


def mask_scores(s, base, start, b, rel):
    key = base + lax.broadcasted_iota(jnp.int32, s.shape, 0)
    allowed = key >= start
    if rel == 0:
        first = lax.axis_index("x") * ROWS + b * QB
        own = first + lax.broadcasted_iota(jnp.int32, (1, QB), 1)
        allowed = allowed & (key <= jnp.concatenate([own, own], axis=1))
    return jnp.where(allowed, s, -1e30)


def block_lanes(b):
    return pl.ds(pl.multiple_of(b * QB, QB), QB)


def beside_lanes(ref, b):
    at = block_lanes(b)
    return jnp.concatenate([ref[0, :, at], ref[1, :, at]], axis=1)


def twice_lanes(ref, b):
    v = ref[:, block_lanes(b)]
    return jnp.concatenate([v, v], axis=1)


def attend_part(q_ref, kv_ref, kvt_ref, start_ref, top_ref, total_ref, acc_ref, b, rel):
    q, start = beside_lanes(q_ref, b), twice_lanes(start_ref, b)

    def step(j, carry):
        top, total, acc = carry
        base = pl.multiple_of(j * KB, KB)
        s = jnp.dot(kv_ref[pl.ds(base, KB), :], q, preferred_element_type=F32)
        s = mask_scores(s, base, start, b, rel)
        new_top = jnp.maximum(top, jnp.max(s, axis=0, keepdims=True))
        p = jnp.exp(s - new_top)
        fade = jnp.exp(top - new_top)
        total = total * fade + jnp.sum(p, axis=0, keepdims=True)
        acc = acc * fade + jnp.dot(
            kvt_ref[:, pl.ds(base, KB)], p.astype(BF), preferred_element_type=F32
        )
        return (new_top, total, acc)

    if rel == 0:
        init = (
            jnp.full((1, WIDE), -1e30, F32),
            jnp.zeros((1, WIDE), F32),
            jnp.zeros((2 * HEAD_DIM, WIDE), F32),
        )
    else:
        init = (top_ref[b], total_ref[b], acc_ref[b])
    low, high = key_blocks(b, rel)
    top_ref[b], total_ref[b], acc_ref[b] = lax.fori_loop(low, high, step, init)


def attend_end(top_ref, total_ref, acc_ref, o_ref, lse_ref, low_ref, b):
    at = block_lanes(b)
    total = total_ref[b]
    o = acc_ref[b][HEAD_DIM:] / total
    lse = top_ref[b] + jnp.log(total)
    for h in range(2):
        o_ref[h, :, at] = o[:, h * QB : (h + 1) * QB]
        lse_ref[h : h + 1, at] = lse[:, h * QB : (h + 1) * QB]
    beside = jnp.concatenate([o[:, :QB], o[:, QB:]], axis=0)
    low_ref[at, :] = beside.T.astype(BF)


def start_block(all_ref, chunk, sems, b):
    pieces = []
    for c in range(2):
        for core in range(2):
            at = pl.ds((2 * c + core) * HALF, HALF)
            copy = pltpu.make_async_copy(
                all_ref.at[2 * b + c, core], chunk.at[at], sems.at[2 * c + core]
            )
            copy.start()
            pieces.append(copy)
    return pieces


def load_block(all_ref, chunk, sems, b):
    finish(start_block(all_ref, chunk, sems, b))


def document_starts(seg_ref):
    every = seg_ref[...].reshape(LENGTH * 8 // 128, 128)
    x = lax.axis_index("x")
    own = jnp.concatenate([seg_ref[x, g, 0:1, :] for g in range(MEMBERS)], axis=1)
    starts = jnp.zeros((1, ROWS), F32)
    for d in range(DOCS - 1):
        same = jnp.where(every == d, 1.0, 0.0)
        count = jnp.sum(jnp.sum(same, axis=0, keepdims=True), axis=1, keepdims=True) * 0.125
        starts = starts + jnp.where(own > d, count, 0.0)
    return starts.astype(jnp.int32)


def forward_kernel(*refs):
    ins, outs, slots, others, sems, gather, rings, keys, deals, seg_sems, lsems = split(
        refs, 12, 19, 6, 22, 4, 15, 12, 3, 15, 5, 3
    )
    (
        tokens_ref, seg_ref, gains_ref, freq_ref, wq_ref, wk_ref, wv_ref, wo_ref, cot_ref,
        gate_ref, up_ref, down_ref,
    ) = ins
    (
        resid_ref, all_m, all_g, w_gu, w_down, kv_ref, kvt_ref, o_ref, lse_ref, low_ref,
        all_a, w_qkv, w_out, w_out_turned, q_ref, tables, start_ref, g_ref, act_ref,
    ) = outs
    (
        stage, total, unit, gu_part, down_part, *states, qkv_part, wo_part, seg_all, w_turned,
        chunk, qkv_slots, wo_slots, seg_own, raw, gate_low, up_low, down_low, unit_a, pairs,
    ) = others
    cos_ref, sin_ref = tables.at[0], tables.at[1]
    ksend, krecv, klocal = keys
    ssend, srecv, xsend, xrecv, slocal = seg_sems
    devices = members() + across()
    hail(devices)
    fetches = []
    for i, ref in enumerate((gate_ref, up_ref, down_ref)):
        c = pltpu.make_async_copy(ref, raw.at[i], lsems[1].at[i])
        c.start()
        fetches.append(c)
    x, z = lax.axis_index("x"), lax.axis_index("z")
    me = place(GROUP, (0, 0))
    gain_a, gain_m = gains_ref[0][:, 0:1], gains_ref[1][:, 0:1]
    wq, wk, wv = (fold(gain_a, ref[...]) for ref in (wq_ref, wk_ref, wv_ref))
    wo = wo_ref[...].astype(BF)
    for c in range(MEMBERS):
        head = slice(c // 2 * HEAD_DIM, (c // 2 + 1) * HEAD_DIM)
        qkv_slots[c] = jnp.concatenate(
            [wq[:, c * 128 : (c + 1) * 128], wk[:, head], wv[:, head]], axis=1
        )
        wo_slots[c] = wo[:, c * 128 : (c + 1) * 128]
    rows = tokens_ref[own_half(tokens_ref), :].astype(F32)
    unit_a[...] = (rows * scale_rows(rows)).astype(BF)
    seg_own[...] = jnp.broadcast_to(seg_ref[...], (8, 128))
    await_all(devices)

    early = deal_start(qkv_slots, qkv_part, deals[9:12]) + deal_start(wo_slots, wo_part, deals[12:])
    tokens = TokenGather(unit_a, all_a, gather[10:])
    seg_copies = [pltpu.make_async_copy(seg_own, seg_all.at[x, me], slocal)]
    seg_copies[0].start()
    for i, s in enumerate(MOVES):
        c = remote(seg_own, seg_all.at[x, me], ssend.at[i], srecv.at[i], peer(GROUP, s))
        c.start()
        seg_copies.append(c)
    finish(early)
    qkv_weights = weight_gather(qkv_part.reshape(256, 256), w_qkv, rings[6:9])
    out_weights = weight_gather(wo_part.reshape(256, 128), w_out, rings[9:])
    finish(seg_copies)
    crossed = []
    for i, to in enumerate(across()[1:]):
        c = remote(seg_all.at[x], seg_all.at[x], xsend.at[i], xrecv.at[i], to)
        c.start()
        crossed.append(c)
    everything = [tokens, qkv_weights]
    for g in everything:
        g.pass_mate()
    for g in everything:
        g.pass_ring(0)
    finish(crossed)
    starts = document_starts(seg_all)
    start_ref[...] = starts
    own = x * ROWS + lax.broadcasted_iota(jnp.int32, (1, ROWS), 1)
    angles = freq_ref[:, 0:1] * (own - starts).astype(F32)
    cos_ref[...] = jnp.cos(angles)
    sin_ref[...] = jnp.sin(angles)
    for c in fetches:
        c.wait()
    gate_low[...] = fold(gain_m, raw[0])
    up_low[...] = fold(gain_m, raw[1])
    down_low[...] = raw[2].astype(BF)
    for g in everything:
        g.pass_ring(1)
    dealt = deal_columns(gate_low, gu_part, 0, 512, deals[:3])
    dealt += deal_columns(up_low, gu_part, 512, 512, deals[3:6])
    dealt += deal_columns(down_low, down_part, 0, 512, deals[6:9])
    out_weights.pass_mate()
    out_weights.pass_ring(0)
    out_weights.pass_ring(1)
    qkv_weights.finish()
    for r in range(8):
        w_turned[:, r * 256 : (r + 1) * 256] = w_qkv[r // 4, r % 4].T
    key_copies = ([], [])

    def project(b):
        load_block(all_a, chunk, lsems[0], b)
        qkv = abt(w_turned[...], chunk[...])
        at = block_lanes(b)
        c, s = cos_ref[:, at], -sin_ref[:, at]
        zeros = jnp.zeros((HEAD_DIM, QB), BF)
        for h in range(2):
            q = turn_back(qkv[h * HEAD_DIM : (h + 1) * HEAD_DIM], c, s)
            q_ref[h, :, at] = jnp.concatenate([(q * HEAD_DIM ** (-0.5)).astype(BF), zeros], axis=0)
        k = turn_back(qkv[128:192], c, s)
        kv = jnp.concatenate([k, qkv[192:]], axis=0)
        here = pl.ds(pl.multiple_of(x * ROWS + b * QB, QB), QB)
        kvt_ref[:, here] = kv.astype(BF)
        kv_ref[here, :] = kv.T.astype(BF)
        k = len(key_copies[0])
        for i in range(2):
            there = kv_ref.at[here]
            c = remote(there, there, ksend.at[i, k], krecv.at[i, k], peer(("x",), (i + 1,)))
            c.start()
            key_copies[i].append(c)

    tokens.wait_own()
    tokens.have(0, 1)
    project(z)
    tokens.have(2, 4)
    project(lax.rem(z + 3, 4))
    tokens.have(3, 5)
    project(lax.rem(z + 1, 4))
    tokens.finish()
    project(lax.rem(z + 2, 4))

    cots = TokenGather(cot_ref.at[own_half(cot_ref)], all_g, gather[:5])

    def turn(rel):
        base = lax.rem(x + 4 - rel, 4) * ROWS
        for c in range(ROWS // KB):
            at = pl.ds(pl.multiple_of(base + c * KB, KB), KB)
            kvt_ref[:, at] = kv_ref[at, :].T

    def part(b, rel):
        attend_part(q_ref, kv_ref, kvt_ref, start_ref, *states, b, rel)

    for b in range(BLOCKS):
        part(b, 0)
    for c in key_copies[0]:
        c.wait_recv()
    turn(1)
    for b in range(BLOCKS):
        part(b, 1)
    finish(dealt)
    cots.pass_mate()
    for c in key_copies[1]:
        c.wait_recv()
    for c in key_copies[0] + key_copies[1]:
        c.wait_send()
    weights = [
        weight_gather(gu_part.reshape(256, 1024), w_gu, rings[:3]),
        weight_gather(down_part.reshape(256, 512), w_down, rings[3:6]),
    ]
    turn(2)
    out_weights.finish()
    sums = TokenScatter(low_ref, w_out.reshape(D, 128), slots, stage, sems)

    def attend(q):
        b = lax.rem(z + q, 4)
        part(b, 2)
        attend_end(*states, o_ref, lse_ref, low_ref, b)
        sums.make(q)
        sums.swap(q)

    attend(2)
    attend(1)
    sums.pair(1, 2)
    sums.send_far(1)
    sums.pair(0, 2)
    sums.send_far(0)
    attend(3)
    for p in (1, 0):
        sums.pair(p, 1)
        sums.pair(p, 3)
        sums.send_near(p)
        sums.send_joined(p)
    attend(0)
    sums.pair_ring(0)
    for g in weights:
        g.pass_mate()
    sums.send_mate()
    cots.pass_ring(0)
    for g in weights:
        g.pass_ring(0)
    cots.pass_ring(1)
    sums.total(total)
    resid = tokens_ref[own_half(tokens_ref), :].astype(F32) + total[...]
    resid_ref[...] = resid
    unit[...] = (resid * scale_rows(resid)).astype(BF)
    tokens = TokenGather(unit, all_m, gather[5:10])
    tokens.pass_mate()
    for g in weights:
        g.pass_ring(1)
    tokens.pass_ring(0)
    tokens.pass_ring(1)
    for r in range(8):
        w_out_turned[:, r * 256 : (r + 1) * 256] = w_out[r // 4, r % 4].T
    cots.finish()
    tokens.finish()
    order = [lax.rem(z + q, 4) for q in (0, 3, 1, 2)]
    blocks = {}

    def fetch(k):
        for i, ref in enumerate((all_m, all_g)):
            blocks[k, i] = start_block(ref, pairs.at[k % 2, i], lsems[2].at[k % 2, i], order[k])

    fetch(0)
    fetch(1)
    for g in weights:
        g.finish()
    w_gate_up, w_act = w_gu.reshape(D, 1024), w_down.reshape(D, 512)
    for k in range(BLOCKS):
        finish(blocks[k, 0] + blocks[k, 1])
        at = block_lanes(order[k])
        gate_up = jnp.dot(pairs[k % 2, 0], w_gate_up[...], preferred_element_type=F32)
        g_act = jnp.dot(pairs[k % 2, 1], w_act[...], preferred_element_type=F32)
        gate, up = gate_up[:, :512], gate_up[:, 512:]
        sig = 1.0 / (1.0 + jnp.exp(-gate))
        silu = gate * sig
        act_ref[at, :] = (silu * up).astype(BF)
        g_gate = g_act * up * sig * (1.0 + gate * (1.0 - sig))
        g_ref[at, :512] = g_gate.astype(BF)
        g_ref[at, 512:] = (g_act * silu).astype(BF)
        if k + 2 < BLOCKS:
            fetch(k + 2)


def forward_exchange(*args):
    slots = (MEMBERS, 2, HALF, D)
    outs = [
        ((HALF, D), F32),
        (slots, BF),
        (slots, BF),
        ((2, 4, 256, 1024), BF),
        ((2, 4, 256, 512), BF),
        ((LENGTH, 128), BF),
        ((128, LENGTH), BF),
        ((2, HEAD_DIM, ROWS), F32),
        ((2, ROWS), F32),
        ((ROWS, 128), BF),
        (slots, BF),
        ((2, 4, 256, 256), BF),
        ((2, 4, 256, 128), BF),
        ((128, D), BF),
        ((2, 128, ROWS), BF),
        ((2, HEAD_DIM // 2, ROWS), F32),
        ((1, ROWS), jnp.int32),
        ((ROWS, 1024), BF),
        ((ROWS, 512), BF),
    ]
    scratch = token_scatter_slots() + [
        STAGE,
        pltpu.VMEM((HALF, D), F32),
        pltpu.VMEM((HALF, D), BF),
        pltpu.VMEM((MEMBERS, 32, 1024), BF),
        pltpu.VMEM((MEMBERS, 32, 512), BF),
        pltpu.VMEM((BLOCKS, 1, WIDE), F32),
        pltpu.VMEM((BLOCKS, 1, WIDE), F32),
        pltpu.VMEM((BLOCKS, 2 * HEAD_DIM, WIDE), F32),
        pltpu.VMEM((MEMBERS, 32, 256), BF),
        pltpu.VMEM((MEMBERS, 32, 128), BF),
        pltpu.VMEM((4, MEMBERS, 8, 128), jnp.int32),
        pltpu.VMEM((256, D), BF),
        pltpu.VMEM((256, D), BF),
        pltpu.VMEM((MEMBERS, 32, 256), BF),
        pltpu.VMEM((MEMBERS, 32, 128), BF),
        pltpu.VMEM((8, 128), jnp.int32),
        pltpu.VMEM((3, 32, 4096), F32),
        pltpu.VMEM((32, 4096), BF),
        pltpu.VMEM((32, 4096), BF),
        pltpu.VMEM((32, 4096), BF),
        pltpu.VMEM((HALF, D), BF),
        pltpu.VMEM((2, 2, 256, D), BF),
    ]
    scratch += TOKEN_SCATTER_SEMS + TOKEN_GATHER_SEMS * 3 + RING_GATHER_SEMS * 4
    scratch += [DMA((2, 4)), DMA((2, 4)), DMA] + DEAL_SEMS * 5
    scratch += [DMA((7,)), DMA((7,)), DMA((3,)), DMA((3,)), DMA, DMA((4,)), DMA((3,))]
    scratch += [DMA((2, 2, 4))]
    (
        resid, all_m, all_g, w_gu, w_down, kv, kvt, o, lse, o_low, all_a, w_qkv, _, w_out, q,
        tables, starts, g_gate_up, act,
    ) = call(
        forward_kernel,
        1,
        "forward_exchange",
        args,
        [VMEM] * 8 + [HBM] * 4,
        outs,
        [VMEM] + [HBM] * 2 + [VMEM] * 7 + [HBM] + [VMEM] * 8,
        scratch,
    )
    return (
        resid,
        all_m.reshape(ROWS, D),
        all_g.reshape(ROWS, D),
        w_gu.reshape(D, 1024),
        w_down.reshape(D, 512),
        kv,
        kvt,
        o,
        lse,
        o_low,
        all_a.reshape(ROWS, D),
        w_qkv.reshape(D, 256),
        w_out,
        q,
        tables,
        starts,
        g_gate_up,
        act,
    )


def attend_back_part(q_ref, kv_ref, kvt_ref, start_ref, lse_ref, g_ref, dot_ref, dq_ref, acc_ref, b, rel):
    q, start, g, row_dot = beside_lanes(q_ref, b), twice_lanes(start_ref, b), g_ref[b], dot_ref[b]
    at = block_lanes(b)
    lse = jnp.concatenate([lse_ref[0:1, at], lse_ref[1:2, at]], axis=1)

    def step(j, dq):
        base = pl.multiple_of(j * KB, KB)
        kv = kv_ref[pl.ds(base, KB), :]
        s = jnp.dot(kv, q, preferred_element_type=F32)
        p = jnp.exp(mask_scores(s, base, start, b, rel) - lse)
        g_p = jnp.dot(kv, g, preferred_element_type=F32)
        g_s = (p * (g_p - row_dot)).astype(BF)
        acc_ref[pl.ds(base, KB), :] += abt(g_s, q) + abt(p.astype(BF), g)
        return dq + jnp.dot(kvt_ref[:, pl.ds(base, KB)], g_s, preferred_element_type=F32)

    low, high = key_blocks(b, rel)
    dq = jnp.zeros((2 * HEAD_DIM, WIDE), F32) if rel == 2 else dq_ref[b]
    dq_ref[b] = lax.fori_loop(low, high, step, dq)


def backward_kernel(*refs):
    ins, outs, slots, mids, others, keys, sems, gsems, gather, ksems, csems, deals = split(
        refs, 20, 5, 18, 12, 12, 6, 12, 6, 5, 4, 7, 6
    )
    (
        g_ref, act_ref, wgu_ref, wdown_ref, resid_ref, cot_ref, wot_ref, q_ref, kv_ref, kvt_ref,
        start_ref, o_ref, lse_ref, low_ref, tables, wqkv_ref, tokens_ref,
        all_m, all_g, all_a,
    ) = ins
    cos_ref, sin_ref = tables.at[0], tables.at[1]
    input_grad, block_out, m_dealt, a_dealt, all_r = outs
    stage, columns, total, grad, g_resid, low, out_low, m_sum, a_sum, chunk, g_qkv, key_sum = others
    acc_ref, key_low, key_land, gw_ref, dot_ref, dq_ref = keys
    devices = members() + across()
    hail(devices)
    t, x = lax.axis_index("t"), lax.axis_index("x")
    sums = TokenScatter(g_ref, wgu_ref, slots[:6], stage, sems[:4])
    grads = GradScatter([(all_m, g_ref), (all_g, act_ref)], mids[:6], columns, gsems[:3])
    scatter_both(sums, grads, devices)
    sums.total(total)
    resid = resid_ref[...]
    inverse = scale_rows(resid)
    back = cot_ref[own_half(cot_ref), :].astype(F32) + norm_back(resid * inverse, inverse, total[...])
    g_resid[...] = back
    low[...] = back.astype(BF)
    tokens = TokenGather(low, all_r, gather)

    downs = TokenScatter(act_ref, wdown_ref, slots[6:12], stage, sems[4:8])

    def lead(b):
        load_block(all_r, chunk, ksems[3], b)
        g = abt(wot_ref[...], chunk[...]).astype(BF)
        beside = jnp.concatenate([g[:HEAD_DIM], g[HEAD_DIM:]], axis=1)
        o = beside_lanes(o_ref, b)
        dot_ref[b] = jnp.sum(o * beside.astype(F32), axis=0, keepdims=True)
        gw_ref[b] = jnp.concatenate([jnp.zeros_like(beside), beside], axis=0)

    def part(b, rel):
        attend_back_part(
            q_ref, kv_ref, kvt_ref, start_ref, lse_ref, gw_ref, dot_ref, dq_ref, acc_ref, b, rel
        )

    def end(b):
        dq = dq_ref[b][:HEAD_DIM] * HEAD_DIM ** (-0.5)
        at = block_lanes(b)
        c, s = cos_ref[:, at], sin_ref[:, at]
        turned = jnp.concatenate(
            [turn_back(dq[:, :QB], c, s), turn_back(dq[:, QB:], c, s)], axis=0
        )
        g_qkv[at, :128] = turned.T.astype(BF)

    key_copies = []

    def send_keys(rel):
        i = rel - 1
        s = 4 - rel
        there = pl.multiple_of(lax.rem(x + s, 4) * ROWS, ROWS)
        add_rows(key_low.at[i], [acc_ref.at[pl.ds(there, ROWS)]], ROWS, 256)
        c = remote(
            key_low.at[i], key_land.at[i], ksems[0].at[i], ksems[1].at[i], peer(("x",), (s,))
        )
        c.start()
        key_copies.append(c)

    z = lax.axis_index("z")
    grads.send_joined(0)
    acc_ref[...] = jnp.zeros_like(acc_ref)
    downs.fill(2, 1)
    tokens.pass_mate()
    tokens.pass_ring(0)
    tokens.wait_own()
    tokens.have(0, 1)
    lead(z)
    downs.fill(3, 0)
    for q in (2, 1, 3):
        downs.pair_ring(q)
    tokens.pass_ring(1)
    grads.send_mate()
    tokens.have(2, 4)
    lead(lax.rem(z + 3, 4))
    tokens.have(3, 5)
    lead(lax.rem(z + 1, 4))
    tokens.finish()
    both(downs.send_far)
    both(downs.send_near)
    lead(lax.rem(z + 2, 4))
    for b in range(BLOCKS):
        part(b, 2)
    send_keys(2)
    both(downs.send_joined)
    downs.pair_ring(0)
    for b in range(BLOCKS):
        part(b, 1)
    send_keys(1)
    downs.send_mate()
    grads.total(m_sum)
    m_deal = deal_start(m_sum.reshape(MEMBERS, 32, 1536), m_dealt, deals[:3])
    for b in range(BLOCKS):
        part(b, 0)
        end(b)
    downs.total(total)
    out_low[...] = (resid_ref[...] + total[...]).astype(BF)
    copies = [
        pltpu.make_async_copy(out_low, block_out.at[t], csems[2]),
        remote(out_low, block_out.at[t], csems[0], csems[1], other_core()),
    ]
    for c in copies:
        c.start()
    for c in key_copies:
        c.wait()
    own = pl.ds(pl.multiple_of(x * ROWS, ROWS), ROWS)
    add_rows(key_sum, [acc_ref.at[own]] + [key_land.at[i] for i in range(2)], ROWS, 256)
    for b in range(BLOCKS):
        at = pl.ds(b * QB, QB)
        v = key_sum[at, :].T
        k = turn_back(v[:HEAD_DIM], cos_ref[:, at], sin_ref[:, at])
        g_qkv[at, 128:] = jnp.concatenate([k, v[HEAD_DIM:]], axis=0).T.astype(BF)

    last = TokenScatter(g_qkv, wqkv_ref, slots[12:], stage, sems[8:])
    attn = GradScatter(
        [(all_a, g_qkv), (all_r.reshape(ROWS, D), low_ref)], mids[6:], columns, gsems[3:]
    )
    scatter_both(last, attn)
    attn.send_mate()
    attn.send_joined(0)
    attn.total(a_sum)
    a_deal = deal_start(a_sum.reshape(MEMBERS, 32, 384), a_dealt, deals[3:])
    last.total(total)
    rows = tokens_ref[own_half(tokens_ref), :].astype(F32)
    inverse = scale_rows(rows)
    grad[...] = g_resid[...] + norm_back(rows * inverse, inverse, total[...])
    more = [
        pltpu.make_async_copy(grad, input_grad.at[t], csems[5]),
        remote(grad, input_grad.at[t], csems[3], csems[4], other_core()),
    ]
    for c in more:
        c.start()
    finish(copies + more + m_deal + a_deal)


def backward_exchange(*args):
    outs = [
        ((2, HALF, D), F32),
        ((2, HALF, D), BF),
        ((MEMBERS, 32, 1536), BF),
        ((MEMBERS, 32, 384), BF),
        ((MEMBERS, 2, HALF, D), BF),
    ]
    wide, low = pltpu.VMEM((HALF, D), F32), pltpu.VMEM((HALF, D), BF)
    scratch = token_scatter_slots() * 3 + grad_scatter_slots(1536) + grad_scatter_slots(384)
    scratch += [STAGE, COLUMNS, wide, wide, wide, low, low]
    scratch += [
        pltpu.VMEM((256, 1536), BF),
        pltpu.VMEM((256, 384), BF),
        pltpu.VMEM((256, D), BF),
        pltpu.VMEM((ROWS, 256), BF),
        pltpu.VMEM((ROWS, 128), F32),
        pltpu.VMEM((LENGTH, 128), F32),
        pltpu.VMEM((2, ROWS, 128), BF),
        pltpu.VMEM((2, ROWS, 128), BF),
        pltpu.VMEM((BLOCKS, 2 * HEAD_DIM, WIDE), BF),
        pltpu.VMEM((BLOCKS, 1, WIDE), F32),
        pltpu.VMEM((BLOCKS, 2 * HEAD_DIM, WIDE), F32),
    ]
    scratch += TOKEN_SCATTER_SEMS * 3 + GRAD_SCATTER_SEMS * 2 + TOKEN_GATHER_SEMS
    scratch += [DMA((2,)), DMA((2,)), DMA, DMA((4,))] + [DMA] * 7 + DEAL_SEMS * 2
    input_grad, block_out, m_dealt, a_dealt, _ = call(
        backward_kernel,
        4,
        "backward_exchange",
        args,
        [VMEM] * 17 + [HBM] * 3,
        outs,
        [HBM] * 5,
        scratch,
    )
    return input_grad.reshape(2 * HALF, D), block_out.reshape(2 * HALF, D), m_dealt, a_dealt


def rope_frequency():
    base_freq = 500000.0 ** (-(np.arange(HEAD_DIM // 2) * 2.0 / HEAD_DIM))
    wavelength = 2.0 * math.pi / base_freq
    smooth = (8192.0 / wavelength - 1.0) / 3.0
    blended = (1.0 - smooth) * base_freq / 32.0 + smooth * base_freq
    frequency = np.where(
        wavelength < 2048.0, base_freq, np.where(wavelength > 8192.0, base_freq / 32.0, blended)
    )
    return np.repeat(frequency.astype(np.float32)[:, None], 128, axis=1)


def swap_cores(x):
    return lax.ppermute(x, "t", [(0, 1), (1, 0)])


def adamw(weight, first_moment, second_moment, gradient, step_rate):
    first_new = 0.9 * first_moment + 0.1 * gradient
    second_new = 0.95 * second_moment + 0.05 * gradient * gradient
    corrected = first_new / (1.0 - 0.9**STEP) / (jnp.sqrt(second_new / (1.0 - 0.95**STEP)) + 1e-08)
    return (first_new, second_new, weight - step_rate * (corrected + 0.1 * weight))


def slots(w, columns):
    return w.reshape(w.shape[0], -1, columns).transpose(1, 0, 2)


def unslots(g):
    return g.transpose(1, 0, 2).reshape(g.shape[1], -1)


def body(
    tokens,
    segments,
    cotangent,
    query_weight,
    key_weight,
    value_weight,
    output_weight,
    gate_weight,
    up_weight,
    down_weight,
    norm_gain_pair,
    query_first,
    key_first,
    value_first,
    output_first,
    gate_first,
    up_first,
    down_first,
    gains_first,
    query_second,
    key_second,
    value_second,
    output_second,
    gate_second,
    up_second,
    down_second,
    gains_second,
):
    gains = norm_gain_pair.astype(BF).astype(F32)
    gain_a, gain_m = gains[0][:, None], gains[1][:, None]
    low = lambda w: w.astype(BF).astype(F32)
    (
        resid,
        all_m,
        all_g,
        w_gate_up,
        w_down,
        kv,
        kvt,
        o_full,
        lse,
        o_low,
        all_a,
        w_qkv,
        w_out,
        q_wide,
        tables,
        starts,
        g_gate_up,
        act,
    ) = forward_exchange(
        tokens[0],
        segments,
        jnp.broadcast_to(gains[:, :, None], (2, 32, 128)),
        jnp.asarray(rope_frequency()),
        query_weight,
        key_weight,
        value_weight,
        output_weight.T,
        cotangent[0],
        gate_weight,
        up_weight,
        down_weight.T,
    )
    input_grad, block_out, mlp_dealt, attn_dealt = backward_exchange(
        g_gate_up,
        act,
        w_gate_up,
        w_down,
        resid,
        cotangent[0],
        w_out,
        q_wide,
        kv,
        kvt,
        starts,
        o_full,
        lse,
        o_low,
        tables,
        w_qkv,
        tokens[0],
        all_m,
        all_g,
        all_a,
    )
    mlp_sum, attn_sum = mlp_dealt.astype(F32), attn_dealt.astype(F32)

    pairs = lambda g: unslots(g.reshape(4, 2, 32, HEAD_DIM).sum(axis=1))
    q_sum = unslots(attn_sum[:, :, :128])
    k_sum = pairs(attn_sum[:, :, 128:192])
    v_sum = pairs(attn_sum[:, :, 192:256])
    gate_sum = unslots(mlp_sum[:, :, :512])
    up_sum = unslots(mlp_sum[:, :, 512:1024])
    dots = lambda g, w: jnp.sum(g * low(w), axis=1)
    gains_half = jnp.stack(
        [
            dots(q_sum, query_weight) + dots(k_sum, key_weight) + dots(v_sum, value_weight),
            dots(gate_sum, gate_weight) + dots(up_sum, up_weight),
        ],
        axis=0,
    )
    gains_grad = gains_half + swap_cores(gains_half)
    query_grad, key_grad, value_grad = gain_a * q_sum, gain_a * k_sum, gain_a * v_sum
    gate_grad, up_grad = gain_m * gate_sum, gain_m * up_sum
    output_grad = unslots(attn_sum[:, :, 256:]).T
    down_grad = unslots(mlp_sum[:, :, 1024:]).T
    wide_rate = 2.0 * D ** (-0.5)
    outs = [block_out[None], input_grad[None]]
    for weight, first, second, grad, rate in (
        (query_weight, query_first, query_second, query_grad, wide_rate),
        (key_weight, key_first, key_second, key_grad, wide_rate),
        (value_weight, value_first, value_second, value_grad, wide_rate),
        (output_weight, output_first, output_second, output_grad, 2.0 * (4 * HEAD_DIM) ** (-0.5)),
        (gate_weight, gate_first, gate_second, gate_grad, wide_rate),
        (up_weight, up_first, up_second, up_grad, wide_rate),
        (down_weight, down_first, down_second, down_grad, 2.0 * FF ** (-0.5)),
        (norm_gain_pair, gains_first, gains_second, gains_grad, 1.5),
    ):
        outs.append(grad)
        outs.extend(adamw(weight, first, second, grad, rate))
    return tuple(outs)


def solution(mesh):
    split = Mesh(
        mesh.devices.reshape(tuple(SIZES.values())), tuple(SIZES)
    )
    heads = ("x", "z", "yl")
    every = ("dp", "x", "z", "yl")
    acts = P("dp", heads, None)
    rows_cut = P(every, "t")
    columns_cut = P("t", every)
    gains = P(None, every)
    weights = (rows_cut,) * 3 + (columns_cut,) + (rows_cut,) * 2 + (columns_cut, gains)
    in_specs = (acts, P("dp", heads), acts) + weights * 3
    out_specs = (acts, acts) + tuple(spec for spec in weights for _ in range(4))
    return jax.shard_map(
        body, mesh=split, in_specs=in_specs, out_specs=out_specs, check_vma=False
    )
```
